128 devices in a mesh: sec: 4 (over x_hi, core), dev: 32 (over x_lo, y, z).
Axes of the slice: x: 4 (x_hi: 2, x_lo: 2; x = x_hi * 2 + x_lo), y: 4, z: 4, core: 2. Of those that a mesh axis runs over, the one named last changes fastest.
Arguments:
- query_latent: bfloat16 [512, 128, 512], P('dev', 'sec'), may hold values from -60 to 60
- query_rope: bfloat16 [512, 8192], P('dev', 'sec'), may hold values from -5 to 5
- cache_latent: bfloat16 [512, 512, 512], P('dev'), may hold values from -5 to 5
- cache_rope: bfloat16 [512, 64, 512], P('dev'), may hold values from -5 to 5
- lengths: int32 [512], P('dev'), may hold values from 2 to 512
- value_up: bfloat16 [128, 512, 128], P('sec'), may hold values from -1 to 1
- output_proj: bfloat16 [16384, 7168], P('sec', 'dev'), may hold values from -0.046875 to 0.046875
- hidden: bfloat16 [512, 7168], P(None, 'dev'), may hold values from -6 to 6
- norm_gain: float32 [7168], replicated, may hold values from 0.1 to 1.9
- route_ids: int32 [512, 8], replicated, may hold values from 0 to 31, all different within a row; in each aligned block of 512 rows (0 to 511, 512 to 1023, ...) at most 256 rows name the same one
- route_weights: float32 [512, 8], replicated, may hold values from 0.1 to 0.5
- gate_proj: bfloat16 [32, 7168, 1024], P('dev', None, 'sec'), may hold values from -0.0625 to 0.0625
- up_proj: bfloat16 [32, 7168, 1024], P('dev', None, 'sec'), may hold values from -0.0625 to 0.0625
- down_proj: bfloat16 [32, 1024, 7168], P('dev', 'sec'), may hold values from -0.1875 to 0.1875
Outputs:
- mixed_out: bfloat16 [512, 7168], P('sec', 'dev')
The draws below stay inside these ranges and needn't reach their ends.
Inputs may be any that keep to these rules, and one draw needn't show every extreme that they name: `route_ids`: each user names 8 different experts; no expert is named by more than 256 users, a bound that some block reaches.
All inputs are finite; a program needn't handle non-finite values.
Results may differ from the reference program's by a relative error of at most 0.008.
Values may be sent and summed in bfloat16 or wider, within the bound.
A program may use at most 128 MiB of HBM per device.

```python
import math
import jax
import jax.numpy as jnp
import numpy as np
from jax import lax

D = 7168
HEADS = 128
LATENT = 512
ROPE = 64
NOPE = 128
VDIM = 128
HID = 1024
TOPK = 8
HIST = 512
ROWS = 512
EXPERTS = 32
CAP = 256
N_SEC = 4


def drawn_rows(key):
    subkeys = jax.random.split(key, 1)
    first_keys = jnp.clip(jax.random.normal(subkeys[0], (ROWS, LATENT), jnp.float32), -3.0, 3.0)
    return first_keys


def draw_cache_latent(key, part):
    first_keys = drawn_rows(key)
    key = jax.random.fold_in(key, 3)
    cache_values = jnp.clip(jax.random.normal(key, (ROWS, HIST, LATENT), jnp.float32), -5.0, 5.0)
    cache_values = cache_values.at[:, 0, :].set(first_keys)
    return cache_values.astype(jnp.bfloat16)


def draw_query_latent(key, part):
    key = jax.random.fold_in(key, 5)
    queries = jnp.clip(jax.random.normal(key, (ROWS, HEADS, LATENT), jnp.float32), -5.0, 5.0)
    return queries.astype(jnp.bfloat16)


def draw_lengths(key, part):
    key = jax.random.fold_in(key, 7)
    subkeys = jax.random.split(key, 3)
    longer = jax.random.randint(subkeys[0], (ROWS,), 2, HIST + 1)
    shorter = jax.random.randint(subkeys[1], (ROWS,), 2, HIST + 1)
    longest_row = jax.random.randint(subkeys[2], (), 0, ROWS)
    return jnp.minimum(longer, shorter).at[longest_row].set(HIST).astype(jnp.int32)


def steps_of(key, shape, pieces, smallest, largest):
    loudness = 1.0
    for axis_at, shards_of in pieces:
        draws = jax.random.uniform(jax.random.fold_in(jax.random.fold_in(key, 6), axis_at), (shards_of,), jnp.float32, smallest / len(pieces), largest / len(pieces))
        loudness = loudness * jnp.repeat(jnp.exp(draws), shape[axis_at] // shards_of).reshape((-1,) + (1,) * (len(shape) - 1 - axis_at))
    return loudness


def routed_block(key, own, number, rows, amount, top, limit, skew):
    order = jax.random.permutation(key, amount)
    crowded, usual = shares(amount, rows * top, limit, skew, True), shares(amount, rows * top, limit, skew, False)
    places = jnp.arange(amount)

    def named(sizes, offset_by):
        used = int((sizes > 0).sum())
        fixed = max(1, used // 4)
        moved = fixed + (places - fixed + offset_by * (used - fixed)) % max(1, amount - fixed)
        return jnp.zeros((amount,), jnp.int32).at[order[jnp.where(places < fixed, places, moved)]].set(jnp.asarray(sizes, jnp.int32))

    sizes = jnp.where(number % 4 == 0, named(crowded, number // 4), named(usual, number - number // 4 - 1))
    mixed = jax.random.permutation(jax.random.fold_in(own, 3), amount)
    source_of, taker = mixed[0:amount // 2 * 2:2], mixed[1:amount // 2 * 2:2]
    margin = jnp.minimum(sizes[source_of] - 1, limit - sizes[taker]) // 2
    margin = jnp.where((source_of == order[0]) | (taker == order[0]) | (sizes[taker] == 0), 0, jnp.maximum(margin, 0))
    moved = jax.random.randint(jax.random.fold_in(own, 4), (amount // 2,), 0, 1 << 20) % (margin + 1)
    sizes = sizes.at[source_of].add(-moved).at[taker].add(moved)
    labels = jnp.searchsorted(jnp.cumsum(sizes), jnp.arange(rows * top), side="right").astype(jnp.int32)
    listing = labels.reshape(top, rows).T
    listing = listing[jax.random.permutation(jax.random.fold_in(own, 1), rows)]
    offset_by = jax.random.randint(jax.random.fold_in(own, 2), (rows, 1), 0, top)
    return jnp.take_along_axis(listing, (jnp.arange(top)[None, :] + offset_by) % top, axis=1)


def shares(amount, total, most, skew, full):
    loads = [(1 << 20) // math.isqrt(rank ** skew) + 1 for rank in range(1, amount + 1)]
    largest = most if full else min(most, max(-(-total // amount), total * loads[0] // sum(loads)))
    least = 1 if total - largest >= amount - 1 else 0
    holding, rest = [largest] + [least] * (amount - 1), total - largest - least * (amount - 1)
    while rest > 0:
        movable = [i for i in range(1, amount) if holding[i] < largest] or [i for i in range(1, amount) if holding[i] < most]
        pool, remaining = sum([loads[i] for i in movable]), rest
        for i in movable:
            extra = min(most - holding[i], max(1, remaining * loads[i] // pool), rest)
            holding[i] = holding[i] + extra
            rest = rest - extra
    return np.array(holding)


def bell_draw(own_key, extent, deviation, limit, cuts=(), kind=jnp.bfloat16):
    result = jax.random.normal(own_key, extent, jnp.float32) * deviation
    if len(cuts) > 0:
        result = steps_of(own_key, extent, cuts, -0.22, 0.18) * result
    return jnp.clip(result, min=-limit, max=limit).astype(kind)


def setup_inputs(seed: int = 0) -> dict:
    seeds = jax.random.split(jax.random.key(seed), 15)
    query_latent = draw_query_latent(jax.random.fold_in(seeds[14], 71), 0)
    query_rope = bell_draw(seeds[1], (ROWS, HEADS * ROPE), 1.0, 5.0, ((0, 32), (1, 4)))
    cache_latent = draw_cache_latent(jax.random.fold_in(seeds[14], 71), 0)
    cache_rope = bell_draw(seeds[3], (ROWS, ROPE, HIST), 1.0, 5.0, ((0, 32),))
    lengths = draw_lengths(jax.random.fold_in(seeds[14], 71), 0)
    value_up = bell_draw(seeds[5], (HEADS, LATENT, VDIM), (LATENT // 16) ** -0.5, 1.0, ((0, 4),))
    output_proj = bell_draw(seeds[6], (HEADS * VDIM, D), (HEADS * VDIM) ** -0.5, 0.046875, ((0, 4), (1, 32)))
    hidden = bell_draw(seeds[7], (ROWS, D), 1.0, 6.0, ((1, 32),))
    norm_gain = jnp.clip(1.0 + 0.18 * jax.random.normal(seeds[8], (D,), jnp.float32), 0.1, 1.9)
    route_ids_keys = jax.random.split(jax.random.fold_in(seeds[9], 1), ROWS // ROWS)
    route_ids_turns = jax.random.permutation(jax.random.fold_in(seeds[9], 3), ROWS // ROWS)
    route_ids = jax.vmap(lambda own, number: routed_block(jax.random.fold_in(seeds[9], 2), own, number, ROWS, EXPERTS, TOPK, CAP, 2))(route_ids_keys, route_ids_turns).reshape((ROWS, TOPK))
    route_weights = jnp.clip(jax.random.uniform(seeds[10], (ROWS, TOPK), jnp.float32, 0.1, 0.5), 0.1, 0.5)
    gate_proj = bell_draw(seeds[11], (EXPERTS, D, HID), D ** -0.5, 0.0625, ((0, 32), (2, 4)))
    up_proj = bell_draw(seeds[12], (EXPERTS, D, HID), D ** -0.5, 0.0625, ((0, 32), (2, 4)))
    down_proj = bell_draw(seeds[13], (EXPERTS, HID, D), HID ** -0.5, 0.1875, ((0, 32), (1, 4)))
    return dict(query_latent=query_latent, query_rope=query_rope, cache_latent=cache_latent, cache_rope=cache_rope, lengths=lengths, value_up=value_up, output_proj=output_proj, hidden=hidden, norm_gain=norm_gain, route_ids=route_ids, route_weights=route_weights, gate_proj=gate_proj, up_proj=up_proj, down_proj=down_proj)


norm_eps = 1e-06

def attend_row(inputs):
    query_lat, query_pos, cache_lat, cache_pos, length = inputs
    positional = query_pos.reshape(HEADS, ROPE)
    scores = jnp.dot(query_lat, cache_lat.T, preferred_element_type=jnp.float32) + jnp.dot(positional, cache_pos, preferred_element_type=jnp.float32)
    scores = scores * (NOPE + ROPE) ** (-0.5)
    visible = jnp.arange(HIST, dtype=jnp.int32)[None, :] < length
    scores = jnp.where(visible, scores, -1e+30)
    highest = lax.optimization_barrier(jnp.max(scores, axis=-1, keepdims=True))
    exponent = jnp.exp(scores - highest)
    weights = (exponent / lax.optimization_barrier(jnp.sum(exponent, axis=-1, keepdims=True))).astype(jnp.bfloat16)
    return jnp.dot(weights, cache_lat, preferred_element_type=jnp.float32).astype(jnp.bfloat16)

def expert_output(inputs_rows, norm_gain, gate_w, up_w, down_w):
    values = inputs_rows.astype(jnp.float32)
    mean_square = lax.optimization_barrier(jnp.mean(values * values, axis=-1, keepdims=True))
    normed = (values * lax.rsqrt(mean_square + norm_eps) * norm_gain).astype(jnp.bfloat16)
    gate = jnp.dot(normed, gate_w, preferred_element_type=jnp.float32)
    upward = jnp.dot(normed, up_w, preferred_element_type=jnp.float32)
    activation = (jax.nn.silu(gate) * upward).astype(jnp.bfloat16)
    slice_width = HID // N_SEC
    summed = jnp.zeros((inputs_rows.shape[0], D), jnp.float32)
    for section in range(N_SEC):
        lower = section * slice_width
        partial_value = jnp.dot(activation[:, lower:lower + slice_width], down_w[lower:lower + slice_width], preferred_element_type=jnp.float32).astype(jnp.bfloat16)
        summed = summed + partial_value.astype(jnp.float32)
    return summed

def reference(query_latent, query_rope, cache_latent, cache_rope, lengths, value_up, output_proj, hidden, norm_gain, route_ids, route_weights, gate_proj, up_proj, down_proj):
    context = lax.map(attend_row, (query_latent, query_rope, cache_latent, cache_rope, lengths))
    head_values = jnp.einsum('rhc,hcv->rhv', context.astype(jnp.float32), value_up.astype(jnp.float32)).astype(jnp.bfloat16).reshape(ROWS, HEADS * VDIM)
    attn_out = jnp.dot(head_values, output_proj, preferred_element_type=jnp.float32)
    residual = hidden.astype(jnp.float32) + attn_out
    routed = residual.astype(jnp.bfloat16)
    expert_ids = route_ids.reshape(-1).astype(jnp.int32)
    onehot = (expert_ids[:, None] == jnp.arange(EXPERTS, dtype=jnp.int32)[None, :]).astype(jnp.int32)
    earlier = (jnp.cumsum(onehot, axis=0) - onehot).astype(jnp.int32)
    slot_rank = lax.optimization_barrier(jnp.sum(earlier * onehot, axis=1)).astype(jnp.int32)
    pair_rows = (jnp.arange(ROWS * TOPK, dtype=jnp.int32) // TOPK).astype(jnp.int32)
    slot_rows = jnp.full((EXPERTS, CAP), ROWS, jnp.int32).at[expert_ids, slot_rank].set(pair_rows)
    padded = jnp.concatenate([routed, jnp.zeros((1, D), jnp.bfloat16)], axis=0)

    def run_expert(inputs):
        rows_here, gate_w, up_w, down_w = inputs
        return expert_output(padded[rows_here], norm_gain, gate_w, up_w, down_w)
    outputs = lax.map(run_expert, (slot_rows, gate_proj, up_proj, down_proj))
    flat_out = outputs.reshape(EXPERTS * CAP, D)
    picked = flat_out[(expert_ids * CAP + slot_rank).astype(jnp.int32)].reshape(ROWS, TOPK, D)
    expert_sum = lax.optimization_barrier(jnp.sum(picked * route_weights[:, :, None], axis=1))
    return (residual + expert_sum).astype(jnp.bfloat16)
```

```python
import jax
import jax.numpy as jnp
from jax import lax
from jax.experimental import pallas as pl
from jax.experimental.pallas import tpu as pltpu
from jax.sharding import PartitionSpec as P

ROPE = 64
NOPE = 128
norm_eps = 1e-06
MESH = pl.DeviceIdType.MESH
F32 = jnp.float32
BF16 = jnp.bfloat16

PARTS = ((0, 80, "xyz"), (80, 80, "zxy"), (160, 64, "yzx"))
FEATS = 224
LANES = 128


def gain_planes(norm_gain):
    g = norm_gain.reshape(2, 4, 4, FEATS)
    z_planes = g[..., 0:80].transpose(2, 0, 1, 3).reshape(4, 1, 640)
    y_planes = g[..., 80:160].transpose(1, 0, 2, 3).reshape(4, 1, 640)
    x_planes = g[..., 160:224].reshape(2, 1, 1024)
    return z_planes, y_planes, x_planes


def weight_plane(ref, p, j):
    first, rows, _ = PARTS[p]
    if p == 0:
        block = ref[:, :, j, first : first + rows, :]
    elif p == 1:
        block = ref[:, j, :, first : first + rows, :]
    else:
        block = ref[j, :, :, first : first + rows, :]
    return block.reshape(-1, block.shape[-1])


def at(ref, **index):
    return ref.at[tuple(index.get(axis, slice(None)) for axis in "xyz")]


def get(ref, **index):
    return ref[tuple(index.get(axis, slice(None)) for axis in "xyz")]


def moe_kernel(
    head_hbm, out_proj_hbm, hidden_hbm, gain0, gain1, gain2, share_ref, gate_hbm, up_hbm, down_hbm,
    out_ref,
    heads0, heads1, out_proj, attn, pair_in, far_in, far_out, hidden,
    gate_in, up_in, down_in, wt0, wt1, wt2, downt,
    rt0, rt1, rt2, gate_up, act, o0, o1, o2,
    r1_0, r1_1, r1_2, r2_0, r2_1, r2_2, r3_0, r3_1, r3_2, r4_0, r4_1, r4_2, r5_0, r5_1, r5_2,
    local_sem, send_sem, recv_sem,
):
    sec = lax.axis_index("sec")
    dev = lax.axis_index("dev")
    x_hi, core = sec // 2, lax.rem(sec, 2)
    x_lo = dev // 16
    me = {
        "x": x_hi * 2 + x_lo,
        "y": lax.rem(dev // 4, 4),
        "z": lax.rem(dev, 4),
    }

    def shift(axis, by):
        return lax.rem(me[axis] + (by % 4), 4)

    def device(x, y, z, c):
        return ((x // 2) * 2 + c, lax.rem(x, 2) * 16 + y * 4 + z)

    def neighbour(axis, by):
        place = dict(me)
        place[axis] = shift(axis, by)
        return device(place["x"], place["y"], place["z"], core)

    partner = device(me["x"], me["y"], me["z"], 1 - core)
    x_lo_partner = (sec, (1 - x_lo) * 16 + me["y"] * 4 + me["z"])

    tags = {}
    sent = []

    def number(tag):
        return tags.setdefault(tag, len(tags))

    def send(tag, src, dst, to):
        i = number(tag)
        copy = pltpu.make_async_remote_copy(
            src_ref=src, dst_ref=dst, send_sem=send_sem.at[i], recv_sem=recv_sem.at[i],
            device_id=to, device_id_type=MESH,
        )
        copy.start()
        sent.append(copy)

    def recv(tag, region):
        i = number(tag)
        pltpu.make_async_remote_copy(
            src_ref=region, dst_ref=region, send_sem=send_sem.at[i], recv_sem=recv_sem.at[i],
            device_id=partner, device_id_type=MESH,
        ).wait_recv()

    heads = (heads0, heads1)
    own_heads = [at(h, x=x_lo, y=me["y"], z=me["z"]) for h in heads]
    my_hidden = hidden_hbm.at[pl.ds(pl.multiple_of(sec * LANES, LANES), LANES)]
    loads = [
        pltpu.make_async_copy(head_hbm.at[0], own_heads[0], local_sem.at[0]),
        pltpu.make_async_copy(head_hbm.at[1], own_heads[1], local_sem.at[1]),
        pltpu.make_async_copy(gate_hbm, gate_in, local_sem.at[2]),
        pltpu.make_async_copy(up_hbm, up_in, local_sem.at[3]),
        pltpu.make_async_copy(out_proj_hbm, out_proj, local_sem.at[4]),
        pltpu.make_async_copy(down_hbm, down_in, local_sem.at[5]),
        pltpu.make_async_copy(my_hidden, hidden, local_sem.at[6]),
    ]
    for load in loads:
        load.start()

    barrier = pltpu.get_barrier_semaphore()
    around = [neighbour(axis, by) for axis in "xyz" for by in (1, 2, 3)] + [partner]
    for other in around:
        pl.semaphore_signal(barrier, inc=1, device_id=other, device_id_type=MESH)
    pl.semaphore_wait(barrier, len(around))

    order = (("y", "z"), ("z", "y"))
    half = heads0.shape[-1]

    def head_block(p, k, **index):
        place = {"x": lax.rem(x_lo + k, 2), "y": me["y"], "z": me["z"]}
        place.update(index)
        return at(heads[p], **place)

    def head_slab(p, **index):
        return at(heads[p], **index)

    for p in range(2):
        loads[p].wait()
        send(("hx", p), own_heads[p], own_heads[p], x_lo_partner)
    for p in range(2):
        b, c = order[p]
        for by in (1, 3):
            send(("hb", p, 0, by), own_heads[p], own_heads[p], neighbour(b, by))

    wts = (wt0, wt1, wt2)
    gains = (gain0, gain1, gain2)

    def transpose_part(p, which):
        source = (gate_in, up_in)[which]

        def step(j, carry):
            block = weight_plane(source, p, j).T.astype(F32) * gains[p][j]
            wts[p][0, j, which * 256 : which * 256 + 256, :] = block.astype(BF16)
            return carry

        lax.fori_loop(0, wts[p].shape[1], step, 0)

    def transpose_down():
        def step(j, carry):
            block = down_in[:, pl.ds(pl.multiple_of(j * 896, 896), 896)].T
            downt[0, j // 4, lax.rem(j, 4)] = block.reshape(4, FEATS, 256)
            return carry

        lax.fori_loop(0, 8, step, 0)

    def share_part(p):
        send(("wt", p), wts[p].at[0], wts[p].at[1], partner)

    def task_first():
        loads[2].wait()
        loads[3].wait()
        transpose_part(0, 0)

    def task_1():
        transpose_part(0, 1)
        share_part(0)

    def task_2():
        transpose_part(1, 0)

    def task_3():
        transpose_part(1, 1)
        share_part(1)

    def task_4():
        transpose_part(2, 0)

    def task_5():
        transpose_part(2, 1)
        share_part(2)

    def task_6():
        loads[5].wait()
        transpose_down()
        send(("dn",), downt.at[0], downt.at[1], partner)

    tasks = [task_first, task_1, task_2, task_3, task_4, task_5, task_6]

    def work():
        if tasks:
            tasks.pop(0)()

    work()

    def slab_sends(p, m):
        b, c = order[p]
        slab = head_slab(p, **{b: shift(b, m), c: me[c]})
        for by in (1, 3):
            send(("hc", p, m, by), slab, slab, neighbour(c, by))

    for p in range(2):
        b, c = order[p]
        other = head_block(p, 1)
        recv(("hx", p), other)
        for by in (1, 3):
            send(("hb", p, 1, by), other, other, neighbour(b, by))
    for p in range(2):
        slab_sends(p, 0)
    work()
    for p in range(2):
        b, c = order[p]
        block = head_block(p, 0, **{b: shift(b, 3)})
        recv(("hb", p, 0, 1), block)
        send(("hf", p, 0), block, block, neighbour(b, 1))
        recv(("hb", p, 0, 3), head_block(p, 0, **{b: shift(b, 1)}))
    for p in range(2):
        b, c = order[p]
        block = head_block(p, 1, **{b: shift(b, 1)})
        recv(("hb", p, 1, 3), block)
        send(("hf", p, 1), block, block, neighbour(b, 3))
        slab_sends(p, 1)
        recv(("hb", p, 1, 1), head_block(p, 1, **{b: shift(b, 3)}))
        slab_sends(p, 3)
    work()
    for p in range(2):
        b, c = order[p]
        for k in range(2):
            recv(("hf", p, k), head_block(p, k, **{b: shift(b, 2)}))
        slab_sends(p, 2)
    work()

    def project(p, by, first=False):
        c = order[p][1]
        j = shift(c, by)
        rows = get(heads[p], **{c: j}).reshape(-1, half)
        product = jnp.dot(rows, out_proj[p * half : (p + 1) * half, :], preferred_element_type=F32)
        product = product.reshape(2, 4, 16, FEATS)
        if c == "z":
            attn[:, :, j] = product
        else:
            attn[:, j] += product

    loads[4].wait()
    project(0, 0)
    for m in (0, 1, 3, 2):
        for p in range(2):
            b, c = order[p]
            for by in (1, 3):
                region = head_slab(p, **{b: shift(b, m), c: shift(c, -by)})
                recv(("hc", p, m, by), region)
                if (m in (0, 1)) == (by == 1):
                    send(("hd", p, m), region, region, neighbour(c, by))
        work()
    while tasks:
        work()
    project(0, 1)
    project(0, 3)
    for m in (0, 3, 1, 2):
        for p in range(2):
            b, c = order[p]
            recv(("hd", p, m), head_slab(p, **{b: shift(b, m), c: shift(c, 2)}))
    project(0, 2)
    for by in (0, 1, 3, 2):
        project(1, by)

    attn_mine = attn.at[:, pl.ds(core * 2, 2)]
    send(("pair",), attn.at[:, pl.ds((1 - core) * 2, 2)], pair_in, partner)
    recv(("pair",), pair_in)
    far_out[...] = (attn_mine[1 - x_hi] + pair_in[1 - x_hi]).astype(BF16)
    send(("far",), far_out, far_in, neighbour("x", 2))
    loads[6].wait()
    near = (attn_mine[x_hi] + pair_in[x_hi]).reshape(LANES, FEATS) + hidden[...].astype(F32)
    recv(("far",), far_in)
    residual = near + far_in[...].reshape(LANES, FEATS).astype(F32)
    residual = jnp.concatenate([residual, jnp.zeros((LANES, 32), F32)], axis=1).T[:FEATS]
    out_ref[...] = residual
    routed = residual.astype(BF16)

    rts = (rt0, rt1, rt2)
    for p, (first, rows, _) in enumerate(PARTS):
        rts[p][me["x"], me["y"], me["z"]] = routed[first : first + rows]

    def spot(p, **index):
        place = dict(me)
        place.update(index)
        return at(rts[p], **place)

    axes = [tuple(o) for _, _, o in PARTS]
    for p in range(3):
        a, b, c = axes[p]
        for by in (1, 3, 2):
            send(("ga", p, by), spot(p), spot(p), neighbour(a, by))
        for by in (1, 3):
            send(("gb", p, 0, by), spot(p), spot(p), neighbour(b, by))

    def plane_group(p, m):
        a, b, c = axes[p]
        slab = at(rts[p], **{b: shift(b, m), c: me[c]})
        for by in (1, 3):
            send(("gc", p, m, by), slab, slab, neighbour(c, by))

    for k in (1, 3, 2):
        for p in range(3):
            a, b, c = axes[p]
            block = spot(p, **{a: shift(a, k)})
            recv(("ga", p, 4 - k), block)
            for by in (1, 3):
                send(("gb", p, k, by), block, block, neighbour(b, by))
    for p in range(3):
        plane_group(p, 0)
    for k in (0, 1, 3, 2):
        for p in range(3):
            a, b, c = axes[p]
            for by in (1, 3):
                block = spot(p, **{a: shift(a, k), b: shift(b, -by)})
                recv(("gb", p, k, by), block)
                if (k in (0, 1)) == (by == 1):
                    send(("gf", p, k), block, block, neighbour(b, by))
    for p in range(3):
        plane_group(p, 3)
        plane_group(p, 1)
    for p in range(3):
        a, b, c = axes[p]
        for k in (0, 1, 3, 2):
            recv(("gf", p, k), spot(p, **{a: shift(a, k), b: shift(b, 2)}))
        plane_group(p, 2)

    for p in range(3):
        recv(("wt", p), wts[p].at[1])
    totals = {"square": jnp.zeros((1, 256), F32), "first": True}

    def users_of(p, by):
        if p == 0:
            block = rts[0][:, :, shift("z", by)]
            low, high = block[0:2], block[2:4]
        elif p == 1:
            block = rts[1][:, shift("y", by)]
            low, high = block[0:2], block[2:4]
        else:
            plane = lax.rem(x_lo + by, 2)
            low, high = rts[2][plane], rts[2][plane + 2]
        return jnp.concatenate([low.reshape(-1, LANES), high.reshape(-1, LANES)], axis=1)

    def plane_of(p, by):
        if p == 2:
            return lax.rem(x_lo + by, 2)
        return shift(axes[p][2], by)

    def multiply(p, by):
        rows = users_of(p, by)
        wide = rows.astype(F32)
        totals["square"] = totals["square"] + jnp.sum(wide * wide, axis=0, keepdims=True)
        for slot in range(2):
            product = jnp.dot(wts[p][slot, plane_of(p, by)], rows, preferred_element_type=F32)
            if totals["first"]:
                gate_up[slot] = product
            else:
                gate_up[slot] += product
        totals["first"] = False

    multiply(0, 0)
    multiply(1, 0)
    for m in (0, 1, 3, 2):
        for p in range(3):
            a, b, c = axes[p]
            for by in (1, 3):
                region = at(rts[p], **{b: shift(b, m), c: shift(c, -by)})
                recv(("gc", p, m, by), region)
                if (m in (0, 1)) == (by == 1):
                    send(("gd", p, m), region, region, neighbour(c, by))
    for by in (1, 3):
        multiply(0, by)
        multiply(1, by)
    multiply(2, 1)
    for p in range(3):
        a, b, c = axes[p]
        for m in (0, 3, 1, 2):
            recv(("gd", p, m), at(rts[p], **{b: shift(b, m), c: shift(c, 2)}))
        multiply(p, 2 if p < 2 else 0)

    scale = lax.rsqrt(totals["square"] * (1.0 / (32 * FEATS)) + norm_eps)
    for slot in range(2):
        gate = gate_up[slot, 0:256] * scale
        upward = gate_up[slot, 256:512] * scale
        act[slot * 256 : slot * 256 + 256] = (gate / (1.0 + jnp.exp(-gate)) * upward).astype(BF16)

    recv(("dn",), downt.at[1])
    outs = (o0, o1, o2)
    r1, r2, r3, r4, r5 = (
        (r1_0, r1_1, r1_2), (r2_0, r2_1, r2_2), (r3_0, r3_1, r3_2), (r4_0, r4_1, r4_2), (r5_0, r5_1, r5_2)
    )
    share = jnp.concatenate([share_ref[core], share_ref[core + 2]], axis=1)

    def down(p, by):
        first, rows, _ = PARTS[p]
        j = plane_of(p, by)
        product = jnp.dot(weight_plane(downt.at[0], p, j), act[0:256], preferred_element_type=F32)
        product += jnp.dot(weight_plane(downt.at[1], p, j), act[256:512], preferred_element_type=F32)
        product = (product * share).astype(BF16)
        for h in range(2):
            lanes = product[:, h * LANES : (h + 1) * LANES]
            if p == 0:
                o0[2 * h : 2 * h + 2, :, j] = lanes.reshape(2, 4, rows, LANES)
            elif p == 1:
                o1[2 * h : 2 * h + 2, j] = lanes.reshape(2, 4, rows, LANES)
            else:
                o2[j + 2 * h] = lanes.reshape(4, 4, rows, LANES)

    def o_slab(p, by, m):
        a, b, c = axes[p]
        return at(outs[p], **{c: shift(c, by), b: shift(b, m)})

    for p in range(3):
        c = axes[p][2]
        down(p, 2 if p < 2 else 0)
        for m in (2, 0, 3, 1):
            by = 1 if m in (0, 1) else 3
            send(("s1", p, m), o_slab(p, 2, m), r1[p].at[m], neighbour(c, by))
    for p in range(3):
        c = axes[p][2]
        if p < 2:
            down(p, 1)
            down(p, 3)
        else:
            down(p, 1)
        for m in (2, 3):
            send(("s2", p, 0, m), o_slab(p, 1, m), r2[p].at[0, m], neighbour(c, 1))
        for m in (1, 0):
            send(("s2", p, 1, m), o_slab(p, 3, m), r2[p].at[1, m], neighbour(c, 3))
    for p in range(2):
        down(p, 0)

    def add_to(slab, other):
        slab[...] = (slab[...].astype(F32) + other[...].astype(F32)).astype(BF16)

    for m in (2, 1, 3, 0):
        for p in range(3):
            c = axes[p][2]
            recv(("s1", p, m), r1[p].at[m])
            by = 1 if m in (0, 1) else 3
            side = 0 if by == 1 else 1
            slab = o_slab(p, by, m)
            add_to(slab, r1[p].at[m])
            send(("s2", p, side, m), slab, r2[p].at[side, m], neighbour(c, by))

    for m in (2, 1, 3, 0):
        for p in range(3):
            a, b, c = axes[p]
            slab = o_slab(p, 0, m)
            for side in range(2):
                recv(("s2", p, side, m), r2[p].at[side, m])
            slab[...] = (
                slab[...].astype(F32) + r2[p][0, m].astype(F32) + r2[p][1, m].astype(F32)
            ).astype(BF16)
            if m == 2:
                send(("s3", p, 0), slab.at[0:2], r3[p].at[0:2], neighbour(b, 1))
                send(("s3", p, 1), slab.at[2:4], r3[p].at[2:4], neighbour(b, 3))
            elif m == 1:
                send(("s4", p, 0, 1), slab.at[2:4], r4[p].at[0, 2:4], neighbour(b, 1))
            elif m == 3:
                send(("s4", p, 1, 0), slab.at[0:2], r4[p].at[1, 0:2], neighbour(b, 3))
    for p in range(3):
        a, b, c = axes[p]
        recv(("s3", p, 0), r3[p].at[0:2])
        slab = o_slab(p, 0, 1).at[0:2]
        add_to(slab, r3[p].at[0:2])
        send(("s4", p, 0, 0), slab, r4[p].at[0, 0:2], neighbour(b, 1))
        recv(("s3", p, 1), r3[p].at[2:4])
        slab = o_slab(p, 0, 3).at[2:4]
        add_to(slab, r3[p].at[2:4])
        send(("s4", p, 1, 1), slab, r4[p].at[1, 2:4], neighbour(b, 3))
    for p in range(3):
        a, b, c = axes[p]
        for side in range(2):
            for lower in range(2):
                recv(("s4", p, side, lower), r4[p].at[side, 2 * lower : 2 * lower + 2])
        slab = o_slab(p, 0, 0)
        slab[...] = (
            slab[...].astype(F32) + r4[p][0].astype(F32) + r4[p][1].astype(F32)
        ).astype(BF16)
        for k in (2, 1, 3):
            send(("s5", p, k), slab.at[shift(a, k)], r5[p].at[k - 1], neighbour(a, k))
    for p, (first, rows, _) in enumerate(PARTS):
        a = axes[p][0]
        total = out_ref[first : first + rows, :] + outs[p][me["x"], me["y"], me["z"]].astype(F32)
        for k in (1, 3, 2):
            recv(("s5", p, k), r5[p].at[k - 1])
            total = total + r5[p][k - 1].astype(F32)
        out_ref[first : first + rows, :] = total
    for copy in sent:
        copy.wait_send()
    print("messages", len(tags))


def remote_part(head_values, output_proj, hidden, gains, share, gate, up, down):
    def bf(*shape):
        return pltpu.VMEM(shape, BF16)

    def f32(*shape):
        return pltpu.VMEM(shape, F32)

    rows = [r for _, r, _ in PARTS]
    any_space = pl.BlockSpec(memory_space=pl.ANY)
    vmem = pl.BlockSpec(memory_space=pltpu.VMEM)
    half = head_values.shape[-1]
    scratch = [
        bf(2, 4, 4, 16, half), bf(2, 4, 4, 16, half), bf(*output_proj.shape), f32(2, 4, 4, 16, FEATS),
        f32(2, 2, 4, 16, FEATS), bf(2, 4, 16, FEATS), bf(2, 4, 16, FEATS), bf(LANES, FEATS),
        bf(2, 4, 4, FEATS, 256), bf(2, 4, 4, FEATS, 256), bf(256, 32 * FEATS),
        bf(2, 4, 512, 640), bf(2, 4, 512, 640), bf(2, 2, 512, 1024), bf(2, 2, 4, 4, FEATS, 256),
        *[bf(4, 4, 4, r, LANES) for r in rows],
        f32(2, 512, 256), bf(512, 256),
        *[bf(4, 4, 4, r, LANES) for r in rows],
        *[bf(4, 4, r, LANES) for r in rows],
        *[bf(2, 4, 4, r, LANES) for r in rows],
        *[bf(4, r, LANES) for r in rows],
        *[bf(2, 4, r, LANES) for r in rows],
        *[bf(3, r, LANES) for r in rows],
        pltpu.SemaphoreType.DMA((7,)),
        pltpu.SemaphoreType.DMA((256,)),
        pltpu.SemaphoreType.DMA((256,)),
    ]
    return pl.pallas_call(
        moe_kernel,
        out_shape=jax.ShapeDtypeStruct((FEATS, LANES), F32),
        in_specs=[any_space, any_space, any_space, vmem, vmem, vmem, vmem, any_space, any_space, any_space],
        out_specs=vmem,
        scratch_shapes=scratch,
        compiler_params=pltpu.CompilerParams(
            collective_id=0, has_side_effects=True, vmem_limit_bytes=60 * 1024 * 1024
        ),
        cost_estimate=pl.CostEstimate(flops=7 * 10**9, bytes_accessed=16 * 2**20, transcendentals=0),
    )(head_values, output_proj, hidden, *gains, share, gate, up, down)


def body(
    query_latent, query_rope, cache_latent, cache_rope, lengths, value_up, output_proj, hidden,
    norm_gain, route_ids, route_weights, gate_proj, up_proj, down_proj,
):
    users_here, heads_here, latent_width = query_latent.shape
    history = cache_latent.shape[1]
    rope_width = cache_rope.shape[1]
    positional = query_rope.reshape(users_here, heads_here, rope_width)
    scores = jnp.einsum(
        "rhc,rtc->rht", query_latent, cache_latent, preferred_element_type=jnp.float32
    )
    scores = scores + jnp.einsum(
        "rhe,ret->rht", positional, cache_rope, preferred_element_type=jnp.float32
    )
    scores = scores * (NOPE + ROPE) ** (-0.5)
    visible = jnp.arange(history, dtype=jnp.int32)[None, None, :] < lengths[:, None, None]
    scores = jnp.where(visible, scores, -1e30)
    highest = jnp.max(scores, axis=-1, keepdims=True)
    exponent = jnp.exp(scores - highest)
    attn_weights = (exponent / jnp.sum(exponent, axis=-1, keepdims=True)).astype(jnp.bfloat16)
    context = jnp.einsum(
        "rht,rtc->rhc", attn_weights, cache_latent, preferred_element_type=jnp.float32
    ).astype(jnp.bfloat16)
    head_values = jnp.einsum(
        "rhc,hcv->rhv", context, value_up, preferred_element_type=jnp.float32
    ).astype(jnp.bfloat16)
    head_values = head_values.reshape(users_here, 2, -1).transpose(1, 0, 2)

    expert = lax.axis_index("dev")
    share = jnp.sum(jnp.where(route_ids == expert, route_weights, 0.0), axis=1).reshape(4, 1, LANES)
    out = remote_part(
        head_values, output_proj, hidden, gain_planes(norm_gain), share,
        gate_proj.reshape(2, 4, 4, FEATS, 256), up_proj.reshape(2, 4, 4, FEATS, 256), down_proj[0],
    )
    return out.T.astype(BF16)


def solution(mesh):
    return jax.shard_map(
        body,
        mesh=mesh,
        in_specs=(
            P("dev", "sec", None),
            P("dev", "sec"),
            P("dev", None, None),
            P("dev", None, None),
            P("dev"),
            P("sec", None, None),
            P("sec", "dev"),
            P(None, "dev"),
            P(),
            P(),
            P(),
            P("dev", None, "sec"),
            P("dev", None, "sec"),
            P("dev", "sec", None),
        ),
        out_specs=P("sec", "dev"),
        check_vma=False,
    )
```

```python
import functools

import jax
import jax.numpy as jnp
from jax import lax
from jax.experimental import pallas as pl
from jax.experimental.pallas import tpu as pltpu
from jax.sharding import PartitionSpec as P

ROPE = 64
NOPE = 128
norm_eps = 1e-06
MESH = pl.DeviceIdType.MESH
F32 = jnp.float32
BF16 = jnp.bfloat16

PARTS = ((0, 80, "xyz"), (80, 80, "zxy"), (160, 64, "yzx"))
FEATS = 224
LANES = 128
GROUP = 4


def weight_plane(ref, p, j):
    first, rows, _ = PARTS[p]
    if p == 0:
        block = ref[:, :, j, first : first + rows, :]
    elif p == 1:
        block = ref[:, j, :, first : first + rows, :]
    else:
        block = ref[j, :, :, first : first + rows, :]
    return block.reshape(-1, block.shape[-1])


def at(ref, **index):
    return ref.at[tuple(index.get(axis, slice(None)) for axis in "xyz")]


def get(ref, **index):
    return ref[tuple(index.get(axis, slice(None)) for axis in "xyz")]


def layer_kernel(
    query_hbm, rope_hbm, cache_hbm, keys_hbm, lengths_ref, value_up_hbm,
    out_proj_hbm, hidden_hbm, gain_ref, ids_ref, weights_ref, gate_hbm, up_hbm, down_hbm,
    out_ref,
    query, rope, positional, cache, keys, context, value_up,
    heads0, heads1, out_proj, attn, pair_in, far_in, far_out, hidden,
    weight_in, down_in, gain0, gain1, gain2, wt0, wt1, wt2, downt,
    rt0, rt1, rt2, gate_up, act, o0, o1, o2,
    r1_0, r1_1, r1_2, r2_0, r2_1, r2_2, r3_0, r3_1, r3_2, r4_0, r4_1, r4_2, r5_0, r5_1, r5_2,
    cache_sem, local_sem, send_sem, recv_sem,
):
    sec = lax.axis_index("sec")
    dev = lax.axis_index("dev")
    x_hi, core = sec // 2, lax.rem(sec, 2)
    x_lo = dev // 16
    me = {
        "x": x_hi * 2 + x_lo,
        "y": lax.rem(dev // 4, 4),
        "z": lax.rem(dev, 4),
    }

    def shift(axis, by):
        return lax.rem(me[axis] + (by % 4), 4)

    def device(x, y, z, c):
        return ((x // 2) * 2 + c, lax.rem(x, 2) * 16 + y * 4 + z)

    def neighbour(axis, by):
        place = dict(me)
        place[axis] = shift(axis, by)
        return device(place["x"], place["y"], place["z"], core)

    partner = device(me["x"], me["y"], me["z"], 1 - core)
    x_lo_partner = (sec, (1 - x_lo) * 16 + me["y"] * 4 + me["z"])

    tags = {}
    sent = []

    def number(tag):
        return tags.setdefault(tag, len(tags))

    def send(tag, src, dst, to):
        i = number(tag)
        copy = pltpu.make_async_remote_copy(
            src_ref=src, dst_ref=dst, send_sem=send_sem.at[i], recv_sem=recv_sem.at[i],
            device_id=to, device_id_type=MESH,
        )
        copy.start()
        sent.append(copy)

    def recv(tag, region):
        i = number(tag)
        pltpu.make_async_remote_copy(
            src_ref=region, dst_ref=region, send_sem=send_sem.at[i], recv_sem=recv_sem.at[i],
            device_id=partner, device_id_type=MESH,
        ).wait_recv()

    around = [neighbour(axis, by) for axis in "xyz" for by in (1, 2, 3)] + [partner]
    barrier = pltpu.get_barrier_semaphore()
    for other in around:
        pl.semaphore_signal(barrier, inc=1, device_id=other, device_id_type=MESH)

    heads = (heads0, heads1)
    half = heads0.shape[-1]
    own_heads = [at(h, x=x_lo, y=me["y"], z=me["z"]) for h in heads]
    my_hidden = hidden_hbm.at[:, pl.ds(pl.multiple_of(sec * LANES, LANES), LANES)]

    def user_loads(step):
        slot = lax.rem(step, 2) if not isinstance(step, int) else step % 2
        users, place = pl.ds(step * GROUP, GROUP), pl.ds(slot * GROUP, GROUP)
        return (
            pltpu.make_async_copy(cache_hbm.at[users], cache.at[place], cache_sem.at[slot, 0]),
            pltpu.make_async_copy(keys_hbm.at[users], keys.at[place], cache_sem.at[slot, 1]),
        )

    loads = [
        pltpu.make_async_copy(rope_hbm, rope, local_sem.at[0]),
        pltpu.make_async_copy(query_hbm, query, local_sem.at[1]),
        pltpu.make_async_copy(value_up_hbm, value_up, local_sem.at[2]),
        pltpu.make_async_copy(gate_hbm, weight_in, local_sem.at[3]),
        pltpu.make_async_copy(out_proj_hbm, out_proj, local_sem.at[4]),
        pltpu.make_async_copy(down_hbm, down_in, local_sem.at[5]),
        pltpu.make_async_copy(my_hidden, hidden, local_sem.at[6]),
        pltpu.make_async_copy(up_hbm, weight_in, local_sem.at[7]),
    ]
    for copy in (loads[0], loads[1], *user_loads(0), *user_loads(1)):
        copy.start()
    for n in (2, 3, 4, 5, 6):
        loads[n].start()

    for p, gain in enumerate((gain0, gain1, gain2)):
        first, rows, _ = PARTS[p]
        width = gain.shape[-1]
        column = lax.broadcasted_iota(jnp.int32, (rows, width), 1)
        spread = (lax.rem(column, rows) == lax.broadcasted_iota(jnp.int32, (rows, width), 0)).astype(F32)
        spread = jnp.dot(
            gain_ref[:, first : first + rows], spread,
            preferred_element_type=F32, precision=lax.Precision.HIGHEST,
        )
        block = lax.broadcasted_iota(jnp.int32, (32, width), 1) // rows
        owner = lax.broadcasted_iota(jnp.int32, (32, width), 0)
        for j in range(gain.shape[0]):
            if p == 0:
                wanted = block * 4 + j
            elif p == 1:
                wanted = (block // 4) * 16 + j * 4 + lax.rem(block, 4)
            else:
                wanted = j * 16 + block
            gain[j] = jnp.sum(jnp.where(owner == wanted, spread, 0.0), axis=0, keepdims=True)

    users_here, heads_here = query.shape[0], query.shape[1]
    loads[0].wait()
    wide = heads_here * ROPE
    owner = lax.broadcasted_iota(jnp.int32, (heads_here, wide), 1) // ROPE
    mask = owner == lax.broadcasted_iota(jnp.int32, (heads_here, wide), 0)
    fold = lax.rem(lax.broadcasted_iota(jnp.int32, (wide, ROPE), 0), ROPE)
    fold = (fold == lax.broadcasted_iota(jnp.int32, (wide, ROPE), 1)).astype(F32).astype(BF16)
    for r in range(users_here):
        row = jnp.broadcast_to(rope[r : r + 1, :].astype(F32), (heads_here, wide))
        row = jnp.where(mask, row, 0.0).astype(BF16)
        positional[r] = jnp.dot(row, fold, preferred_element_type=F32).astype(BF16)
    loads[1].wait()
    history = cache.shape[1]
    moment = lax.broadcasted_iota(jnp.int32, (heads_here, history), 1)

    def attend(step, carry):
        slot = lax.rem(step, 2)
        for copy in user_loads(step):
            copy.wait()
        weights = []
        for n in range(GROUP):
            r = step * GROUP + n
            place = slot * GROUP + n
            scores = lax.dot_general(
                query[r], cache[place], (((1,), (1,)), ((), ())), preferred_element_type=F32
            )
            scores += jnp.dot(positional[r], keys[place], preferred_element_type=F32)
            scores = scores * (NOPE + ROPE) ** (-0.5)
            scores = jnp.where(moment < lengths_ref[r], scores, -1e30)
            exponent = jnp.exp(scores - jnp.max(scores, axis=-1, keepdims=True))
            weights.append((exponent / jnp.sum(exponent, axis=-1, keepdims=True)).astype(BF16))
        for n in range(GROUP):
            r = step * GROUP + n
            value = jnp.dot(weights[n], cache[slot * GROUP + n], preferred_element_type=F32)
            value = value.astype(BF16).astype(F32)
            rows = pl.ds(pl.multiple_of(r * heads_here, heads_here), heads_here)
            for t in range(context.shape[0]):
                context[t, rows, :] = value[:, t * LANES : (t + 1) * LANES]

        @pl.when(step < users_here // GROUP - 2)
        def _():
            for copy in user_loads(step + 2):
                copy.start()

        return carry

    lax.fori_loop(0, users_here // GROUP, attend, 0)
    loads[2].wait()

    def head_value(h):
        tiles = [context[t, pl.ds(h, users_here, stride=heads_here), :] for t in range(context.shape[0])]
        rows = jnp.concatenate(tiles, axis=1).astype(BF16)
        value = jnp.dot(rows, value_up[h], preferred_element_type=F32)
        return value.astype(BF16)

    order = (("y", "z"), ("z", "y"))

    def head_block(p, k, **index):
        place = {"x": lax.rem(x_lo + k, 2), "y": me["y"], "z": me["z"]}
        place.update(index)
        return at(heads[p], **place)

    def head_slab(p, **index):
        return at(heads[p], **index)

    for p in range(2):
        for h in range(heads_here // 2):
            heads[p][x_lo, me["y"], me["z"], :, h * 128 : h * 128 + 128] = head_value(p * (heads_here // 2) + h)
        if p == 0:
            pl.semaphore_wait(barrier, len(around))
        send(("hx", p), own_heads[p], own_heads[p], x_lo_partner)
        b, c = order[p]
        for by in (1, 3):
            send(("hb", p, 0, by), own_heads[p], own_heads[p], neighbour(b, by))

    wts = (wt0, wt1, wt2)
    gains = (gain0, gain1, gain2)

    def transpose_part(p, which):
        def step(j, carry):
            block = weight_plane(weight_in, p, j).T.astype(F32) * gains[p][j]
            wts[p][j, 0, which * 256 : which * 256 + 256, :] = block.astype(BF16)
            return carry

        lax.fori_loop(0, wts[p].shape[0], step, 0)

    def transpose_down():
        def step(j, carry):
            block = down_in[:, pl.ds(pl.multiple_of(j * 896, 896), 896)].T
            downt[0, j // 4, lax.rem(j, 4)] = block.reshape(4, FEATS, 256)
            return carry

        lax.fori_loop(0, 8, step, 0)

    def share_part(p):
        send(("wt", p), wts[p].at[:, 0], wts[p].at[:, 1], partner)

    def gate_task(p):
        if p == 0:
            loads[3].wait()
        transpose_part(p, 0)
        if p == 2:
            loads[7].start()

    def up_task(p):
        if p == 0:
            loads[7].wait()
        transpose_part(p, 1)
        share_part(p)

    def down_task():
        loads[5].wait()
        transpose_down()
        send(("dn",), downt.at[0], downt.at[1], partner)

    tasks = [functools.partial(gate_task, p) for p in range(3)] + [down_task]
    tasks += [functools.partial(up_task, p) for p in range(3)]

    def work():
        if tasks:
            tasks.pop(0)()

    work()

    def slab_sends(p, m):
        b, c = order[p]
        slab = head_slab(p, **{b: shift(b, m), c: me[c]})
        for by in (1, 3):
            send(("hc", p, m, by), slab, slab, neighbour(c, by))

    for p in range(2):
        b, c = order[p]
        other = head_block(p, 1)
        recv(("hx", p), other)
        for by in (1, 3):
            send(("hb", p, 1, by), other, other, neighbour(b, by))
    for p in range(2):
        slab_sends(p, 0)
    work()
    for p in range(2):
        b, c = order[p]
        block = head_block(p, 0, **{b: shift(b, 3)})
        recv(("hb", p, 0, 1), block)
        send(("hf", p, 0), block, block, neighbour(b, 1))
        recv(("hb", p, 0, 3), head_block(p, 0, **{b: shift(b, 1)}))
    for p in range(2):
        b, c = order[p]
        block = head_block(p, 1, **{b: shift(b, 1)})
        recv(("hb", p, 1, 3), block)
        send(("hf", p, 1), block, block, neighbour(b, 3))
        slab_sends(p, 1)
        recv(("hb", p, 1, 1), head_block(p, 1, **{b: shift(b, 3)}))
        slab_sends(p, 3)
    work()
    for p in range(2):
        b, c = order[p]
        for k in range(2):
            recv(("hf", p, k), head_block(p, k, **{b: shift(b, 2)}))
        slab_sends(p, 2)
    work()

    def project(p, by, first=False):
        c = order[p][1]
        j = shift(c, by)
        rows = get(heads[p], **{c: j}).reshape(-1, half)
        product = lax.dot_general(
            rows, out_proj[:, p * half : (p + 1) * half], (((1,), (1,)), ((), ())), preferred_element_type=F32
        )
        product = product.reshape(2, 4, 16, FEATS)
        if c == "z":
            attn[:, :, j] = product
        else:
            attn[:, j] += product

    loads[4].wait()
    project(0, 0)
    for m in (0, 1, 3, 2):
        for p in range(2):
            b, c = order[p]
            for by in (1, 3):
                region = head_slab(p, **{b: shift(b, m), c: shift(c, -by)})
                recv(("hc", p, m, by), region)
                if (m in (0, 1)) == (by == 1):
                    send(("hd", p, m), region, region, neighbour(c, by))
        work()
    while tasks:
        work()
    project(0, 1)
    project(0, 3)
    for m in (0, 3, 1, 2):
        for p in range(2):
            b, c = order[p]
            recv(("hd", p, m), head_slab(p, **{b: shift(b, m), c: shift(c, 2)}))
    project(0, 2)
    for by in (0, 1, 3, 2):
        project(1, by)

    attn_mine = attn.at[:, pl.ds(core * 2, 2)]
    send(("pair",), attn.at[:, pl.ds((1 - core) * 2, 2)], pair_in, partner)
    recv(("pair",), pair_in)
    far_out[...] = (attn_mine[1 - x_hi] + pair_in[1 - x_hi]).astype(BF16)
    send(("far",), far_out, far_in, neighbour("x", 2))
    loads[6].wait()
    near = (attn_mine[x_hi] + pair_in[x_hi]).reshape(LANES, FEATS)
    recv(("far",), far_in)
    residual = near + far_in[...].reshape(LANES, FEATS).astype(F32)
    residual = jnp.concatenate([residual, jnp.zeros((LANES, 32), F32)], axis=1).T[:FEATS]
    residual = residual + hidden[...].astype(F32)
    out_ref[...] = residual
    routed = residual.astype(BF16)

    rts = (rt0, rt1, rt2)
    for p, (first, rows, _) in enumerate(PARTS):
        rts[p][me["x"], me["y"], me["z"]] = routed[first : first + rows]

    def spot(p, **index):
        place = dict(me)
        place.update(index)
        return at(rts[p], **place)

    axes = [tuple(o) for _, _, o in PARTS]
    for p in range(3):
        a, b, c = axes[p]
        for by in (1, 3, 2):
            send(("ga", p, by), spot(p), spot(p), neighbour(a, by))
        for by in (1, 3):
            send(("gb", p, 0, by), spot(p), spot(p), neighbour(b, by))

    def plane_group(p, m):
        a, b, c = axes[p]
        slab = at(rts[p], **{b: shift(b, m), c: me[c]})
        for by in (1, 3):
            send(("gc", p, m, by), slab, slab, neighbour(c, by))

    for k in (1, 3, 2):
        for p in range(3):
            a, b, c = axes[p]
            block = spot(p, **{a: shift(a, k)})
            recv(("ga", p, 4 - k), block)
            for by in (1, 3):
                send(("gb", p, k, by), block, block, neighbour(b, by))
    for p in range(3):
        plane_group(p, 0)
    for k in (0, 1, 3, 2):
        for p in range(3):
            a, b, c = axes[p]
            for by in (1, 3):
                block = spot(p, **{a: shift(a, k), b: shift(b, -by)})
                recv(("gb", p, k, by), block)
                if (k in (0, 1)) == (by == 1):
                    send(("gf", p, k), block, block, neighbour(b, by))
    for p in range(3):
        plane_group(p, 3)
        plane_group(p, 1)
    def pass_on(m):
        for p in range(3):
            a, b, c = axes[p]
            for by in (1, 3):
                region = at(rts[p], **{b: shift(b, m), c: shift(c, -by)})
                recv(("gc", p, m, by), region)
                if (m in (0, 1)) == (by == 1):
                    send(("gd", p, m), region, region, neighbour(c, by))

    for p in range(3):
        a, b, c = axes[p]
        for k in (0, 1, 3, 2):
            recv(("gf", p, k), spot(p, **{a: shift(a, k), b: shift(b, 2)}))
        plane_group(p, 2)
    pass_on(0)

    for p in range(3):
        recv(("wt", p), wts[p].at[:, 1])
    totals = {"square": jnp.zeros((1, 256), F32), "first": True}

    def users_of(p, by):
        if p == 0:
            block = rts[0][:, :, shift("z", by)]
            low, high = block[0:2], block[2:4]
        elif p == 1:
            block = rts[1][:, shift("y", by)]
            low, high = block[0:2], block[2:4]
        else:
            plane = lax.rem(x_lo + by, 2)
            low, high = rts[2][plane], rts[2][plane + 2]
        return jnp.concatenate([low.reshape(-1, LANES), high.reshape(-1, LANES)], axis=1)

    def plane_of(p, by):
        if p == 2:
            return lax.rem(x_lo + by, 2)
        return shift(axes[p][2], by)

    def multiply(p, by):
        rows = users_of(p, by)
        wide = rows.astype(F32)
        totals["square"] = totals["square"] + jnp.sum(wide * wide, axis=0, keepdims=True)
        weight = wts[p][plane_of(p, by)]
        product = jnp.dot(weight.reshape(1024, weight.shape[-1]), rows, preferred_element_type=F32)
        if totals["first"]:
            gate_up[...] = product
        else:
            gate_up[...] += product
        totals["first"] = False

    multiply(0, 0)
    multiply(1, 0)
    for m in (1, 3, 2):
        pass_on(m)
    for by in (1, 3):
        multiply(0, by)
        multiply(1, by)
    multiply(2, 1)
    for p in range(3):
        a, b, c = axes[p]
        for m in (0, 3, 1, 2):
            recv(("gd", p, m), at(rts[p], **{b: shift(b, m), c: shift(c, 2)}))
        multiply(p, 2 if p < 2 else 0)

    scale = lax.rsqrt(totals["square"] * (1.0 / (32 * FEATS)) + norm_eps)
    for slot in range(2):
        gate = gate_up[slot * 512 : slot * 512 + 256] * scale
        upward = gate_up[slot * 512 + 256 : slot * 512 + 512] * scale
        act[slot * 256 : slot * 256 + 256] = (gate / (1.0 + jnp.exp(-gate)) * upward).astype(BF16)

    recv(("dn",), downt.at[1])
    outs = (o0, o1, o2)
    r1, r2, r3, r4, r5 = (
        (r1_0, r1_1, r1_2), (r2_0, r2_1, r2_2), (r3_0, r3_1, r3_2), (r4_0, r4_1, r4_2), (r5_0, r5_1, r5_2)
    )
    share = jnp.sum(jnp.where(ids_ref[...] == dev, weights_ref[...], 0.0), axis=0, keepdims=True)
    share = jnp.where(
        core == 0,
        jnp.concatenate([share[:, 0:128], share[:, 256:384]], axis=1),
        jnp.concatenate([share[:, 128:256], share[:, 384:512]], axis=1),
    )

    def down(p, by):
        first, rows, _ = PARTS[p]
        j = plane_of(p, by)
        product = jnp.dot(weight_plane(downt.at[0], p, j), act[0:256], preferred_element_type=F32)
        product += jnp.dot(weight_plane(downt.at[1], p, j), act[256:512], preferred_element_type=F32)
        product = (product * share).astype(BF16)
        for h in range(2):
            lanes = product[:, h * LANES : (h + 1) * LANES]
            if p == 0:
                o0[2 * h : 2 * h + 2, :, j] = lanes.reshape(2, 4, rows, LANES)
            elif p == 1:
                o1[2 * h : 2 * h + 2, j] = lanes.reshape(2, 4, rows, LANES)
            else:
                o2[j + 2 * h] = lanes.reshape(4, 4, rows, LANES)

    def o_slab(p, by, m):
        a, b, c = axes[p]
        return at(outs[p], **{c: shift(c, by), b: shift(b, m)})

    for p in range(3):
        c = axes[p][2]
        down(p, 2 if p < 2 else 0)
        for m in (2, 0, 3, 1):
            by = 1 if m in (0, 1) else 3
            send(("s1", p, m), o_slab(p, 2, m), r1[p].at[m], neighbour(c, by))
    for p in range(3):
        c = axes[p][2]
        if p < 2:
            down(p, 1)
            down(p, 3)
        else:
            down(p, 1)
        for m in (2, 3):
            send(("s2", p, 0, m), o_slab(p, 1, m), r2[p].at[0, m], neighbour(c, 1))
        for m in (1, 0):
            send(("s2", p, 1, m), o_slab(p, 3, m), r2[p].at[1, m], neighbour(c, 3))
    for p in range(2):
        down(p, 0)

    def add_to(slab, other):
        slab[...] = (slab[...].astype(F32) + other[...].astype(F32)).astype(BF16)

    for m in (2, 1, 3, 0):
        for p in range(3):
            c = axes[p][2]
            recv(("s1", p, m), r1[p].at[m])
            by = 1 if m in (0, 1) else 3
            side = 0 if by == 1 else 1
            slab = o_slab(p, by, m)
            add_to(slab, r1[p].at[m])
            send(("s2", p, side, m), slab, r2[p].at[side, m], neighbour(c, by))

    for m in (2, 1, 3, 0):
        for p in range(3):
            a, b, c = axes[p]
            slab = o_slab(p, 0, m)
            for side in range(2):
                recv(("s2", p, side, m), r2[p].at[side, m])
            slab[...] = (
                slab[...].astype(F32) + r2[p][0, m].astype(F32) + r2[p][1, m].astype(F32)
            ).astype(BF16)
            if m == 2:
                send(("s3", p, 0), slab.at[0:2], r3[p].at[0:2], neighbour(b, 1))
                send(("s3", p, 1), slab.at[2:4], r3[p].at[2:4], neighbour(b, 3))
            elif m == 1:
                send(("s4", p, 0, 1), slab.at[2:4], r4[p].at[0, 2:4], neighbour(b, 1))
            elif m == 3:
                send(("s4", p, 1, 0), slab.at[0:2], r4[p].at[1, 0:2], neighbour(b, 3))
    for p in range(3):
        a, b, c = axes[p]
        recv(("s3", p, 0), r3[p].at[0:2])
        slab = o_slab(p, 0, 1).at[0:2]
        add_to(slab, r3[p].at[0:2])
        send(("s4", p, 0, 0), slab, r4[p].at[0, 0:2], neighbour(b, 1))
        recv(("s3", p, 1), r3[p].at[2:4])
        slab = o_slab(p, 0, 3).at[2:4]
        add_to(slab, r3[p].at[2:4])
        send(("s4", p, 1, 1), slab, r4[p].at[1, 2:4], neighbour(b, 3))
    for p in range(3):
        a, b, c = axes[p]
        for side in range(2):
            for lower in range(2):
                recv(("s4", p, side, lower), r4[p].at[side, 2 * lower : 2 * lower + 2])
        slab = o_slab(p, 0, 0)
        slab[...] = (
            slab[...].astype(F32) + r4[p][0].astype(F32) + r4[p][1].astype(F32)
        ).astype(BF16)
        for k in (2, 1, 3):
            send(("s5", p, k), slab.at[shift(a, k)], r5[p].at[k - 1], neighbour(a, k))
    for p, (first, rows, _) in enumerate(PARTS):
        a = axes[p][0]
        total = out_ref[first : first + rows, :] + outs[p][me["x"], me["y"], me["z"]].astype(F32)
        for k in (1, 3, 2):
            recv(("s5", p, k), r5[p].at[k - 1])
            total = total + r5[p][k - 1].astype(F32)
        out_ref[first : first + rows, :] = total
    for copy in sent:
        copy.wait_send()


def body(
    query_latent, query_rope, cache_latent, cache_rope, lengths, value_up, output_proj, hidden,
    norm_gain, route_ids, route_weights, gate_proj, up_proj, down_proj,
):
    def bf(*shape):
        return pltpu.VMEM(shape, BF16)

    def f32(*shape):
        return pltpu.VMEM(shape, F32)

    users, heads, latent = query_latent.shape
    history = cache_latent.shape[1]
    half = heads * LANES // 2
    rows = [r for _, r, _ in PARTS]
    hbm = pl.BlockSpec(memory_space=pl.ANY)
    vmem = pl.BlockSpec(memory_space=pltpu.VMEM)
    scratch = [
        bf(users, heads, latent), bf(users, heads * ROPE), bf(users, heads, ROPE),
        bf(2 * GROUP, history, latent), bf(2 * GROUP, ROPE, history), f32(latent // LANES, users * heads, LANES),
        bf(*value_up.shape),
        bf(2, 4, 4, 16, half), bf(2, 4, 4, 16, half), bf(FEATS, 2 * half), f32(2, 4, 4, 16, FEATS),
        f32(2, 2, 4, 16, FEATS), bf(2, 4, 16, FEATS), bf(2, 4, 16, FEATS), bf(FEATS, LANES),
        bf(2, 4, 4, FEATS, 256), bf(256, 32 * FEATS),
        f32(4, 1, 640), f32(4, 1, 640), f32(2, 1, 1024),
        bf(4, 2, 512, 640), bf(4, 2, 512, 640), bf(2, 2, 512, 1024), bf(2, 2, 4, 4, FEATS, 256),
        *[bf(4, 4, 4, r, LANES) for r in rows],
        f32(1024, 256), bf(512, 256),
        *[bf(4, 4, 4, r, LANES) for r in rows],
        *[bf(4, 4, r, LANES) for r in rows],
        *[bf(2, 4, 4, r, LANES) for r in rows],
        *[bf(4, r, LANES) for r in rows],
        *[bf(2, 4, r, LANES) for r in rows],
        *[bf(3, r, LANES) for r in rows],
        pltpu.SemaphoreType.DMA((2, 2)),
        pltpu.SemaphoreType.DMA((8,)),
        pltpu.SemaphoreType.DMA((256,)),
        pltpu.SemaphoreType.DMA((256,)),
    ]
    out = pl.pallas_call(
        layer_kernel,
        out_shape=jax.ShapeDtypeStruct((FEATS, LANES), F32),
        in_specs=[
            hbm, hbm, hbm, hbm, pl.BlockSpec(memory_space=pltpu.SMEM), hbm,
            hbm, hbm, vmem, vmem, vmem, hbm, hbm, hbm,
        ],
        out_specs=vmem,
        scratch_shapes=scratch,
        compiler_params=pltpu.CompilerParams(
            collective_id=0, has_side_effects=True, vmem_limit_bytes=63 * 1024 * 1024
        ),
        cost_estimate=pl.CostEstimate(flops=9 * 10**9, bytes_accessed=27 * 2**20, transcendentals=0),
    )(
        query_latent, query_rope, cache_latent, cache_rope, lengths, value_up,
        output_proj.T, hidden.T, norm_gain.reshape(32, FEATS), route_ids.T, route_weights.T,
        gate_proj.reshape(2, 4, 4, FEATS, 256), up_proj.reshape(2, 4, 4, FEATS, 256), down_proj[0],
    )
    return out.T.astype(BF16)


def solution(mesh):
    return jax.shard_map(
        body,
        mesh=mesh,
        in_specs=(
            P("dev", "sec", None),
            P("dev", "sec"),
            P("dev", None, None),
            P("dev", None, None),
            P("dev"),
            P("sec", None, None),
            P("sec", "dev"),
            P(None, "dev"),
            P(),
            P(),
            P(),
            P("dev", None, "sec"),
            P("dev", None, "sec"),
            P("dev", "sec", None),
        ),
        out_specs=P("sec", "dev"),
        check_vma=False,
    )
```

```python
import functools

import jax
import jax.numpy as jnp
from jax import lax
from jax.experimental import pallas as pl
from jax.experimental.pallas import tpu as pltpu
from jax.sharding import PartitionSpec as P

ROPE = 64
NOPE = 128
norm_eps = 1e-06
MESH = pl.DeviceIdType.MESH
F32 = jnp.float32
BF16 = jnp.bfloat16

PARTS = ((0, 80, "xyz"), (80, 80, "zxy"), (160, 64, "yzx"))
FEATS = 224
LANES = 128
GROUP = 4


def weight_plane(ref, p, j):
    first, rows, _ = PARTS[p]
    if p == 0:
        block = ref[:, :, j, first : first + rows, :]
    elif p == 1:
        block = ref[:, j, :, first : first + rows, :]
    else:
        block = ref[j, :, :, first : first + rows, :]
    return block.reshape(-1, block.shape[-1])


def at(ref, **index):
    return ref.at[tuple(index.get(axis, slice(None)) for axis in "xyz")]


def get(ref, **index):
    return ref[tuple(index.get(axis, slice(None)) for axis in "xyz")]


def layer_kernel(
    query_hbm, rope_hbm, cache_hbm, keys_hbm, lengths_ref, value_up_hbm,
    out_proj_hbm, hidden_hbm, gain_ref, ids_ref, weights_ref, gate_hbm, up_hbm, down_hbm,
    out_ref, gate_far, up_far, down_far,
    query, rope, positional, cache, keys, context, value_up,
    heads0, heads1, out_proj, attn, pair_in, far_in, far_out, hidden,
    weight_in, down_in, gain0, gain1, gain2, wt0, wt1, wt2, downt,
    rt0, rt1, rt2, gate_up, act, o0, o1, o2,
    r1_0, r1_1, r1_2, r2_0, r2_1, r2_2, r3_0, r3_1, r3_2, r4_0, r4_1, r4_2, r5_0, r5_1, r5_2,
    kept, cache_sem, local_sem, stage_sem, send_sem, recv_sem,
):
    sec = lax.axis_index("sec")
    dev = lax.axis_index("dev")
    x_hi, core = sec // 2, lax.rem(sec, 2)
    x_lo = dev // 16
    me = {
        "x": x_hi * 2 + x_lo,
        "y": lax.rem(dev // 4, 4),
        "z": lax.rem(dev, 4),
    }

    def shift(axis, by):
        return lax.rem(me[axis] + (by % 4), 4)

    def device(x, y, z, c):
        return ((x // 2) * 2 + c, lax.rem(x, 2) * 16 + y * 4 + z)

    def neighbour(axis, by):
        place = dict(me)
        place[axis] = shift(axis, by)
        return device(place["x"], place["y"], place["z"], core)

    partner = device(me["x"], me["y"], me["z"], 1 - core)
    x_lo_partner = (sec, (1 - x_lo) * 16 + me["y"] * 4 + me["z"])

    tags = {}
    sent = []

    def number(tag):
        return tags.setdefault(tag, len(tags))

    def send(tag, src, dst, to):
        i = number(tag)
        copy = pltpu.make_async_remote_copy(
            src_ref=src, dst_ref=dst, send_sem=send_sem.at[len(sent)], recv_sem=recv_sem.at[i],
            device_id=to, device_id_type=MESH,
        )
        copy.start()
        sent.append(copy)

    def drain():
        while sent:
            sent.pop().wait_send()

    def recv(tag, region):
        i = number(tag)
        pltpu.make_async_remote_copy(
            src_ref=region, dst_ref=region, send_sem=send_sem.at[0], recv_sem=recv_sem.at[i],
            device_id=partner, device_id_type=MESH,
        ).wait_recv()


    around = [neighbour(axis, by) for axis in "xyz" for by in (1, 2, 3)] + [partner]
    barrier = pltpu.get_barrier_semaphore()
    for other in around:
        pl.semaphore_signal(barrier, inc=1, device_id=other, device_id_type=MESH)

    heads = (heads0, heads1)
    half = heads0.shape[-1]
    own_heads = [at(h, x=x_lo, y=me["y"], z=me["z"]) for h in heads]
    my_hidden = hidden_hbm.at[:, pl.ds(pl.multiple_of(sec * LANES, LANES), LANES)]

    def user_loads(step):
        slot = lax.rem(step, 2) if not isinstance(step, int) else step % 2
        users, place = pl.ds(step * GROUP, GROUP), pl.ds(slot * GROUP, GROUP)
        return (
            pltpu.make_async_copy(cache_hbm.at[users], cache.at[place], cache_sem.at[slot, 0]),
            pltpu.make_async_copy(keys_hbm.at[users], keys.at[place], cache_sem.at[slot, 1]),
        )

    def stage_up(source, n):
        copies = []
        for p, (first, rows, _) in enumerate(PARTS):
            for q in range(2):
                copies.append(
                    pltpu.make_async_copy(
                        source.at[:, :, :, pl.ds(first, rows), pl.ds(q * LANES, LANES)],
                        (o0, o1, o2)[p].at[pl.ds(2 * q, 2)],
                        stage_sem.at[n, 2 * p + q],
                    )
                )
        return copies

    loads = [
        pltpu.make_async_copy(rope_hbm, rope, local_sem.at[0]),
        pltpu.make_async_copy(query_hbm, query, local_sem.at[1]),
        pltpu.make_async_copy(value_up_hbm, value_up, local_sem.at[2]),
        pltpu.make_async_copy(gate_hbm, weight_in, local_sem.at[3]),
        pltpu.make_async_copy(out_proj_hbm, out_proj, local_sem.at[4]),
        pltpu.make_async_copy(down_hbm, down_in, local_sem.at[5]),
        pltpu.make_async_copy(my_hidden, hidden, local_sem.at[6]),
        pltpu.make_async_copy(gate_far, weight_in, local_sem.at[7]),
        pltpu.make_async_copy(down_far, down_in, local_sem.at[8]),
    ]
    up_loads = stage_up(up_hbm, 0), stage_up(up_far, 1)
    for copy in (loads[0], loads[1], *user_loads(0), *user_loads(1)):
        copy.start()
    loads[2].start()

    for p, gain in enumerate((gain0, gain1, gain2)):
        first, rows, _ = PARTS[p]
        width = gain.shape[-1]
        block = lax.broadcasted_iota(jnp.int32, (LANES, width), 1) // rows
        offset = lax.rem(lax.broadcasted_iota(jnp.int32, (LANES, width), 1), rows) + first
        lane = lax.broadcasted_iota(jnp.int32, (LANES, width), 0)
        for j in range(gain.shape[0]):
            if p == 0:
                owner = block * 4 + j
            elif p == 1:
                owner = (block // 4) * 16 + j * 4 + lax.rem(block, 4)
            else:
                owner = j * 16 + block
            place = owner * FEATS + offset
            spread = jnp.dot(
                gain_ref[...], (lax.rem(place, LANES) == lane).astype(F32),
                preferred_element_type=F32, precision=lax.Precision.HIGHEST,
            )
            held = (place // LANES)[:56] == lane[:56]
            gain[j] = jnp.sum(jnp.where(held, spread, 0.0), axis=0, keepdims=True)

    users_here, heads_here = query.shape[0], query.shape[1]
    loads[0].wait()
    wide = heads_here * ROPE
    owner = lax.broadcasted_iota(jnp.int32, (heads_here, wide), 1) // ROPE
    mask = owner == lax.broadcasted_iota(jnp.int32, (heads_here, wide), 0)
    fold = lax.rem(lax.broadcasted_iota(jnp.int32, (wide, ROPE), 0), ROPE)
    fold = (fold == lax.broadcasted_iota(jnp.int32, (wide, ROPE), 1)).astype(F32).astype(BF16)
    for r in range(users_here):
        row = jnp.broadcast_to(rope[r : r + 1, :].astype(F32), (heads_here, wide))
        row = jnp.where(mask, row, 0.0).astype(BF16)
        positional[r] = jnp.dot(row, fold, preferred_element_type=F32).astype(BF16)
    loads[1].wait()
    history = cache.shape[1]
    moment = lax.broadcasted_iota(jnp.int32, (heads_here, history), 1)

    def attend(step, carry):
        slot = lax.rem(step, 2)
        for copy in user_loads(step):
            copy.wait()
        weights = []
        for n in range(GROUP):
            r = step * GROUP + n
            place = slot * GROUP + n
            scores = lax.dot_general(
                query[r], cache[place], (((1,), (1,)), ((), ())), preferred_element_type=F32
            )
            scores += jnp.dot(positional[r], keys[place], preferred_element_type=F32)
            scores = scores * (NOPE + ROPE) ** (-0.5)
            scores = jnp.where(moment < lengths_ref[r], scores, -1e30)
            exponent = jnp.exp(scores - jnp.max(scores, axis=-1, keepdims=True))
            weights.append((exponent / jnp.sum(exponent, axis=-1, keepdims=True)).astype(BF16))
        for n in range(GROUP):
            r = step * GROUP + n
            value = jnp.dot(weights[n], cache[slot * GROUP + n], preferred_element_type=F32)
            value = value.astype(BF16).astype(F32)
            rows = pl.ds(pl.multiple_of(r * heads_here, heads_here), heads_here)
            for t in range(context.shape[0]):
                context[t, rows, :] = value[:, t * LANES : (t + 1) * LANES]

        @pl.when(step < users_here // GROUP - 2)
        def _():
            for copy in user_loads(step + 2):
                copy.start()

        return carry

    lax.fori_loop(0, 1, attend, 0)
    pl.semaphore_wait(barrier, len(around))
    send(("wg",), gate_hbm, gate_far, partner)
    send(("wu",), up_hbm, up_far, partner)
    send(("wd",), down_hbm, down_far, partner)
    lax.fori_loop(1, users_here // GROUP, attend, 0)
    for copy in (loads[3], *up_loads[0], *loads[4:7]):
        copy.start()
    loads[2].wait()

    def head_value(h):
        tiles = [context[t, pl.ds(h, users_here, stride=heads_here), :] for t in range(context.shape[0])]
        rows = jnp.concatenate(tiles, axis=1).astype(BF16)
        value = jnp.dot(rows, value_up[h], preferred_element_type=F32)
        return value.astype(BF16)

    order = (("y", "z"), ("z", "y"))

    def head_block(p, k, **index):
        place = {"x": lax.rem(x_lo + k, 2), "y": me["y"], "z": me["z"]}
        place.update(index)
        return at(heads[p], **place)

    def head_slab(p, **index):
        return at(heads[p], **index)

    for p in range(2):
        for h in range(heads_here // 2):
            heads[p][x_lo, me["y"], me["z"], :, h * 128 : h * 128 + 128] = head_value(p * (heads_here // 2) + h)
        send(("hx", p), own_heads[p], own_heads[p], x_lo_partner)
        b, c = order[p]
        for by in (1, 3):
            send(("hb", p, 0, by), own_heads[p], own_heads[p], neighbour(b, by))

    wts = (wt0, wt1, wt2)
    gains = (gain0, gain1, gain2)

    def gate_task(slot, p):
        if p == 0:
            loads[7 if slot else 3].wait()

        def step(j, carry):
            block = weight_plane(weight_in, p, j).T.astype(F32) * gains[p][j]
            wts[p][j, slot, 0:256, :] = block.astype(BF16)
            return carry

        lax.fori_loop(0, wts[p].shape[0], step, 0)
        if slot == 0 and p == 2:
            recv(("wg",), gate_far)
            loads[7].start()

    def up_task(slot, p):
        if p == 0:
            for copy in up_loads[slot]:
                copy.wait()

        def step(j, carry):
            for q in range(2):
                if p == 0:
                    block = o0[2 * q : 2 * q + 2, :, j]
                elif p == 1:
                    block = o1[2 * q : 2 * q + 2, j]
                else:
                    block = o2[2 * q + j]
                block = block.reshape(-1, LANES).T.astype(F32) * gains[p][j]
                wts[p][j, slot, 256 + q * LANES : 256 + (q + 1) * LANES, :] = block.astype(BF16)
            return carry

        lax.fori_loop(0, wts[p].shape[0], step, 0)
        if slot == 1 and p == 0:
            recv(("wd",), down_far)
            loads[8].start()
        if slot == 0 and p == 2:
            recv(("wu",), up_far)
            for copy in up_loads[1]:
                copy.start()

    def down_task(slot, half_of):
        if half_of == 0:
            loads[8 if slot else 5].wait()

        def step(j, carry):
            block = down_in[:, pl.ds(pl.multiple_of(j * 896, 896), 896)].T
            downt[slot, j // 4, lax.rem(j, 4)] = block.reshape(4, FEATS, 256)
            return carry

        lax.fori_loop(4 * half_of, 4 * half_of + 4, step, 0)

    tasks = []
    for slot in range(2):
        tasks += [functools.partial(gate_task, slot, p) for p in range(3)]
        tasks += [functools.partial(up_task, slot, p) for p in range(3)]
        tasks += [functools.partial(down_task, slot, n) for n in range(2)]

    def work(count=1):
        for task in tasks[:count]:
            task()
        del tasks[:count]

    work(8)

    def slab_sends(p, m):
        b, c = order[p]
        slab = head_slab(p, **{b: shift(b, m), c: me[c]})
        for by in (1, 3):
            send(("hc", p, m, by), slab, slab, neighbour(c, by))

    for p in range(2):
        b, c = order[p]
        other = head_block(p, 1)
        recv(("hx", p), other)
        for by in (1, 3):
            send(("hb", p, 1, by), other, other, neighbour(b, by))
    for p in range(2):
        slab_sends(p, 0)
    work()
    for p in range(2):
        b, c = order[p]
        block = head_block(p, 0, **{b: shift(b, 3)})
        recv(("hb", p, 0, 1), block)
        send(("hf", p), block, block, neighbour(b, 1))
        recv(("hb", p, 0, 3), head_block(p, 0, **{b: shift(b, 1)}))
    for p in range(2):
        b, c = order[p]
        block = head_block(p, 1, **{b: shift(b, 1)})
        recv(("hb", p, 1, 3), block)
        send(("hf", p), block, block, neighbour(b, 3))
        slab_sends(p, 1)
        recv(("hb", p, 1, 1), head_block(p, 1, **{b: shift(b, 3)}))
        slab_sends(p, 3)
    work()
    for p in range(2):
        b, c = order[p]
        recv(("hf", p), head_slab(p, **{b: shift(b, 2), c: me[c]}))
        slab_sends(p, 2)
    work()

    def project(p, by, first=False):
        c = order[p][1]
        j = shift(c, by)
        rows = get(heads[p], **{c: j}).reshape(-1, half)
        product = lax.dot_general(
            rows, out_proj[:, p * half : (p + 1) * half], (((1,), (1,)), ((), ())), preferred_element_type=F32
        )
        product = product.reshape(2, 4, 16, FEATS)
        if c == "z":
            attn[:, :, j] = product
        else:
            attn[:, j] += product

    loads[4].wait()
    project(0, 0)
    for m in (0, 1, 3, 2):
        for p in range(2):
            b, c = order[p]
            for by in (1, 3):
                region = head_slab(p, **{b: shift(b, m), c: shift(c, -by)})
                recv(("hc", p, m, by), region)
                if (m in (0, 1)) == (by == 1):
                    send(("hd", p), region, region, neighbour(c, by))
        work()
    work(len(tasks))
    project(0, 1)
    project(0, 3)
    recv(("hd", 0), head_slab(0, **{order[0][1]: shift(order[0][1], 2)}))
    project(0, 2)
    for by in (0, 1, 3):
        project(1, by)
    recv(("hd", 1), head_slab(1, **{order[1][1]: shift(order[1][1], 2)}))
    project(1, 2)

    attn_mine = attn.at[:, pl.ds(core * 2, 2)]
    send(("pair",), attn.at[:, pl.ds((1 - core) * 2, 2)], pair_in, partner)
    recv(("pair",), pair_in)
    far_out[...] = (attn_mine[1 - x_hi] + pair_in[1 - x_hi]).astype(BF16)
    send(("far",), far_out, far_in, neighbour("x", 2))
    loads[6].wait()
    near = (attn_mine[x_hi] + pair_in[x_hi]).reshape(LANES, FEATS)
    recv(("far",), far_in)
    residual = near + far_in[...].reshape(LANES, FEATS).astype(F32)
    residual = jnp.concatenate([residual, jnp.zeros((LANES, 32), F32)], axis=1).T[:FEATS]
    residual = residual + hidden[...].astype(F32)
    kept[...] = residual
    routed = residual.astype(BF16)

    rts = (rt0, rt1, rt2)
    for p, (first, rows, _) in enumerate(PARTS):
        rts[p][me["x"], me["y"], me["z"]] = routed[first : first + rows]

    def spot(p, **index):
        place = dict(me)
        place.update(index)
        return at(rts[p], **place)

    axes = [tuple(o) for _, _, o in PARTS]
    drain()
    for p in range(3):
        a, b, c = axes[p]
        for by in (1, 3, 2):
            send(("ga", p, by), spot(p), spot(p), neighbour(a, by))
        for by in (1, 3):
            send(("gb", p, 0, by), spot(p), spot(p), neighbour(b, by))

    def plane_group(p, m):
        a, b, c = axes[p]
        slab = at(rts[p], **{b: shift(b, m), c: me[c]})
        for by in (1, 3):
            send(("gc", p, m, by), slab, slab, neighbour(c, by))

    for k in (1, 3, 2):
        for p in range(3):
            a, b, c = axes[p]
            block = spot(p, **{a: shift(a, k)})
            recv(("ga", p, 4 - k), block)
            for by in (1, 3):
                send(("gb", p, k, by), block, block, neighbour(b, by))
    for p in range(3):
        plane_group(p, 0)
    for k in (0, 1, 3, 2):
        for p in range(3):
            a, b, c = axes[p]
            for by in (1, 3):
                block = spot(p, **{a: shift(a, k), b: shift(b, -by)})
                recv(("gb", p, k, by), block)
                if (k in (0, 1)) == (by == 1):
                    send(("gf", p), block, block, neighbour(b, by))
    for p in range(3):
        plane_group(p, 3)
        plane_group(p, 1)
    def pass_on(m):
        for p in range(3):
            a, b, c = axes[p]
            for by in (1, 3):
                region = at(rts[p], **{b: shift(b, m), c: shift(c, -by)})
                recv(("gc", p, m, by), region)
                if (m in (0, 1)) == (by == 1):
                    send(("gd", p), region, region, neighbour(c, by))

    for p in range(3):
        a, b, c = axes[p]
        recv(("gf", p), spot(p, **{a: slice(None), b: shift(b, 2)}))
        plane_group(p, 2)
    pass_on(0)

    totals = {"square": jnp.zeros((1, 256), F32), "first": True}

    def users_of(p, by):
        if p == 0:
            block = rts[0][:, :, shift("z", by)]
            low, high = block[0:2], block[2:4]
        elif p == 1:
            block = rts[1][:, shift("y", by)]
            low, high = block[0:2], block[2:4]
        else:
            plane = lax.rem(x_lo + by, 2)
            low, high = rts[2][plane], rts[2][plane + 2]
        return jnp.concatenate([low.reshape(-1, LANES), high.reshape(-1, LANES)], axis=1)

    def plane_of(p, by):
        if p == 2:
            return lax.rem(x_lo + by, 2)
        return shift(axes[p][2], by)

    def multiply(p, by):
        rows = users_of(p, by)
        wide = rows.astype(F32)
        totals["square"] = totals["square"] + jnp.sum(wide * wide, axis=0, keepdims=True)
        weight = wts[p][plane_of(p, by)]
        product = jnp.dot(weight.reshape(1024, weight.shape[-1]), rows, preferred_element_type=F32)
        if totals["first"]:
            gate_up[...] = product
        else:
            gate_up[...] += product
        totals["first"] = False

    multiply(0, 0)
    multiply(1, 0)
    for m in (1, 3, 2):
        pass_on(m)
    for by in (1, 3):
        multiply(0, by)
        multiply(1, by)
    multiply(2, 1)
    for p in range(3):
        a, b, c = axes[p]
        recv(("gd", p), at(rts[p], **{c: shift(c, 2)}))
        multiply(p, 2 if p < 2 else 0)

    scale = lax.rsqrt(totals["square"] * (1.0 / (32 * FEATS)) + norm_eps)
    for slot in range(2):
        gate = gate_up[slot * 512 : slot * 512 + 256] * scale
        upward = gate_up[slot * 512 + 256 : slot * 512 + 512] * scale
        act[slot * 256 : slot * 256 + 256] = (gate / (1.0 + jnp.exp(-gate)) * upward).astype(BF16)

    drain()
    outs = (o0, o1, o2)
    r1, r2, r3, r4, r5 = (
        (r1_0, r1_1, r1_2), (r2_0, r2_1, r2_2), (r3_0, r3_1, r3_2), (r4_0, r4_1, r4_2), (r5_0, r5_1, r5_2)
    )
    share = jnp.sum(jnp.where(ids_ref[...] == dev, weights_ref[...], 0.0), axis=0, keepdims=True)
    share = jnp.where(
        core == 0,
        jnp.concatenate([share[:, 0:128], share[:, 256:384]], axis=1),
        jnp.concatenate([share[:, 128:256], share[:, 384:512]], axis=1),
    )

    def down(p, by):
        first, rows, _ = PARTS[p]
        j = plane_of(p, by)
        product = jnp.dot(weight_plane(downt.at[0], p, j), act[0:256], preferred_element_type=F32)
        product += jnp.dot(weight_plane(downt.at[1], p, j), act[256:512], preferred_element_type=F32)
        product = (product * share).astype(BF16)
        for h in range(2):
            lanes = product[:, h * LANES : (h + 1) * LANES]
            if p == 0:
                o0[2 * h : 2 * h + 2, :, j] = lanes.reshape(2, 4, rows, LANES)
            elif p == 1:
                o1[2 * h : 2 * h + 2, j] = lanes.reshape(2, 4, rows, LANES)
            else:
                o2[j + 2 * h] = lanes.reshape(4, 4, rows, LANES)

    def o_slab(p, by, m):
        a, b, c = axes[p]
        return at(outs[p], **{c: shift(c, by), b: shift(b, m)})

    for p in range(3):
        c = axes[p][2]
        down(p, 2 if p < 2 else 0)
        for m in (2, 0, 3, 1):
            by = 1 if m in (0, 1) else 3
            send(("s1", p, m), o_slab(p, 2, m), r1[p].at[m], neighbour(c, by))
    for p in range(3):
        c = axes[p][2]
        if p < 2:
            down(p, 1)
            down(p, 3)
        else:
            down(p, 1)
        for m in (2, 3):
            send(("s2", p, m), o_slab(p, 1, m), r2[p].at[m, 0], neighbour(c, 1))
        for m in (1, 0):
            send(("s2", p, m), o_slab(p, 3, m), r2[p].at[m, 1], neighbour(c, 3))
    for p in range(2):
        down(p, 0)

    def add_to(slab, other):
        slab[...] = (slab[...].astype(F32) + other[...].astype(F32)).astype(BF16)

    for m in (2, 1, 3, 0):
        for p in range(3):
            c = axes[p][2]
            recv(("s1", p, m), r1[p].at[m])
            by = 1 if m in (0, 1) else 3
            side = 0 if by == 1 else 1
            slab = o_slab(p, by, m)
            add_to(slab, r1[p].at[m])
            send(("s2", p, m), slab, r2[p].at[m, side], neighbour(c, by))

    for m in (2, 1, 3, 0):
        for p in range(3):
            a, b, c = axes[p]
            slab = o_slab(p, 0, m)
            recv(("s2", p, m), r2[p].at[m])
            slab[...] = (
                slab[...].astype(F32) + r2[p][m, 0].astype(F32) + r2[p][m, 1].astype(F32)
            ).astype(BF16)
            if m == 2:
                send(("s3", p, 0), slab.at[0:2], r3[p].at[0:2], neighbour(b, 1))
                send(("s3", p, 1), slab.at[2:4], r3[p].at[2:4], neighbour(b, 3))
            elif m == 1:
                send(("s4", p), slab.at[2:4], r4[p].at[0, 2:4], neighbour(b, 1))
            elif m == 3:
                send(("s4", p), slab.at[0:2], r4[p].at[1, 0:2], neighbour(b, 3))
    for p in range(3):
        a, b, c = axes[p]
        recv(("s3", p, 0), r3[p].at[0:2])
        slab = o_slab(p, 0, 1).at[0:2]
        add_to(slab, r3[p].at[0:2])
        send(("s4", p), slab, r4[p].at[0, 0:2], neighbour(b, 1))
        recv(("s3", p, 1), r3[p].at[2:4])
        slab = o_slab(p, 0, 3).at[2:4]
        add_to(slab, r3[p].at[2:4])
        send(("s4", p), slab, r4[p].at[1, 2:4], neighbour(b, 3))
    for p in range(3):
        a, b, c = axes[p]
        recv(("s4", p), r4[p])
        slab = o_slab(p, 0, 0)
        slab[...] = (
            slab[...].astype(F32) + r4[p][0].astype(F32) + r4[p][1].astype(F32)
        ).astype(BF16)
        for k in (2, 1, 3):
            send(("s5", p), slab.at[shift(a, k)], r5[p].at[k - 1], neighbour(a, k))
    for p, (first, rows, _) in enumerate(PARTS):
        a = axes[p][0]
        total = kept[first : first + rows, :] + outs[p][me["x"], me["y"], me["z"]].astype(F32)
        recv(("s5", p), r5[p])
        for k in (1, 3, 2):
            total = total + r5[p][k - 1].astype(F32)
        out_ref[first : first + rows, :] = total.astype(BF16)
    drain()


def body(
    query_latent, query_rope, cache_latent, cache_rope, lengths, value_up, output_proj, hidden,
    norm_gain, route_ids, route_weights, gate_proj, up_proj, down_proj,
):
    def bf(*shape):
        return pltpu.VMEM(shape, BF16)

    def f32(*shape):
        return pltpu.VMEM(shape, F32)

    users, heads, latent = query_latent.shape
    history = cache_latent.shape[1]
    half = heads * LANES // 2
    rows = [r for _, r, _ in PARTS]
    hbm = pl.BlockSpec(memory_space=pl.ANY)
    vmem = pl.BlockSpec(memory_space=pltpu.VMEM)
    scratch = [
        bf(users, heads, latent), bf(users, heads * ROPE), bf(users, heads, ROPE),
        bf(2 * GROUP, history, latent), bf(2 * GROUP, ROPE, history), f32(latent // LANES, users * heads, LANES),
        bf(*value_up.shape),
        bf(2, 4, 4, 16, half), bf(2, 4, 4, 16, half), bf(FEATS, 2 * half), f32(2, 4, 4, 16, FEATS),
        f32(2, 2, 4, 16, FEATS), bf(2, 4, 16, FEATS), bf(2, 4, 16, FEATS), bf(FEATS, LANES),
        bf(2, 4, 4, FEATS, 256), bf(256, 32 * FEATS),
        f32(4, 1, 640), f32(4, 1, 640), f32(2, 1, 1024),
        bf(4, 2, 512, 640), bf(4, 2, 512, 640), bf(2, 2, 512, 1024), bf(2, 2, 4, 4, FEATS, 256),
        *[bf(4, 4, 4, r, LANES) for r in rows],
        f32(1024, 256), bf(512, 256),
        *[bf(4, 4, 4, r, LANES) for r in rows],
        *[bf(4, 4, r, LANES) for r in rows],
        *[bf(4, 2, 4, r, LANES) for r in rows],
        *[bf(4, r, LANES) for r in rows],
        *[bf(2, 4, r, LANES) for r in rows],
        *[bf(3, r, LANES) for r in rows],
        f32(FEATS, LANES),
        pltpu.SemaphoreType.DMA((2, 2)),
        pltpu.SemaphoreType.DMA((9,)),
        pltpu.SemaphoreType.DMA((2, 6)),
        pltpu.SemaphoreType.DMA((81,)),
        pltpu.SemaphoreType.DMA((134,)),
    ]
    gate_proj = gate_proj.reshape(2, 4, 4, FEATS, 256)
    up_proj = up_proj.reshape(2, 4, 4, FEATS, 256)
    down_proj = down_proj[0]
    out, *_ = pl.pallas_call(
        layer_kernel,
        out_shape=(
            jax.ShapeDtypeStruct((FEATS, LANES), BF16),
            *[jax.ShapeDtypeStruct(a.shape, BF16) for a in (gate_proj, up_proj, down_proj)],
        ),
        in_specs=[
            hbm, hbm, hbm, hbm, pl.BlockSpec(memory_space=pltpu.SMEM), hbm,
            hbm, hbm, vmem, vmem, vmem, hbm, hbm, hbm,
        ],
        out_specs=(vmem, hbm, hbm, hbm),
        scratch_shapes=scratch,
        compiler_params=pltpu.CompilerParams(
            collective_id=0, has_side_effects=True, vmem_limit_bytes=63 * 1024 * 1024
        ),
        cost_estimate=pl.CostEstimate(flops=9 * 10**9, bytes_accessed=27 * 2**20, transcendentals=0),
    )(
        query_latent, query_rope, cache_latent, cache_rope, lengths, value_up,
        output_proj.T, hidden.T, norm_gain.reshape(56, LANES), route_ids.T, route_weights.T,
        gate_proj, up_proj, down_proj,
    )
    return out.T


def solution(mesh):
    return jax.shard_map(
        body,
        mesh=mesh,
        in_specs=(
            P("dev", "sec", None),
            P("dev", "sec"),
            P("dev", None, None),
            P("dev", None, None),
            P("dev"),
            P("sec", None, None),
            P("sec", "dev"),
            P(None, "dev"),
            P(),
            P(),
            P(),
            P("dev", None, "sec"),
            P("dev", None, "sec"),
            P("dev", "sec", None),
        ),
        out_specs=P("sec", "dev"),
        check_vma=False,
    )
```

```python
import functools

import jax
import jax.numpy as jnp
from jax import lax
from jax.experimental import pallas as pl
from jax.experimental.pallas import tpu as pltpu
from jax.sharding import PartitionSpec as P

ROPE = 64
NOPE = 128
norm_eps = 1e-06
MESH = pl.DeviceIdType.MESH
F32 = jnp.float32
BF16 = jnp.bfloat16

PARTS = ((0, 80, "xyz"), (80, 80, "zxy"), (160, 64, "yzx"))
FEATS = 224
LANES = 128
GROUP = 4


def weight_plane(ref, p, j):
    first, rows, _ = PARTS[p]
    if p == 0:
        block = ref[:, :, j, first : first + rows, :]
    elif p == 1:
        block = ref[:, j, :, first : first + rows, :]
    else:
        block = ref[j, :, :, first : first + rows, :]
    return block.reshape(-1, block.shape[-1])


def at(ref, **index):
    return ref.at[tuple(index.get(axis, slice(None)) for axis in "xyz")]


def get(ref, **index):
    return ref[tuple(index.get(axis, slice(None)) for axis in "xyz")]


def layer_kernel(
    query_hbm, rope_hbm, cache_hbm, keys_hbm, lengths_ref, value_up_hbm,
    out_proj_hbm, hidden_hbm, gain_ref, ids_ref, weights_ref, gate_hbm, up_hbm, down_hbm,
    out_ref, gate_far, up_far, down_far,
    query, rope, positional, cache, keys, context, value_up,
    heads0, heads1, out_proj, attn, pair_in, far_in, far_out, hidden,
    weight_in, down_in, gain0, gain1, gain2, wt0, wt1, wt2, downt,
    rt0, rt1, rt2, gate_up, act, o0, o1, o2,
    r1_0, r1_1, r1_2, r2_0, r2_1, r2_2, r3_0, r3_1, r3_2, r4_0, r4_1, r4_2, r5_0, r5_1, r5_2,
    kept, cache_sem, local_sem, stage_sem, send_sem, recv_sem,
):
    sec = lax.axis_index("sec")
    dev = lax.axis_index("dev")
    x_hi, core = sec // 2, lax.rem(sec, 2)
    x_lo = dev // 16
    me = {
        "x": x_hi * 2 + x_lo,
        "y": lax.rem(dev // 4, 4),
        "z": lax.rem(dev, 4),
    }

    def shift(axis, by):
        return lax.rem(me[axis] + (by % 4), 4)

    def device(x, y, z, c):
        return ((x // 2) * 2 + c, lax.rem(x, 2) * 16 + y * 4 + z)

    def neighbour(axis, by):
        place = dict(me)
        place[axis] = shift(axis, by)
        return device(place["x"], place["y"], place["z"], core)

    partner = device(me["x"], me["y"], me["z"], 1 - core)
    x_lo_partner = (sec, (1 - x_lo) * 16 + me["y"] * 4 + me["z"])

    tags = {}
    sent = []

    def number(tag):
        return tags.setdefault(tag, len(tags))

    def send(tag, src, dst, to):
        i = number(tag)
        copy = pltpu.make_async_remote_copy(
            src_ref=src, dst_ref=dst, send_sem=send_sem.at[len(sent)], recv_sem=recv_sem.at[i],
            device_id=to, device_id_type=MESH,
        )
        copy.start()
        sent.append(copy)

    def drain():
        while sent:
            sent.pop().wait_send()

    def recv(tag, region):
        i = number(tag)
        pltpu.make_async_remote_copy(
            src_ref=region, dst_ref=region, send_sem=send_sem.at[0], recv_sem=recv_sem.at[i],
            device_id=partner, device_id_type=MESH,
        ).wait_recv()


    around = [neighbour(axis, by) for axis in "xyz" for by in (1, 2, 3)] + [partner]
    barrier = pltpu.get_barrier_semaphore()
    for other in around:
        pl.semaphore_signal(barrier, inc=1, device_id=other, device_id_type=MESH)

    heads = (heads0, heads1)
    half = heads0.shape[-1]
    own_heads = [at(h, x=x_lo, y=me["y"], z=me["z"]) for h in heads]
    my_hidden = hidden_hbm.at[:, pl.ds(pl.multiple_of(sec * LANES, LANES), LANES)]

    def user_loads(step):
        slot = lax.rem(step, 2) if not isinstance(step, int) else step % 2
        users, place = pl.ds(step * GROUP, GROUP), pl.ds(slot * GROUP, GROUP)
        return (
            pltpu.make_async_copy(cache_hbm.at[users], cache.at[place], cache_sem.at[slot, 0]),
            pltpu.make_async_copy(keys_hbm.at[users], keys.at[place], cache_sem.at[slot, 1]),
        )

    def stage_up(source, n):
        copies = []
        for p, (first, rows, _) in enumerate(PARTS):
            for q in range(2):
                copies.append(
                    pltpu.make_async_copy(
                        source.at[:, :, :, pl.ds(first, rows), pl.ds(q * LANES, LANES)],
                        (o0, o1, o2)[p].at[pl.ds(2 * q, 2)],
                        stage_sem.at[n, 2 * p + q],
                    )
                )
        return copies

    loads = [
        pltpu.make_async_copy(rope_hbm, rope, local_sem.at[0]),
        pltpu.make_async_copy(query_hbm, query, local_sem.at[1]),
        pltpu.make_async_copy(value_up_hbm, value_up, local_sem.at[2]),
        pltpu.make_async_copy(gate_hbm, weight_in, local_sem.at[3]),
        pltpu.make_async_copy(out_proj_hbm, out_proj, local_sem.at[4]),
        pltpu.make_async_copy(down_hbm, down_in, local_sem.at[5]),
        pltpu.make_async_copy(my_hidden, hidden, local_sem.at[6]),
        pltpu.make_async_copy(gate_far, weight_in, local_sem.at[7]),
        pltpu.make_async_copy(down_far, down_in, local_sem.at[8]),
    ]
    up_loads = stage_up(up_hbm, 0), stage_up(up_far, 1)
    for copy in (loads[0], loads[1], *user_loads(0), *user_loads(1)):
        copy.start()
    loads[2].start()

    for p, gain in enumerate((gain0, gain1, gain2)):
        first, rows, _ = PARTS[p]
        width = gain.shape[-1]
        block = lax.broadcasted_iota(jnp.int32, (LANES, width), 1) // rows
        offset = lax.rem(lax.broadcasted_iota(jnp.int32, (LANES, width), 1), rows) + first
        lane = lax.broadcasted_iota(jnp.int32, (LANES, width), 0)
        for j in range(gain.shape[0]):
            if p == 0:
                owner = block * 4 + j
            elif p == 1:
                owner = (block // 4) * 16 + j * 4 + lax.rem(block, 4)
            else:
                owner = j * 16 + block
            place = owner * FEATS + offset
            spread = jnp.dot(
                gain_ref[...], (lax.rem(place, LANES) == lane).astype(F32),
                preferred_element_type=F32, precision=lax.Precision.HIGHEST,
            )
            held = (place // LANES)[:56] == lane[:56]
            gain[j] = jnp.sum(jnp.where(held, spread, 0.0), axis=0, keepdims=True)

    users_here, heads_here = query.shape[0], query.shape[1]
    loads[0].wait()
    wide = heads_here * ROPE
    owner = lax.broadcasted_iota(jnp.int32, (heads_here, wide), 1) // ROPE
    mask = owner == lax.broadcasted_iota(jnp.int32, (heads_here, wide), 0)
    fold = lax.rem(lax.broadcasted_iota(jnp.int32, (wide, ROPE), 0), ROPE)
    fold = (fold == lax.broadcasted_iota(jnp.int32, (wide, ROPE), 1)).astype(F32).astype(BF16)
    for r in range(users_here):
        row = jnp.broadcast_to(rope[r : r + 1, :].astype(F32), (heads_here, wide))
        row = jnp.where(mask, row, 0.0).astype(BF16)
        positional[r] = jnp.dot(row, fold, preferred_element_type=F32).astype(BF16)
    loads[1].wait()
    history = cache.shape[1]
    moment = lax.broadcasted_iota(jnp.int32, (heads_here, history), 1)

    def attend(step, carry):
        slot = lax.rem(step, 2)
        for copy in user_loads(step):
            copy.wait()
        weights = []
        for n in range(GROUP):
            r = step * GROUP + n
            place = slot * GROUP + n
            scores = lax.dot_general(
                query[r], cache[place], (((1,), (1,)), ((), ())), preferred_element_type=F32
            )
            scores += jnp.dot(positional[r], keys[place], preferred_element_type=F32)
            scores = scores * (NOPE + ROPE) ** (-0.5)
            scores = jnp.where(moment < lengths_ref[r], scores, -1e30)
            exponent = jnp.exp(scores - jnp.max(scores, axis=-1, keepdims=True))
            weights.append((exponent / jnp.sum(exponent, axis=-1, keepdims=True)).astype(BF16))
        for n in range(GROUP):
            r = step * GROUP + n
            value = jnp.dot(weights[n], cache[slot * GROUP + n], preferred_element_type=F32)
            value = value.astype(BF16).astype(F32)
            rows = pl.ds(pl.multiple_of(r * heads_here, heads_here), heads_here)
            for t in range(context.shape[0]):
                context[t, rows, :] = value[:, t * LANES : (t + 1) * LANES]

        @pl.when(step < users_here // GROUP - 2)
        def _():
            for copy in user_loads(step + 2):
                copy.start()

        return carry

    lax.fori_loop(0, 1, attend, 0)
    pl.semaphore_wait(barrier, len(around))
    send(("wg",), gate_hbm, gate_far, partner)
    send(("wu",), up_hbm, up_far, partner)
    send(("wd",), down_hbm, down_far, partner)
    lax.fori_loop(1, users_here // GROUP, attend, 0)
    for copy in (loads[3], *up_loads[0], *loads[4:7]):
        copy.start()
    loads[2].wait()

    def head_value(h):
        tiles = [context[t, pl.ds(h, users_here, stride=heads_here), :] for t in range(context.shape[0])]
        rows = jnp.concatenate(tiles, axis=1).astype(BF16)
        value = jnp.dot(rows, value_up[h], preferred_element_type=F32)
        return value.astype(BF16)

    order = (("y", "z"), ("z", "y"))

    def head_block(p, k, **index):
        place = {"x": lax.rem(x_lo + k, 2), "y": me["y"], "z": me["z"]}
        place.update(index)
        return at(heads[p], **place)

    def head_slab(p, **index):
        return at(heads[p], **index)

    for p in range(2):
        for h in range(heads_here // 2):
            heads[p][x_lo, me["y"], me["z"], :, h * 128 : h * 128 + 128] = head_value(p * (heads_here // 2) + h)
        send(("hx", p), own_heads[p], own_heads[p], x_lo_partner)
        b, c = order[p]
        for by in (1, 3):
            send(("hb", p, 0, by), own_heads[p], own_heads[p], neighbour(b, by))
        for by in (1, 3):
            send(("hc", p, 0, by), own_heads[p], own_heads[p], neighbour(c, by))

    wts = (wt0, wt1, wt2)
    gains = (gain0, gain1, gain2)

    def gate_task(slot, p):
        if p == 0:
            loads[7 if slot else 3].wait()

        def step(j, carry):
            block = weight_plane(weight_in, p, j).T.astype(F32) * gains[p][j]
            wts[p][j, slot, 0:256, :] = block.astype(BF16)
            return carry

        lax.fori_loop(0, wts[p].shape[0], step, 0)

    def up_task(slot, p):
        if p == 0:
            for copy in up_loads[slot]:
                copy.wait()

        def step(j, carry):
            for q in range(2):
                if p == 0:
                    block = o0[2 * q : 2 * q + 2, :, j]
                elif p == 1:
                    block = o1[2 * q : 2 * q + 2, j]
                else:
                    block = o2[2 * q + j]
                block = block.reshape(-1, LANES).T.astype(F32) * gains[p][j]
                wts[p][j, slot, 256 + q * LANES : 256 + (q + 1) * LANES, :] = block.astype(BF16)
            return carry

        lax.fori_loop(0, wts[p].shape[0], step, 0)

    def down_task(slot, half_of):
        if half_of == 0:
            loads[8 if slot else 5].wait()

        def step(j, carry):
            block = down_in[:, pl.ds(pl.multiple_of(j * 896, 896), 896)].T
            downt[slot, j // 4, lax.rem(j, 4)] = block.reshape(4, FEATS, 256)
            return carry

        lax.fori_loop(4 * half_of, 4 * half_of + 4, step, 0)

    tasks = []
    for slot in range(2):
        tasks += [functools.partial(gate_task, slot, p) for p in range(3)]
        tasks += [functools.partial(up_task, slot, p) for p in range(3)]
        tasks += [functools.partial(down_task, slot, n) for n in range(2)]

    def fetch_partner():
        recv(("wg",), gate_far)
        loads[7].start()
        recv(("wu",), up_far)
        for copy in up_loads[1]:
            copy.start()
        recv(("wd",), down_far)
        loads[8].start()

    def work(count=1):
        for task in tasks[:count]:
            task()
        del tasks[:count]

    work(8)

    def slab_sends(p, m):
        b, c = order[p]
        slab = head_slab(p, **{b: shift(b, m), c: me[c]})
        for by in (1, 3):
            send(("hc", p, m, by), slab, slab, neighbour(c, by))

    for p in range(2):
        b, c = order[p]
        other = head_block(p, 1)
        recv(("hx", p), other)
        for by in (1, 3):
            send(("hb", p, 1, by), other, other, neighbour(b, by))
    for p in range(2):
        other = head_block(p, 1)
        for by in (1, 3):
            send(("hc", p, 0, by), other, other, neighbour(order[p][1], by))
    for p in range(2):
        b, c = order[p]
        block = head_block(p, 0, **{b: shift(b, 3)})
        recv(("hb", p, 0, 1), block)
        send(("hf", p), block, block, neighbour(b, 1))
        recv(("hb", p, 0, 3), head_block(p, 0, **{b: shift(b, 1)}))
    for p in range(2):
        b, c = order[p]
        block = head_block(p, 1, **{b: shift(b, 1)})
        recv(("hb", p, 1, 3), block)
        send(("hf", p), block, block, neighbour(b, 3))
        slab_sends(p, 1)
        recv(("hb", p, 1, 1), head_block(p, 1, **{b: shift(b, 3)}))
        slab_sends(p, 3)
    for p in range(2):
        b, c = order[p]
        recv(("hf", p), head_slab(p, **{b: shift(b, 2), c: me[c]}))
        slab_sends(p, 2)
    fetch_partner()

    def project(p, by, first=False):
        c = order[p][1]
        j = shift(c, by)
        rows = get(heads[p], **{c: j}).reshape(-1, half)
        product = lax.dot_general(
            rows, out_proj[:, p * half : (p + 1) * half], (((1,), (1,)), ((), ())), preferred_element_type=F32
        )
        product = product.reshape(2, 4, 16, FEATS)
        if c == "z":
            attn[:, :, j] = product
        else:
            attn[:, j] += product

    loads[4].wait()
    project(0, 0)
    for m in (0, 1, 3, 2):
        for p in range(2):
            b, c = order[p]
            for by in (1, 3):
                region = head_slab(p, **{b: shift(b, m), c: shift(c, -by)})
                recv(("hc", p, m, by), region)
                if (m in (0, 1)) == (by == 1):
                    send(("hd", p), region, region, neighbour(c, by))
        work(2)
    work(len(tasks))
    project(0, 1)
    project(0, 3)
    recv(("hd", 0), head_slab(0, **{order[0][1]: shift(order[0][1], 2)}))
    project(0, 2)
    for by in (0, 1, 3):
        project(1, by)
    recv(("hd", 1), head_slab(1, **{order[1][1]: shift(order[1][1], 2)}))
    project(1, 2)

    attn_mine = attn.at[:, pl.ds(core * 2, 2)]
    send(("pair",), attn.at[:, pl.ds((1 - core) * 2, 2)], pair_in, partner)
    recv(("pair",), pair_in)
    far_out[...] = (attn_mine[1 - x_hi] + pair_in[1 - x_hi]).astype(BF16)
    send(("far",), far_out, far_in, neighbour("x", 2))
    loads[6].wait()
    near = (attn_mine[x_hi] + pair_in[x_hi]).reshape(LANES, FEATS)
    recv(("far",), far_in)
    residual = near + far_in[...].reshape(LANES, FEATS).astype(F32)
    residual = jnp.concatenate([residual, jnp.zeros((LANES, 32), F32)], axis=1).T[:FEATS]
    residual = residual + hidden[...].astype(F32)
    kept[...] = residual
    routed = residual.astype(BF16)

    rts = (rt0, rt1, rt2)
    for p, (first, rows, _) in enumerate(PARTS):
        rts[p][me["x"], me["y"], me["z"]] = routed[first : first + rows]

    def spot(p, **index):
        place = dict(me)
        place.update(index)
        return at(rts[p], **place)

    axes = [tuple(o) for _, _, o in PARTS]
    drain()
    for p in range(3):
        a, b, c = axes[p]
        for by in (1, 3, 2):
            send(("ga", p, by), spot(p), spot(p), neighbour(a, by))
        for by in (1, 3):
            send(("gb", p, 0, by), spot(p), spot(p), neighbour(b, by))
        for by in (1, 3):
            send(("gc", p, 0, by), spot(p), spot(p), neighbour(c, by))

    def plane_group(p, m):
        a, b, c = axes[p]
        slab = at(rts[p], **{b: shift(b, m), c: me[c]})
        for by in (1, 3):
            send(("gc", p, m, by), slab, slab, neighbour(c, by))

    for k in (1, 3, 2):
        for p in range(3):
            a, b, c = axes[p]
            block = spot(p, **{a: shift(a, k)})
            recv(("ga", p, 4 - k), block)
            for by in (1, 3):
                send(("gb", p, k, by), block, block, neighbour(b, by))
            for by in (1, 3):
                send(("gc", p, 0, by), block, block, neighbour(c, by))
    for k in (0, 1, 3, 2):
        for p in range(3):
            a, b, c = axes[p]
            for by in (1, 3):
                block = spot(p, **{a: shift(a, k), b: shift(b, -by)})
                recv(("gb", p, k, by), block)
                if (k in (0, 1)) == (by == 1):
                    send(("gf", p), block, block, neighbour(b, by))
    for p in range(3):
        plane_group(p, 3)
        plane_group(p, 1)
    def pass_on(m):
        for p in range(3):
            a, b, c = axes[p]
            for by in (1, 3):
                region = at(rts[p], **{b: shift(b, m), c: shift(c, -by)})
                recv(("gc", p, m, by), region)
                if (m in (0, 1)) == (by == 1):
                    send(("gd", p), region, region, neighbour(c, by))

    for p in range(3):
        a, b, c = axes[p]
        recv(("gf", p), spot(p, **{a: slice(None), b: shift(b, 2)}))
        plane_group(p, 2)
    pass_on(0)

    totals = {"square": jnp.zeros((1, 256), F32), "first": True}

    def users_of(p, by):
        if p == 0:
            block = rts[0][:, :, shift("z", by)]
            low, high = block[0:2], block[2:4]
        elif p == 1:
            block = rts[1][:, shift("y", by)]
            low, high = block[0:2], block[2:4]
        else:
            plane = lax.rem(x_lo + by, 2)
            low, high = rts[2][plane], rts[2][plane + 2]
        return jnp.concatenate([low.reshape(-1, LANES), high.reshape(-1, LANES)], axis=1)

    def plane_of(p, by):
        if p == 2:
            return lax.rem(x_lo + by, 2)
        return shift(axes[p][2], by)

    def multiply(*planes):
        weights, rows = [], []
        for p, by in planes:
            block = users_of(p, by)
            wide = block.astype(F32)
            totals["square"] = totals["square"] + jnp.sum(wide * wide, axis=0, keepdims=True)
            weight = wts[p][plane_of(p, by)]
            weights.append(weight.reshape(1024, weight.shape[-1]))
            rows.append(block)
        if len(planes) > 1:
            weights, rows = [jnp.concatenate(weights, axis=1)], [jnp.concatenate(rows, axis=0)]
        product = jnp.dot(weights[0], rows[0], preferred_element_type=F32)
        if totals["first"]:
            gate_up[...] = product
        else:
            gate_up[...] += product
        totals["first"] = False

    multiply((0, 0), (1, 0))
    for m in (1, 3, 2):
        pass_on(m)
    multiply((0, 1), (0, 3))
    multiply((1, 1), (1, 3))
    multiply((2, 1),)
    for p in range(2):
        c = axes[p][2]
        recv(("gd", p), at(rts[p], **{c: shift(c, 2)}))
    multiply((0, 2), (1, 2))
    recv(("gd", 2), at(rts[2], x=shift("x", 2)))
    multiply((2, 0),)

    scale = lax.rsqrt(totals["square"] * (1.0 / (32 * FEATS)) + norm_eps)
    for slot in range(2):
        gate = gate_up[slot * 512 : slot * 512 + 256] * scale
        upward = gate_up[slot * 512 + 256 : slot * 512 + 512] * scale
        act[slot * 256 : slot * 256 + 256] = (gate / (1.0 + jnp.exp(-gate)) * upward).astype(BF16)

    drain()
    outs = (o0, o1, o2)
    r1, r2, r3, r4, r5 = (
        (r1_0, r1_1, r1_2), (r2_0, r2_1, r2_2), (r3_0, r3_1, r3_2), (r4_0, r4_1, r4_2), (r5_0, r5_1, r5_2)
    )
    share = jnp.sum(jnp.where(ids_ref[...] == dev, weights_ref[...], 0.0), axis=0, keepdims=True)
    share = jnp.where(
        core == 0,
        jnp.concatenate([share[:, 0:128], share[:, 256:384]], axis=1),
        jnp.concatenate([share[:, 128:256], share[:, 384:512]], axis=1),
    )

    def down(p, by):
        first, rows, _ = PARTS[p]
        j = plane_of(p, by)
        weight = jnp.concatenate([weight_plane(downt.at[n], p, j) for n in range(2)], axis=1)
        product = jnp.dot(weight, act[...], preferred_element_type=F32)
        product = (product * share).astype(BF16)
        for h in range(2):
            lanes = product[:, h * LANES : (h + 1) * LANES]
            if p == 0:
                o0[2 * h : 2 * h + 2, :, j] = lanes.reshape(2, 4, rows, LANES)
            elif p == 1:
                o1[2 * h : 2 * h + 2, j] = lanes.reshape(2, 4, rows, LANES)
            else:
                o2[j + 2 * h] = lanes.reshape(4, 4, rows, LANES)

    def o_slab(p, by, m):
        a, b, c = axes[p]
        return at(outs[p], **{c: shift(c, by), b: shift(b, m)})

    for p in range(3):
        c = axes[p][2]
        down(p, 2 if p < 2 else 0)
        for m in (2, 0, 3, 1):
            by = 1 if m in (0, 1) else 3
            send(("s1", p, m), o_slab(p, 2, m), r1[p].at[m], neighbour(c, by))
    for p in range(3):
        c = axes[p][2]
        if p < 2:
            down(p, 1)
            down(p, 3)
        else:
            down(p, 1)
        for m in (2, 3):
            send(("s2", p, m), o_slab(p, 1, m), r2[p].at[m, 0], neighbour(c, 1))
        for m in (1, 0):
            send(("s2", p, m), o_slab(p, 3, m), r2[p].at[m, 1], neighbour(c, 3))
    for p in range(2):
        down(p, 0)

    def add_to(slab, other):
        slab[...] = (slab[...].astype(F32) + other[...].astype(F32)).astype(BF16)

    for m in (2, 1, 3, 0):
        for p in range(3):
            c = axes[p][2]
            recv(("s1", p, m), r1[p].at[m])
            by = 1 if m in (0, 1) else 3
            side = 0 if by == 1 else 1
            slab = o_slab(p, by, m)
            add_to(slab, r1[p].at[m])
            send(("s2", p, m), slab, r2[p].at[m, side], neighbour(c, by))

    for m in (2, 1, 3, 0):
        for p in range(3):
            a, b, c = axes[p]
            slab = o_slab(p, 0, m)
            recv(("s2", p, m), r2[p].at[m])
            slab[...] = (
                slab[...].astype(F32) + r2[p][m, 0].astype(F32) + r2[p][m, 1].astype(F32)
            ).astype(BF16)
            if m == 2:
                send(("s3", p, 0), slab.at[0:2], r3[p].at[0:2], neighbour(b, 1))
                send(("s3", p, 1), slab.at[2:4], r3[p].at[2:4], neighbour(b, 3))
            elif m == 1:
                send(("s4", p), slab.at[2:4], r4[p].at[0, 2:4], neighbour(b, 1))
            elif m == 3:
                send(("s4", p), slab.at[0:2], r4[p].at[1, 0:2], neighbour(b, 3))
    for p in range(3):
        a, b, c = axes[p]
        recv(("s3", p, 0), r3[p].at[0:2])
        slab = o_slab(p, 0, 1).at[0:2]
        add_to(slab, r3[p].at[0:2])
        send(("s4", p), slab, r4[p].at[0, 0:2], neighbour(b, 1))
        recv(("s3", p, 1), r3[p].at[2:4])
        slab = o_slab(p, 0, 3).at[2:4]
        add_to(slab, r3[p].at[2:4])
        send(("s4", p), slab, r4[p].at[1, 2:4], neighbour(b, 3))
    for p in range(3):
        a, b, c = axes[p]
        recv(("s4", p), r4[p])
        slab = o_slab(p, 0, 0)
        slab[...] = (
            slab[...].astype(F32) + r4[p][0].astype(F32) + r4[p][1].astype(F32)
        ).astype(BF16)
        for k in (2, 1, 3):
            send(("s5", p), slab.at[shift(a, k)], r5[p].at[k - 1], neighbour(a, k))
    for p, (first, rows, _) in enumerate(PARTS):
        a = axes[p][0]
        total = kept[first : first + rows, :] + outs[p][me["x"], me["y"], me["z"]].astype(F32)
        recv(("s5", p), r5[p])
        for k in (1, 3, 2):
            total = total + r5[p][k - 1].astype(F32)
        out_ref[first : first + rows, :] = total.astype(BF16)
    drain()


def body(
    query_latent, query_rope, cache_latent, cache_rope, lengths, value_up, output_proj, hidden,
    norm_gain, route_ids, route_weights, gate_proj, up_proj, down_proj,
):
    def bf(*shape):
        return pltpu.VMEM(shape, BF16)

    def f32(*shape):
        return pltpu.VMEM(shape, F32)

    users, heads, latent = query_latent.shape
    history = cache_latent.shape[1]
    half = heads * LANES // 2
    rows = [r for _, r, _ in PARTS]
    hbm = pl.BlockSpec(memory_space=pl.ANY)
    vmem = pl.BlockSpec(memory_space=pltpu.VMEM)
    scratch = [
        bf(users, heads, latent), bf(users, heads * ROPE), bf(users, heads, ROPE),
        bf(2 * GROUP, history, latent), bf(2 * GROUP, ROPE, history), f32(latent // LANES, users * heads, LANES),
        bf(*value_up.shape),
        bf(2, 4, 4, 16, half), bf(2, 4, 4, 16, half), bf(FEATS, 2 * half), f32(2, 4, 4, 16, FEATS),
        f32(2, 2, 4, 16, FEATS), bf(2, 4, 16, FEATS), bf(2, 4, 16, FEATS), bf(FEATS, LANES),
        bf(2, 4, 4, FEATS, 256), bf(256, 32 * FEATS),
        f32(4, 1, 640), f32(4, 1, 640), f32(2, 1, 1024),
        bf(4, 2, 512, 640), bf(4, 2, 512, 640), bf(2, 2, 512, 1024), bf(2, 2, 4, 4, FEATS, 256),
        *[bf(4, 4, 4, r, LANES) for r in rows],
        f32(1024, 256), bf(512, 256),
        *[bf(4, 4, 4, r, LANES) for r in rows],
        *[bf(4, 4, r, LANES) for r in rows],
        *[bf(4, 2, 4, r, LANES) for r in rows],
        *[bf(4, r, LANES) for r in rows],
        *[bf(2, 4, r, LANES) for r in rows],
        *[bf(3, r, LANES) for r in rows],
        f32(FEATS, LANES),
        pltpu.SemaphoreType.DMA((2, 2)),
        pltpu.SemaphoreType.DMA((9,)),
        pltpu.SemaphoreType.DMA((2, 6)),
        pltpu.SemaphoreType.DMA((99,)),
        pltpu.SemaphoreType.DMA((134,)),
    ]
    gate_proj = gate_proj.reshape(2, 4, 4, FEATS, 256)
    up_proj = up_proj.reshape(2, 4, 4, FEATS, 256)
    down_proj = down_proj[0]
    out, *_ = pl.pallas_call(
        layer_kernel,
        out_shape=(
            jax.ShapeDtypeStruct((FEATS, LANES), BF16),
            *[jax.ShapeDtypeStruct(a.shape, BF16) for a in (gate_proj, up_proj, down_proj)],
        ),
        in_specs=[
            hbm, hbm, hbm, hbm, pl.BlockSpec(memory_space=pltpu.SMEM), hbm,
            hbm, hbm, vmem, vmem, vmem, hbm, hbm, hbm,
        ],
        out_specs=(vmem, hbm, hbm, hbm),
        scratch_shapes=scratch,
        compiler_params=pltpu.CompilerParams(
            collective_id=0, has_side_effects=True, vmem_limit_bytes=63 * 1024 * 1024
        ),
        cost_estimate=pl.CostEstimate(flops=9 * 10**9, bytes_accessed=27 * 2**20, transcendentals=0),
    )(
        query_latent, query_rope, cache_latent, cache_rope, lengths, value_up,
        output_proj.T, hidden.T, norm_gain.reshape(56, LANES), route_ids.T, route_weights.T,
        gate_proj, up_proj, down_proj,
    )
    return out.T


def solution(mesh):
    return jax.shard_map(
        body,
        mesh=mesh,
        in_specs=(
            P("dev", "sec", None),
            P("dev", "sec"),
            P("dev", None, None),
            P("dev", None, None),
            P("dev"),
            P("sec", None, None),
            P("sec", "dev"),
            P(None, "dev"),
            P(),
            P(),
            P(),
            P("dev", None, "sec"),
            P("dev", None, "sec"),
            P("dev", "sec", None),
        ),
        out_specs=P("sec", "dev"),
        check_vma=False,
    )
```

```python
import functools

import jax
import jax.numpy as jnp
from jax import lax
from jax.experimental import pallas as pl
from jax.experimental.pallas import tpu as pltpu
from jax.sharding import PartitionSpec as P

ROPE = 64
NOPE = 128
norm_eps = 1e-06
MESH = pl.DeviceIdType.MESH
F32 = jnp.float32
BF16 = jnp.bfloat16

PARTS = ((0, 80, "xyz"), (80, 80, "zxy"), (160, 64, "yzx"))
FEATS = 224
LANES = 128
GROUP = 4


def weight_plane(ref, p, j):
    first, rows, _ = PARTS[p]
    if p == 0:
        block = ref[:, :, j, first : first + rows, :]
    elif p == 1:
        block = ref[:, j, :, first : first + rows, :]
    else:
        block = ref[j, :, :, first : first + rows, :]
    return block.reshape(-1, block.shape[-1])


def at(ref, **index):
    return ref.at[tuple(index.get(axis, slice(None)) for axis in "xyz")]


def get(ref, **index):
    return ref[tuple(index.get(axis, slice(None)) for axis in "xyz")]


def layer_kernel(
    query_hbm, rope_hbm, cache_hbm, keys_hbm, lengths_ref, value_up_hbm,
    out_proj_hbm, hidden_hbm, gain_ref, ids_ref, weights_ref, gate_hbm, up_hbm, down_hbm,
    out_ref, gate_far, up_far, down_far,
    query, rope, positional, cache, keys, context, value_up,
    heads0, heads1, out_proj, attn, pair_in, far_in, far_out, hidden,
    weight_in, down_in, gain0, gain1, gain2, wt0, wt1, wt2, downt,
    rt0, rt1, rt2, gate_up, act, o0, o1, o2,
    r1_0, r1_1, r1_2, r2_0, r2_1, r2_2, r5_0, r5_1, r5_2,
    kept, cache_sem, local_sem, stage_sem, send_sem, recv_sem,
):
    sec = lax.axis_index("sec")
    dev = lax.axis_index("dev")
    x_hi, core = sec // 2, lax.rem(sec, 2)
    x_lo = dev // 16
    me = {
        "x": x_hi * 2 + x_lo,
        "y": lax.rem(dev // 4, 4),
        "z": lax.rem(dev, 4),
    }

    def device(x, y, z, c):
        return ((x // 2) * 2 + c, lax.rem(x, 2) * 16 + y * 4 + z)

    shifted = {(axis, by): lax.rem(me[axis] + by, 4) for axis in "xyz" for by in (1, 2, 3)}

    def shift(axis, by):
        return me[axis] if by % 4 == 0 else shifted[axis, by % 4]

    def away(**by):
        place = [shift(axis, by.get(axis, 0)) for axis in "xyz"]
        return device(*place, core)

    def neighbour(axis, by):
        return away(**{axis: by})

    partner = device(me["x"], me["y"], me["z"], 1 - core)
    x_lo_partner = (sec, (1 - x_lo) * 16 + me["y"] * 4 + me["z"])

    tags = {}
    sent = []

    def number(tag):
        return tags.setdefault(tag, len(tags))

    def send(tag, src, dst, to):
        i = number(tag)
        copy = pltpu.make_async_remote_copy(
            src_ref=src, dst_ref=dst, send_sem=send_sem.at[len(sent)], recv_sem=recv_sem.at[i],
            device_id=to, device_id_type=MESH,
        )
        copy.start()
        sent.append(copy)

    def drain():
        while sent:
            sent.pop().wait_send()

    def recv(tag, region):
        i = number(tag)
        pltpu.make_async_remote_copy(
            src_ref=region, dst_ref=region, send_sem=send_sem.at[0], recv_sem=recv_sem.at[i],
            device_id=partner, device_id_type=MESH,
        ).wait_recv()


    offsets = {}
    for first, second in ("xy", "zx", "yz"):
        for m in range(4):
            for k in range(4):
                offset = {"x": 0, "y": 0, "z": 0, first: k, second: m}
                if k or m:
                    offsets[tuple(offset.values())] = offset
    around = [away(**offset) for offset in offsets.values()] + [partner]
    barrier = pltpu.get_barrier_semaphore()
    for other in around:
        pl.semaphore_signal(barrier, inc=1, device_id=other, device_id_type=MESH)

    heads = (heads0, heads1)
    half = heads0.shape[-1]
    own_heads = [at(h, x=x_lo, y=me["y"], z=me["z"]) for h in heads]
    my_hidden = hidden_hbm.at[:, pl.ds(pl.multiple_of(sec * LANES, LANES), LANES)]

    def user_loads(step):
        slot = lax.rem(step, 2) if not isinstance(step, int) else step % 2
        users, place = pl.ds(step * GROUP, GROUP), pl.ds(slot * GROUP, GROUP)
        return (
            pltpu.make_async_copy(cache_hbm.at[users], cache.at[place], cache_sem.at[slot, 0]),
            pltpu.make_async_copy(keys_hbm.at[users], keys.at[place], cache_sem.at[slot, 1]),
        )

    def stage_up(source, n):
        copies = []
        for p, (first, rows, _) in enumerate(PARTS):
            for q in range(2):
                copies.append(
                    pltpu.make_async_copy(
                        source.at[:, :, :, pl.ds(first, rows), pl.ds(q * LANES, LANES)],
                        (o0, o1, o2)[p].at[pl.ds(2 * q, 2)],
                        stage_sem.at[n, 2 * p + q],
                    )
                )
        return copies

    loads = [
        pltpu.make_async_copy(rope_hbm, rope, local_sem.at[0]),
        pltpu.make_async_copy(query_hbm, query, local_sem.at[1]),
        pltpu.make_async_copy(value_up_hbm, value_up, local_sem.at[2]),
        pltpu.make_async_copy(gate_hbm, weight_in, local_sem.at[3]),
        pltpu.make_async_copy(out_proj_hbm, out_proj, local_sem.at[4]),
        pltpu.make_async_copy(down_hbm, down_in, local_sem.at[5]),
        pltpu.make_async_copy(my_hidden, hidden, local_sem.at[6]),
        pltpu.make_async_copy(gate_far, weight_in, local_sem.at[7]),
        pltpu.make_async_copy(down_far, down_in, local_sem.at[8]),
    ]
    up_loads = stage_up(up_hbm, 0), stage_up(up_far, 1)
    for copy in (loads[0], loads[1], *user_loads(0), *user_loads(1)):
        copy.start()
    loads[2].start()

    for p, gain in enumerate((gain0, gain1, gain2)):
        first, rows, _ = PARTS[p]
        width = gain.shape[-1]
        block = lax.broadcasted_iota(jnp.int32, (LANES, width), 1) // rows
        offset = lax.rem(lax.broadcasted_iota(jnp.int32, (LANES, width), 1), rows) + first
        lane = lax.broadcasted_iota(jnp.int32, (LANES, width), 0)
        for j in range(gain.shape[0]):
            if p == 0:
                owner = block * 4 + j
            elif p == 1:
                owner = (block // 4) * 16 + j * 4 + lax.rem(block, 4)
            else:
                owner = j * 16 + block
            place = owner * FEATS + offset
            spread = jnp.dot(
                gain_ref[...], (lax.rem(place, LANES) == lane).astype(F32),
                preferred_element_type=F32, precision=lax.Precision.HIGHEST,
            )
            held = (place // LANES)[:56] == lane[:56]
            gain[j] = jnp.sum(jnp.where(held, spread, 0.0), axis=0, keepdims=True)

    users_here, heads_here = query.shape[0], query.shape[1]
    loads[0].wait()
    wide = heads_here * ROPE
    owner = lax.broadcasted_iota(jnp.int32, (heads_here, wide), 1) // ROPE
    mask = owner == lax.broadcasted_iota(jnp.int32, (heads_here, wide), 0)
    fold = lax.rem(lax.broadcasted_iota(jnp.int32, (wide, ROPE), 0), ROPE)
    fold = (fold == lax.broadcasted_iota(jnp.int32, (wide, ROPE), 1)).astype(F32).astype(BF16)
    for r in range(users_here):
        row = jnp.broadcast_to(rope[r : r + 1, :].astype(F32), (heads_here, wide))
        row = jnp.where(mask, row, 0.0).astype(BF16)
        positional[r] = jnp.dot(row, fold, preferred_element_type=F32).astype(BF16)
    loads[1].wait()
    history = cache.shape[1]
    moment = lax.broadcasted_iota(jnp.int32, (heads_here, history), 1)

    def attend(step, carry):
        slot = lax.rem(step, 2)
        for copy in user_loads(step):
            copy.wait()
        weights = []
        for n in range(GROUP):
            r = step * GROUP + n
            place = slot * GROUP + n
            scores = lax.dot_general(
                query[r], cache[place], (((1,), (1,)), ((), ())), preferred_element_type=F32
            )
            scores += jnp.dot(positional[r], keys[place], preferred_element_type=F32)
            scores = scores * (NOPE + ROPE) ** (-0.5)
            scores = jnp.where(moment < lengths_ref[r], scores, -1e30)
            exponent = jnp.exp(scores - jnp.max(scores, axis=-1, keepdims=True))
            weights.append((exponent / jnp.sum(exponent, axis=-1, keepdims=True)).astype(BF16))
        for n in range(GROUP):
            r = step * GROUP + n
            value = jnp.dot(weights[n], cache[slot * GROUP + n], preferred_element_type=F32)
            value = value.astype(BF16).astype(F32)
            rows = pl.ds(pl.multiple_of(r * heads_here, heads_here), heads_here)
            for t in range(context.shape[0]):
                context[t, rows, :] = value[:, t * LANES : (t + 1) * LANES]

        @pl.when(step < users_here // GROUP - 2)
        def _():
            for copy in user_loads(step + 2):
                copy.start()

        return carry

    lax.fori_loop(0, 1, attend, 0)
    pl.semaphore_wait(barrier, len(around))
    send(("wg",), gate_hbm, gate_far, partner)
    send(("wu",), up_hbm, up_far, partner)
    send(("wd",), down_hbm, down_far, partner)
    lax.fori_loop(1, users_here // GROUP, attend, 0)
    for copy in (loads[3], *up_loads[0], *loads[4:7]):
        copy.start()
    loads[2].wait()

    def head_value(h):
        tiles = [context[t, pl.ds(h, users_here, stride=heads_here), :] for t in range(context.shape[0])]
        rows = jnp.concatenate(tiles, axis=1).astype(BF16)
        value = jnp.dot(rows, value_up[h], preferred_element_type=F32)
        return value.astype(BF16)

    order = (("y", "z"), ("z", "y"))

    def head_block(p, k, **index):
        place = {"x": lax.rem(x_lo + k, 2), "y": me["y"], "z": me["z"]}
        place.update(index)
        return at(heads[p], **place)

    def head_slab(p, **index):
        return at(heads[p], **index)

    for p in range(2):
        for h in range(heads_here // 2):
            heads[p][x_lo, me["y"], me["z"], :, h * 128 : h * 128 + 128] = head_value(p * (heads_here // 2) + h)
        send(("hx", p), own_heads[p], own_heads[p], x_lo_partner)
        b, c = order[p]
        for by in (1, 3):
            send(("hb", p, 0, by), own_heads[p], own_heads[p], neighbour(b, by))
        for by in (1, 3):
            send(("hc", p, 0, by), own_heads[p], own_heads[p], neighbour(c, by))

    wts = (wt0, wt1, wt2)
    gains = (gain0, gain1, gain2)

    def gate_task(slot, p):
        if p == 0:
            loads[7 if slot else 3].wait()

        def step(j, carry):
            block = weight_plane(weight_in, p, j).T.astype(F32) * gains[p][j]
            wts[p][j, slot, 0:256, :] = block.astype(BF16)
            return carry

        lax.fori_loop(0, wts[p].shape[0], step, 0)

    def up_task(slot, p):
        if p == 0:
            for copy in up_loads[slot]:
                copy.wait()

        def step(j, carry):
            for q in range(2):
                if p == 0:
                    block = o0[2 * q : 2 * q + 2, :, j]
                elif p == 1:
                    block = o1[2 * q : 2 * q + 2, j]
                else:
                    block = o2[2 * q + j]
                block = block.reshape(-1, LANES).T.astype(F32) * gains[p][j]
                wts[p][j, slot, 256 + q * LANES : 256 + (q + 1) * LANES, :] = block.astype(BF16)
            return carry

        lax.fori_loop(0, wts[p].shape[0], step, 0)

    def down_task(slot, half_of):
        if half_of == 0:
            loads[8 if slot else 5].wait()

        def step(j, carry):
            block = down_in[:, pl.ds(pl.multiple_of(j * 896, 896), 896)].T
            downt[slot, j // 4, lax.rem(j, 4)] = block.reshape(4, FEATS, 256)
            return carry

        lax.fori_loop(4 * half_of, 4 * half_of + 4, step, 0)

    tasks = []
    for slot in range(2):
        tasks += [functools.partial(gate_task, slot, p) for p in range(3)]
        tasks += [functools.partial(up_task, slot, p) for p in range(3)]
        tasks += [functools.partial(down_task, slot, n) for n in range(2)]

    def fetch_partner():
        recv(("wg",), gate_far)
        loads[7].start()
        recv(("wu",), up_far)
        for copy in up_loads[1]:
            copy.start()
        recv(("wd",), down_far)
        loads[8].start()

    def work(count=1):
        for task in tasks[:count]:
            task()
        del tasks[:count]

    work(8)

    def slab_sends(p, m):
        b, c = order[p]
        slab = head_slab(p, **{b: shift(b, m), c: me[c]})
        for by in (1, 3):
            send(("hc", p, m, by), slab, slab, neighbour(c, by))

    for p in range(2):
        b, c = order[p]
        other = head_block(p, 1)
        recv(("hx", p), other)
        for by in (1, 3):
            send(("hb", p, 1, by), other, other, neighbour(b, by))
    for p in range(2):
        other = head_block(p, 1)
        for by in (1, 3):
            send(("hc", p, 0, by), other, other, neighbour(order[p][1], by))
    for p in range(2):
        b, c = order[p]
        block = head_block(p, 0, **{b: shift(b, 3)})
        recv(("hb", p, 0, 1), block)
        send(("hf", p), block, block, neighbour(b, 1))
        recv(("hb", p, 0, 3), head_block(p, 0, **{b: shift(b, 1)}))
    for p in range(2):
        b, c = order[p]
        block = head_block(p, 1, **{b: shift(b, 1)})
        recv(("hb", p, 1, 3), block)
        send(("hf", p), block, block, neighbour(b, 3))
        slab_sends(p, 1)
        recv(("hb", p, 1, 1), head_block(p, 1, **{b: shift(b, 3)}))
        slab_sends(p, 3)
    for p in range(2):
        b, c = order[p]
        recv(("hf", p), head_slab(p, **{b: shift(b, 2), c: me[c]}))
        slab_sends(p, 2)
    fetch_partner()

    def project(p, by, first=False):
        c = order[p][1]
        j = shift(c, by)
        rows = get(heads[p], **{c: j}).reshape(-1, half)
        product = lax.dot_general(
            rows, out_proj[:, p * half : (p + 1) * half], (((1,), (1,)), ((), ())), preferred_element_type=F32
        )
        product = product.reshape(2, 4, 16, FEATS)
        if c == "z":
            attn[:, :, j] = product
        else:
            attn[:, j] += product

    loads[4].wait()
    project(0, 0)
    for m in (0, 1, 3, 2):
        for p in range(2):
            b, c = order[p]
            for by in (1, 3):
                region = head_slab(p, **{b: shift(b, m), c: shift(c, -by)})
                recv(("hc", p, m, by), region)
                passed = head_slab(p, **{"x": by // 2, b: shift(b, m), c: shift(c, -by)})
                send(("hd", p), passed, passed, neighbour(c, by))
        work(2)
    work(len(tasks))
    project(0, 1)
    project(0, 3)
    recv(("hd", 0), head_slab(0, **{order[0][1]: shift(order[0][1], 2)}))
    project(0, 2)
    for by in (0, 1, 3):
        project(1, by)
    recv(("hd", 1), head_slab(1, **{order[1][1]: shift(order[1][1], 2)}))
    project(1, 2)

    attn_mine = attn.at[:, pl.ds(core * 2, 2)]
    send(("pair",), attn.at[:, pl.ds((1 - core) * 2, 2)], pair_in, partner)
    recv(("pair",), pair_in)
    far_out[...] = (attn_mine[1 - x_hi] + pair_in[1 - x_hi]).astype(BF16)
    send(("far",), far_out, far_in, neighbour("x", 2))
    loads[6].wait()
    near = (attn_mine[x_hi] + pair_in[x_hi]).reshape(LANES, FEATS)
    recv(("far",), far_in)
    residual = near + far_in[...].reshape(LANES, FEATS).astype(F32)
    residual = jnp.concatenate([residual, jnp.zeros((LANES, 32), F32)], axis=1).T[:FEATS]
    residual = residual + hidden[...].astype(F32)
    kept[...] = residual
    routed = residual.astype(BF16)

    rts = (rt0, rt1, rt2)
    for p, (first, rows, _) in enumerate(PARTS):
        rts[p][me["x"], me["y"], me["z"]] = routed[first : first + rows]

    def spot(p, **index):
        place = dict(me)
        place.update(index)
        return at(rts[p], **place)

    axes = [tuple(o) for _, _, o in PARTS]
    drain()
    for p in range(3):
        a, b, c = axes[p]
        for k in (1, 3, 2):
            send(("ga", p, k), spot(p), spot(p), away(**{a: k}))
        for by in (1, 3):
            send(("gc", p, 0, by), spot(p), spot(p), neighbour(c, by))
    for m in (1, 3, 2):
        for p in range(3):
            a, b, c = axes[p]
            for k in (0, 1, 3, 2):
                send(("gb", p, m), spot(p), spot(p), away(**{a: k, b: m}))

    for k in (1, 3, 2):
        for p in range(3):
            a, b, c = axes[p]
            block = spot(p, **{a: shift(a, k)})
            recv(("ga", p, 4 - k), block)
            for by in (1, 3):
                send(("gc", p, 0, by), block, block, neighbour(c, by))
    for m in (1, 3, 2):
        for p in range(3):
            a, b, c = axes[p]
            slab = at(rts[p], **{b: shift(b, m), c: me[c]})
            recv(("gb", p, 4 - m), slab)
            for by in (1, 3):
                send(("gc", p, m, by), slab, slab, neighbour(c, by))

    def pass_on(m):
        for p in range(3):
            a, b, c = axes[p]
            for by in (1, 3):
                region = at(rts[p], **{b: shift(b, m), c: shift(c, -by)})
                recv(("gc", p, m, by), region)
                half_of = pl.ds(0, 2) if by == 1 else pl.ds(2, 2)
                passed = at(rts[p], **{a: half_of, b: shift(b, m), c: shift(c, -by)})
                send(("gd", p), passed, passed, neighbour(c, by))

    pass_on(0)

    totals = {"square": jnp.zeros((1, 256), F32), "first": True}

    def users_of(p, by):
        if p == 0:
            block = rts[0][:, :, shift("z", by)]
            low, high = block[0:2], block[2:4]
        elif p == 1:
            block = rts[1][:, shift("y", by)]
            low, high = block[0:2], block[2:4]
        else:
            plane = lax.rem(x_lo + by, 2)
            low, high = rts[2][plane], rts[2][plane + 2]
        return jnp.concatenate([low.reshape(-1, LANES), high.reshape(-1, LANES)], axis=1)

    def plane_of(p, by):
        if p == 2:
            return lax.rem(x_lo + by, 2)
        return shift(axes[p][2], by)

    def multiply(*planes):
        weights, rows = [], []
        for p, by in planes:
            block = users_of(p, by)
            wide = block.astype(F32)
            totals["square"] = totals["square"] + jnp.sum(wide * wide, axis=0, keepdims=True)
            weight = wts[p][plane_of(p, by)]
            weights.append(weight.reshape(1024, weight.shape[-1]))
            rows.append(block)
        if len(planes) > 1:
            weights, rows = [jnp.concatenate(weights, axis=1)], [jnp.concatenate(rows, axis=0)]
        product = jnp.dot(weights[0], rows[0], preferred_element_type=F32)
        if totals["first"]:
            gate_up[...] = product
        else:
            gate_up[...] += product
        totals["first"] = False

    multiply((0, 0), (1, 0))
    for m in (1, 3, 2):
        pass_on(m)
    multiply((0, 1), (0, 3))
    multiply((1, 1), (1, 3))
    multiply((2, 1),)
    for p in range(2):
        c = axes[p][2]
        recv(("gd", p), at(rts[p], **{c: shift(c, 2)}))
    multiply((0, 2), (1, 2))
    recv(("gd", 2), at(rts[2], x=shift("x", 2)))
    multiply((2, 0),)

    scale = lax.rsqrt(totals["square"] * (1.0 / (32 * FEATS)) + norm_eps)
    for slot in range(2):
        gate = gate_up[slot * 512 : slot * 512 + 256] * scale
        upward = gate_up[slot * 512 + 256 : slot * 512 + 512] * scale
        act[slot * 256 : slot * 256 + 256] = (gate / (1.0 + jnp.exp(-gate)) * upward).astype(BF16)

    drain()
    outs = (o0, o1, o2)
    r1, r2, r5 = (r1_0, r1_1, r1_2), (r2_0, r2_1, r2_2), (r5_0, r5_1, r5_2)
    share = jnp.sum(jnp.where(ids_ref[...] == dev, weights_ref[...], 0.0), axis=0, keepdims=True)
    share = jnp.where(
        core == 0,
        jnp.concatenate([share[:, 0:128], share[:, 256:384]], axis=1),
        jnp.concatenate([share[:, 128:256], share[:, 384:512]], axis=1),
    )

    def down(p, by):
        first, rows, _ = PARTS[p]
        j = plane_of(p, by)
        weight = jnp.concatenate([weight_plane(downt.at[n], p, j) for n in range(2)], axis=1)
        product = jnp.dot(weight, act[...], preferred_element_type=F32)
        product = (product * share).astype(BF16)
        for h in range(2):
            lanes = product[:, h * LANES : (h + 1) * LANES]
            if p == 0:
                o0[2 * h : 2 * h + 2, :, j] = lanes.reshape(2, 4, rows, LANES)
            elif p == 1:
                o1[2 * h : 2 * h + 2, j] = lanes.reshape(2, 4, rows, LANES)
            else:
                o2[j + 2 * h] = lanes.reshape(4, 4, rows, LANES)

    def o_slab(p, by, m):
        a, b, c = axes[p]
        return at(outs[p], **{c: shift(c, by), b: shift(b, m)})

    for p in range(3):
        c = axes[p][2]
        down(p, 2 if p < 2 else 0)
        for m in (2, 0, 3, 1):
            by = 1 if m in (0, 1) else 3
            send(("s1", p, m), o_slab(p, 2, m), r1[p].at[m], neighbour(c, by))
    for p in range(3):
        c = axes[p][2]
        if p < 2:
            down(p, 1)
            down(p, 3)
        else:
            down(p, 1)
        for m in (2, 3):
            send(("s2", p, m), o_slab(p, 1, m), r2[p].at[m, 0], neighbour(c, 1))
        for m in (1, 0):
            send(("s2", p, m), o_slab(p, 3, m), r2[p].at[m, 1], neighbour(c, 3))
    for p in range(2):
        down(p, 0)

    def add_to(slab, other):
        slab[...] = (slab[...].astype(F32) + other[...].astype(F32)).astype(BF16)

    for m in (2, 1, 3, 0):
        for p in range(3):
            c = axes[p][2]
            recv(("s1", p, m), r1[p].at[m])
            by = 1 if m in (0, 1) else 3
            side = 0 if by == 1 else 1
            slab = o_slab(p, by, m)
            add_to(slab, r1[p].at[m])
            send(("s2", p, m), slab, r2[p].at[m, side], neighbour(c, by))

    for m in (2, 1, 3, 0):
        for p in range(3):
            a, b, c = axes[p]
            slab = o_slab(p, 0, m)
            recv(("s2", p, m), r2[p].at[m])
            slab[...] = (
                slab[...].astype(F32) + r2[p][m, 0].astype(F32) + r2[p][m, 1].astype(F32)
            ).astype(BF16)
            for k in (2, 1, 3, 0):
                if k or m:
                    send(("s5", p), slab.at[shift(a, k)], r5[p].at[4 * m + k - 1], away(**{a: k, b: m}))
    for p, (first, rows, _) in enumerate(PARTS):
        a = axes[p][0]
        total = kept[first : first + rows, :] + outs[p][me["x"], me["y"], me["z"]].astype(F32)
        recv(("s5", p), r5[p])
        for n in range(15):
            total = total + r5[p][n].astype(F32)
        out_ref[first : first + rows, :] = total.astype(BF16)
    drain()


def body(
    query_latent, query_rope, cache_latent, cache_rope, lengths, value_up, output_proj, hidden,
    norm_gain, route_ids, route_weights, gate_proj, up_proj, down_proj,
):
    def bf(*shape):
        return pltpu.VMEM(shape, BF16)

    def f32(*shape):
        return pltpu.VMEM(shape, F32)

    users, heads, latent = query_latent.shape
    history = cache_latent.shape[1]
    half = heads * LANES // 2
    rows = [r for _, r, _ in PARTS]
    hbm = pl.BlockSpec(memory_space=pl.ANY)
    vmem = pl.BlockSpec(memory_space=pltpu.VMEM)
    scratch = [
        bf(users, heads, latent), bf(users, heads * ROPE), bf(users, heads, ROPE),
        bf(2 * GROUP, history, latent), bf(2 * GROUP, ROPE, history), f32(latent // LANES, users * heads, LANES),
        bf(*value_up.shape),
        bf(2, 4, 4, 16, half), bf(2, 4, 4, 16, half), bf(FEATS, 2 * half), f32(2, 4, 4, 16, FEATS),
        f32(2, 2, 4, 16, FEATS), bf(2, 4, 16, FEATS), bf(2, 4, 16, FEATS), bf(FEATS, LANES),
        bf(2, 4, 4, FEATS, 256), bf(256, 32 * FEATS),
        f32(4, 1, 640), f32(4, 1, 640), f32(2, 1, 1024),
        bf(4, 2, 512, 640), bf(4, 2, 512, 640), bf(2, 2, 512, 1024), bf(2, 2, 4, 4, FEATS, 256),
        *[bf(4, 4, 4, r, LANES) for r in rows],
        f32(1024, 256), bf(512, 256),
        *[bf(4, 4, 4, r, LANES) for r in rows],
        *[bf(4, 4, r, LANES) for r in rows],
        *[bf(4, 2, 4, r, LANES) for r in rows],
        *[bf(15, r, LANES) for r in rows],
        f32(FEATS, LANES),
        pltpu.SemaphoreType.DMA((2, 2)),
        pltpu.SemaphoreType.DMA((9,)),
        pltpu.SemaphoreType.DMA((2, 6)),
        pltpu.SemaphoreType.DMA((111,)),
        pltpu.SemaphoreType.DMA((107,)),
    ]
    gate_proj = gate_proj.reshape(2, 4, 4, FEATS, 256)
    up_proj = up_proj.reshape(2, 4, 4, FEATS, 256)
    down_proj = down_proj[0]
    out, *_ = pl.pallas_call(
        layer_kernel,
        out_shape=(
            jax.ShapeDtypeStruct((FEATS, LANES), BF16),
            *[jax.ShapeDtypeStruct(a.shape, BF16) for a in (gate_proj, up_proj, down_proj)],
        ),
        in_specs=[
            hbm, hbm, hbm, hbm, pl.BlockSpec(memory_space=pltpu.SMEM), hbm,
            hbm, hbm, vmem, vmem, vmem, hbm, hbm, hbm,
        ],
        out_specs=(vmem, hbm, hbm, hbm),
        scratch_shapes=scratch,
        compiler_params=pltpu.CompilerParams(
            collective_id=0, has_side_effects=True, vmem_limit_bytes=63 * 1024 * 1024
        ),
        cost_estimate=pl.CostEstimate(flops=9 * 10**9, bytes_accessed=27 * 2**20, transcendentals=0),
    )(
        query_latent, query_rope, cache_latent, cache_rope, lengths, value_up,
        output_proj.T, hidden.T, norm_gain.reshape(56, LANES), route_ids.T, route_weights.T,
        gate_proj, up_proj, down_proj,
    )
    return out.T


def solution(mesh):
    return jax.shard_map(
        body,
        mesh=mesh,
        in_specs=(
            P("dev", "sec", None),
            P("dev", "sec"),
            P("dev", None, None),
            P("dev", None, None),
            P("dev"),
            P("sec", None, None),
            P("sec", "dev"),
            P(None, "dev"),
            P(),
            P(),
            P(),
            P("dev", None, "sec"),
            P("dev", None, "sec"),
            P("dev", "sec", None),
        ),
        out_specs=P("sec", "dev"),
        check_vma=False,
    )
```

```python
import functools

import jax
import jax.numpy as jnp
from jax import lax
from jax.experimental import pallas as pl
from jax.experimental.pallas import tpu as pltpu
from jax.sharding import PartitionSpec as P

ROPE = 64
NOPE = 128
norm_eps = 1e-06
MESH = pl.DeviceIdType.MESH
F32 = jnp.float32
BF16 = jnp.bfloat16

PARTS = ((0, 80, "xyz"), (80, 80, "zxy"), (160, 64, "yzx"))
FEATS = 224
LANES = 128
GROUP = 4


def weight_plane(ref, p, j):
    first, rows, _ = PARTS[p]
    if p == 0:
        block = ref[:, :, j, first : first + rows, :]
    elif p == 1:
        block = ref[:, j, :, first : first + rows, :]
    else:
        block = ref[j, :, :, first : first + rows, :]
    return block.reshape(-1, block.shape[-1])


def at(ref, **index):
    return ref.at[tuple(index.get(axis, slice(None)) for axis in "xyz")]


def get(ref, **index):
    return ref[tuple(index.get(axis, slice(None)) for axis in "xyz")]


def layer_kernel(
    query_hbm, rope_hbm, cache_hbm, keys_hbm, lengths_ref, value_up_hbm,
    out_proj_hbm, hidden_hbm, gain_ref, ids_ref, weights_ref, gate_hbm, up_hbm, down_hbm,
    out_ref, gate_far, up_far, down_far,
    query, rope, positional, cache, keys, context, value_up,
    heads0, heads1, out_proj, attn, pair_in, far_in, far_out, hidden,
    weight_in, down_in, gain0, gain1, gain2, wt0, wt1, wt2, downt,
    rt0, rt1, rt2, gate_up, act, o0, o1, o2,
    r1_0, r1_1, r1_2, r2_0, r2_1, r2_2, r5_0, r5_1, r5_2,
    kept, cache_sem, local_sem, stage_sem, send_sem, recv_sem,
):
    sec = lax.axis_index("sec")
    dev = lax.axis_index("dev")
    x_hi, core = lax.div(sec, 2), lax.rem(sec, 2)
    x_lo = lax.div(dev, 16)
    me = {
        "x": x_hi * 2 + x_lo,
        "y": lax.rem(lax.div(dev, 4), 4),
        "z": lax.rem(dev, 4),
    }

    def device(x, y, z, c):
        return (lax.div(x, 2) * 2 + c, lax.rem(x, 2) * 16 + y * 4 + z)

    shifted = {(axis, by): lax.rem(me[axis] + by, 4) for axis in "xyz" for by in (1, 2, 3)}

    def shift(axis, by):
        return me[axis] if by % 4 == 0 else shifted[axis, by % 4]

    ids = {}

    def away(**by):
        offset = tuple(by.get(axis, 0) for axis in "xyz")
        if offset not in ids:
            ids[offset] = device(*[shift(axis, n) for axis, n in zip("xyz", offset)], core)
        return ids[offset]

    def neighbour(axis, by):
        return away(**{axis: by})

    partner = device(me["x"], me["y"], me["z"], 1 - core)
    x_lo_partner = (sec, (1 - x_lo) * 16 + me["y"] * 4 + me["z"])

    tags = {}
    kinds = {}
    sent = []

    def number(tag):
        return tags.setdefault(tag, len(tags))

    def send(tag, src, dst, to):
        i = number(tag)
        kind = tag[:2]
        copy = pltpu.make_async_remote_copy(
            src_ref=src, dst_ref=dst, send_sem=send_sem.at[kinds.setdefault(kind, len(kinds))],
            recv_sem=recv_sem.at[i], device_id=to, device_id_type=MESH,
        )
        copy.start()
        sent.append((kind, copy))

    def drain():
        blocks = dict(hb=4, hf=2, hc=16, hd=8, ga=3, gb=12, gc=32, gd=16, s1=16, s2=32, s5=15)
        alone = {kind: copy for kind, copy in sent}
        for kind, i in kinds.items():
            if kind[0] not in blocks:
                alone[kind].wait_send()
                continue
            p = kind[1]
            held = heads[p] if kind[0][0] == "h" else rts[p]
            views = {
                2: lambda: held.at[:, 0, 0], 3: lambda: held.at[0, 0, 0:3], 4: lambda: held.at[0, 0],
                8: lambda: held.at[0, 0:2], 12: lambda: held.at[0, 0:3], 15: lambda: r5[p],
                16: lambda: held.at[0], 32: lambda: held.at[0:2],
            }
            view = views[blocks[kind[0]]]()
            pltpu.make_async_remote_copy(
                src_ref=view, dst_ref=view, send_sem=send_sem.at[i], recv_sem=recv_sem.at[0],
                device_id=partner, device_id_type=MESH,
            ).wait_send()

    def recv(tag, region):
        i = number(tag)
        pltpu.make_async_remote_copy(
            src_ref=region, dst_ref=region, send_sem=send_sem.at[0], recv_sem=recv_sem.at[i],
            device_id=partner, device_id_type=MESH,
        ).wait_recv()


    offsets = {}
    for first, second in ("xy", "zx", "yz"):
        for m in range(4):
            for k in range(4):
                offset = {"x": 0, "y": 0, "z": 0, first: k, second: m}
                if k or m:
                    offsets[tuple(offset.values())] = offset
    around = [away(**offset) for offset in offsets.values()] + [partner]
    barrier = pltpu.get_barrier_semaphore()
    for other in around:
        pl.semaphore_signal(barrier, inc=1, device_id=other, device_id_type=MESH)

    heads = (heads0, heads1)
    rts = (rt0, rt1, rt2)
    r1, r2, r5 = (r1_0, r1_1, r1_2), (r2_0, r2_1, r2_2), (r5_0, r5_1, r5_2)
    half = heads0.shape[-1]
    own_heads = [at(h, x=x_lo, y=me["y"], z=me["z"]) for h in heads]
    my_hidden = hidden_hbm.at[:, pl.ds(pl.multiple_of(sec * LANES, LANES), LANES)]

    def user_loads(step):
        slot = lax.rem(step, 2) if not isinstance(step, int) else step % 2
        users, place = pl.ds(step * GROUP, GROUP), pl.ds(slot * GROUP, GROUP)
        return (
            pltpu.make_async_copy(cache_hbm.at[users], cache.at[place], cache_sem.at[slot, 0]),
            pltpu.make_async_copy(keys_hbm.at[users], keys.at[place], cache_sem.at[slot, 1]),
        )

    def stage_up(source, n):
        copies = []
        for p, (first, rows, _) in enumerate(PARTS):
            for q in range(2):
                copies.append(
                    pltpu.make_async_copy(
                        source.at[:, :, :, pl.ds(first, rows), pl.ds(q * LANES, LANES)],
                        (o0, o1, o2)[p].at[pl.ds(2 * q, 2)],
                        stage_sem.at[n, 2 * p + q],
                    )
                )
        return copies

    loads = [
        pltpu.make_async_copy(rope_hbm, rope, local_sem.at[0]),
        pltpu.make_async_copy(query_hbm, query, local_sem.at[1]),
        pltpu.make_async_copy(value_up_hbm, value_up, local_sem.at[2]),
        pltpu.make_async_copy(gate_hbm, weight_in, local_sem.at[3]),
        pltpu.make_async_copy(out_proj_hbm, out_proj, local_sem.at[4]),
        pltpu.make_async_copy(down_hbm, down_in, local_sem.at[5]),
        pltpu.make_async_copy(my_hidden, hidden, local_sem.at[6]),
        pltpu.make_async_copy(gate_far, weight_in, local_sem.at[7]),
        pltpu.make_async_copy(down_far, down_in, local_sem.at[8]),
    ]
    up_loads = stage_up(up_hbm, 0), stage_up(up_far, 1)
    for copy in (loads[0], loads[1], *user_loads(0), *user_loads(1)):
        copy.start()
    loads[2].start()

    for p, gain in enumerate((gain0, gain1, gain2)):
        first, rows, _ = PARTS[p]
        width = gain.shape[-1]
        block = lax.broadcasted_iota(jnp.int32, (LANES, width), 1) // rows
        offset = lax.rem(lax.broadcasted_iota(jnp.int32, (LANES, width), 1), rows) + first
        lane = lax.broadcasted_iota(jnp.int32, (LANES, width), 0)
        for j in range(gain.shape[0]):
            if p == 0:
                owner = block * 4 + j
            elif p == 1:
                owner = (block // 4) * 16 + j * 4 + lax.rem(block, 4)
            else:
                owner = j * 16 + block
            place = owner * FEATS + offset
            spread = jnp.dot(
                gain_ref[...], (lax.rem(place, LANES) == lane).astype(F32),
                preferred_element_type=F32, precision=lax.Precision.HIGHEST,
            )
            held = (place // LANES)[:56] == lane[:56]
            gain[j] = jnp.sum(jnp.where(held, spread, 0.0), axis=0, keepdims=True)

    users_here, heads_here = query.shape[0], query.shape[1]
    loads[0].wait()
    wide = heads_here * ROPE
    owner = lax.broadcasted_iota(jnp.int32, (heads_here, wide), 1) // ROPE
    mask = owner == lax.broadcasted_iota(jnp.int32, (heads_here, wide), 0)
    fold = lax.rem(lax.broadcasted_iota(jnp.int32, (wide, ROPE), 0), ROPE)
    fold = (fold == lax.broadcasted_iota(jnp.int32, (wide, ROPE), 1)).astype(F32).astype(BF16)
    for r in range(users_here):
        row = jnp.broadcast_to(rope[r : r + 1, :].astype(F32), (heads_here, wide))
        row = jnp.where(mask, row, 0.0).astype(BF16)
        positional[r] = jnp.dot(row, fold, preferred_element_type=F32).astype(BF16)
    loads[1].wait()
    history = cache.shape[1]
    moment = lax.broadcasted_iota(jnp.int32, (heads_here, history), 1)

    def attend(step, carry):
        slot = lax.rem(step, 2)
        for copy in user_loads(step):
            copy.wait()
        weights = []
        for n in range(GROUP):
            r = step * GROUP + n
            place = slot * GROUP + n
            scores = lax.dot_general(
                query[r], cache[place], (((1,), (1,)), ((), ())), preferred_element_type=F32
            )
            scores += jnp.dot(positional[r], keys[place], preferred_element_type=F32)
            scores = scores * (NOPE + ROPE) ** (-0.5)
            scores = jnp.where(moment < lengths_ref[r], scores, -1e30)
            exponent = jnp.exp(scores - jnp.max(scores, axis=-1, keepdims=True))
            weights.append((exponent / jnp.sum(exponent, axis=-1, keepdims=True)).astype(BF16))
        for n in range(GROUP):
            r = step * GROUP + n
            value = jnp.dot(weights[n], cache[slot * GROUP + n], preferred_element_type=F32)
            value = value.astype(BF16).astype(F32)
            rows = pl.ds(pl.multiple_of(r * heads_here, heads_here), heads_here)
            for t in range(context.shape[0]):
                context[t, rows, :] = value[:, t * LANES : (t + 1) * LANES]

        @pl.when(step < users_here // GROUP - 2)
        def _():
            for copy in user_loads(step + 2):
                copy.start()

        return carry

    lax.fori_loop(0, 1, attend, 0)
    pl.semaphore_wait(barrier, len(around))
    send(("wg",), gate_hbm, gate_far, partner)
    send(("wu",), up_hbm, up_far, partner)
    send(("wd",), down_hbm, down_far, partner)
    lax.fori_loop(1, users_here // GROUP, attend, 0)
    for copy in (loads[3], *up_loads[0], *loads[4:7]):
        copy.start()
    loads[2].wait()

    def head_value(h):
        tiles = [context[t, pl.ds(h, users_here, stride=heads_here), :] for t in range(context.shape[0])]
        rows = jnp.concatenate(tiles, axis=1).astype(BF16)
        value = jnp.dot(rows, value_up[h], preferred_element_type=F32)
        return value.astype(BF16)

    order = (("y", "z"), ("z", "y"))

    def head_block(p, k, **index):
        place = {"x": lax.rem(x_lo + k, 2), "y": me["y"], "z": me["z"]}
        place.update(index)
        return at(heads[p], **place)

    def head_slab(p, **index):
        return at(heads[p], **index)

    for p in range(2):
        for h in range(heads_here // 2):
            heads[p][x_lo, me["y"], me["z"], :, h * 128 : h * 128 + 128] = head_value(p * (heads_here // 2) + h)
        send(("hx", p), own_heads[p], own_heads[p], x_lo_partner)
        b, c = order[p]
        for by in (1, 3):
            send(("hb", p, 0, by), own_heads[p], own_heads[p], neighbour(b, by))
        for by in (1, 3):
            send(("hc", p, 0, by), own_heads[p], own_heads[p], neighbour(c, by))

    wts = (wt0, wt1, wt2)
    gains = (gain0, gain1, gain2)

    def gate_task(slot, p):
        if p == 0:
            loads[7 if slot else 3].wait()

        def step(j, carry):
            block = weight_plane(weight_in, p, j).T.astype(F32) * gains[p][j]
            wts[p][j, slot, 0:256, :] = block.astype(BF16)
            return carry

        lax.fori_loop(0, wts[p].shape[0], step, 0)

    def up_task(slot, p):
        if p == 0:
            for copy in up_loads[slot]:
                copy.wait()

        def step(j, carry):
            for q in range(2):
                if p == 0:
                    block = o0[2 * q : 2 * q + 2, :, j]
                elif p == 1:
                    block = o1[2 * q : 2 * q + 2, j]
                else:
                    block = o2[2 * q + j]
                block = block.reshape(-1, LANES).T.astype(F32) * gains[p][j]
                wts[p][j, slot, 256 + q * LANES : 256 + (q + 1) * LANES, :] = block.astype(BF16)
            return carry

        lax.fori_loop(0, wts[p].shape[0], step, 0)

    def down_task(slot, half_of):
        if half_of == 0:
            loads[8 if slot else 5].wait()

        def step(j, carry):
            block = down_in[:, pl.ds(pl.multiple_of(j * 896, 896), 896)].T
            downt[slot, j // 4, lax.rem(j, 4)] = block.reshape(4, FEATS, 256)
            return carry

        lax.fori_loop(4 * half_of, 4 * half_of + 4, step, 0)

    tasks = []
    for slot in range(2):
        tasks += [functools.partial(gate_task, slot, p) for p in range(3)]
        tasks += [functools.partial(up_task, slot, p) for p in range(3)]
        tasks += [functools.partial(down_task, slot, n) for n in range(2)]

    def fetch_partner():
        recv(("wg",), gate_far)
        loads[7].start()
        recv(("wu",), up_far)
        for copy in up_loads[1]:
            copy.start()
        recv(("wd",), down_far)
        loads[8].start()

    def work(count=1):
        for task in tasks[:count]:
            task()
        del tasks[:count]

    work(8)

    def slab_sends(p, m):
        b, c = order[p]
        slab = head_slab(p, **{b: shift(b, m), c: me[c]})
        for by in (1, 3):
            send(("hc", p, m, by), slab, slab, neighbour(c, by))

    for p in range(2):
        b, c = order[p]
        other = head_block(p, 1)
        recv(("hx", p), other)
        for by in (1, 3):
            send(("hb", p, 1, by), other, other, neighbour(b, by))
    for p in range(2):
        other = head_block(p, 1)
        for by in (1, 3):
            send(("hc", p, 0, by), other, other, neighbour(order[p][1], by))
    for p in range(2):
        b, c = order[p]
        block = head_block(p, 0, **{b: shift(b, 3)})
        recv(("hb", p, 0, 1), block)
        send(("hf", p), block, block, neighbour(b, 1))
        recv(("hb", p, 0, 3), head_block(p, 0, **{b: shift(b, 1)}))
    for p in range(2):
        b, c = order[p]
        block = head_block(p, 1, **{b: shift(b, 1)})
        recv(("hb", p, 1, 3), block)
        send(("hf", p), block, block, neighbour(b, 3))
        slab_sends(p, 1)
        recv(("hb", p, 1, 1), head_block(p, 1, **{b: shift(b, 3)}))
        slab_sends(p, 3)
    for p in range(2):
        b, c = order[p]
        recv(("hf", p), head_slab(p, **{b: shift(b, 2), c: me[c]}))
        slab_sends(p, 2)
    fetch_partner()

    def project(p, by, first=False):
        c = order[p][1]
        j = shift(c, by)
        rows = get(heads[p], **{c: j}).reshape(-1, half)
        product = lax.dot_general(
            rows, out_proj[:, p * half : (p + 1) * half], (((1,), (1,)), ((), ())), preferred_element_type=F32
        )
        product = product.reshape(2, 4, 16, FEATS)
        if c == "z":
            attn[:, :, j] = product
        else:
            attn[:, j] += product

    loads[4].wait()
    project(0, 0)
    for m in (0, 1, 3, 2):
        for p in range(2):
            b, c = order[p]
            for by in (1, 3):
                region = head_slab(p, **{b: shift(b, m), c: shift(c, -by)})
                recv(("hc", p, m, by), region)
                passed = head_slab(p, **{"x": by // 2, b: shift(b, m), c: shift(c, -by)})
                send(("hd", p), passed, passed, neighbour(c, by))
        work(2)
    work(len(tasks))
    project(0, 1)
    project(0, 3)
    recv(("hd", 0), head_slab(0, **{order[0][1]: shift(order[0][1], 2)}))
    project(0, 2)
    for by in (0, 1, 3):
        project(1, by)
    recv(("hd", 1), head_slab(1, **{order[1][1]: shift(order[1][1], 2)}))
    project(1, 2)

    attn_mine = attn.at[:, pl.ds(core * 2, 2)]
    send(("pair",), attn.at[:, pl.ds((1 - core) * 2, 2)], pair_in, partner)
    recv(("pair",), pair_in)
    far_out[...] = (attn_mine[1 - x_hi] + pair_in[1 - x_hi]).astype(BF16)
    send(("far",), far_out, far_in, neighbour("x", 2))
    loads[6].wait()
    near = (attn_mine[x_hi] + pair_in[x_hi]).reshape(LANES, FEATS)
    recv(("far",), far_in)
    residual = near + far_in[...].reshape(LANES, FEATS).astype(F32)
    residual = jnp.concatenate([residual, jnp.zeros((LANES, 32), F32)], axis=1).T[:FEATS]
    residual = residual + hidden[...].astype(F32)
    kept[...] = residual
    routed = residual.astype(BF16)

    for p, (first, rows, _) in enumerate(PARTS):
        rts[p][me["x"], me["y"], me["z"]] = routed[first : first + rows]

    def spot(p, **index):
        place = dict(me)
        place.update(index)
        return at(rts[p], **place)

    axes = [tuple(o) for _, _, o in PARTS]
    for p in range(3):
        a, b, c = axes[p]
        for k in (1, 3, 2):
            send(("ga", p, k), spot(p), spot(p), away(**{a: k}))
        for by in (1, 3):
            send(("gc", p, 0, by), spot(p), spot(p), neighbour(c, by))
    for p in range(3):
        a, b, c = axes[p]
        for m in (2, 1, 3):
            send(("gb", p, m), spot(p), spot(p), away(**{b: m}))
    for k in (1, 3, 2):
        for p in range(3):
            a, b, c = axes[p]
            block = spot(p, **{a: shift(a, k)})
            recv(("ga", p, 4 - k), block)
            for m in (2, 1, 3):
                send(("gb", p, m), block, block, away(**{b: m}))
            for by in (1, 3):
                send(("gc", p, 0, by), block, block, neighbour(c, by))
    for m in (1, 3, 2):
        for p in range(3):
            a, b, c = axes[p]
            slab = at(rts[p], **{b: shift(b, m), c: me[c]})
            recv(("gb", p, 4 - m), slab)
            for by in (1, 3):
                send(("gc", p, m, by), slab, slab, neighbour(c, by))

    def pass_on(m):
        for p in range(3):
            a, b, c = axes[p]
            for by in (1, 3):
                region = at(rts[p], **{b: shift(b, m), c: shift(c, -by)})
                recv(("gc", p, m, by), region)
                half_of = pl.ds(0, 2) if by == 1 else pl.ds(2, 2)
                passed = at(rts[p], **{a: half_of, b: shift(b, m), c: shift(c, -by)})
                send(("gd", p), passed, passed, neighbour(c, by))

    pass_on(0)

    totals = {"square": jnp.zeros((1, 256), F32), "first": True}

    def users_of(p, by):
        if p == 0:
            block = rts[0][:, :, shift("z", by)]
            low, high = block[0:2], block[2:4]
        elif p == 1:
            block = rts[1][:, shift("y", by)]
            low, high = block[0:2], block[2:4]
        else:
            plane = lax.rem(x_lo + by, 2)
            low, high = rts[2][plane], rts[2][plane + 2]
        return jnp.concatenate([low.reshape(-1, LANES), high.reshape(-1, LANES)], axis=1)

    def plane_of(p, by):
        if p == 2:
            return lax.rem(x_lo + by, 2)
        return shift(axes[p][2], by)

    def multiply(*planes):
        weights, rows = [], []
        for p, by in planes:
            block = users_of(p, by)
            wide = block.astype(F32)
            totals["square"] = totals["square"] + jnp.sum(wide * wide, axis=0, keepdims=True)
            weight = wts[p][plane_of(p, by)]
            weights.append(weight.reshape(1024, weight.shape[-1]))
            rows.append(block)
        if len(planes) > 1:
            weights, rows = [jnp.concatenate(weights, axis=1)], [jnp.concatenate(rows, axis=0)]
        product = jnp.dot(weights[0], rows[0], preferred_element_type=F32)
        if totals["first"]:
            gate_up[...] = product
        else:
            gate_up[...] += product
        totals["first"] = False

    multiply((0, 0), (1, 0))
    for m in (1, 3, 2):
        pass_on(m)
    multiply((0, 1), (0, 3))
    multiply((1, 1), (1, 3))
    multiply((2, 1),)
    for p in range(2):
        c = axes[p][2]
        recv(("gd", p), at(rts[p], **{c: shift(c, 2)}))
    multiply((0, 2), (1, 2))
    recv(("gd", 2), at(rts[2], x=shift("x", 2)))
    multiply((2, 0),)

    scale = lax.rsqrt(totals["square"] * (1.0 / (32 * FEATS)) + norm_eps)
    for slot in range(2):
        gate = gate_up[slot * 512 : slot * 512 + 256] * scale
        upward = gate_up[slot * 512 + 256 : slot * 512 + 512] * scale
        act[slot * 256 : slot * 256 + 256] = (gate / (1.0 + jnp.exp(-gate)) * upward).astype(BF16)

    outs = (o0, o1, o2)
    share = jnp.sum(jnp.where(ids_ref[...] == dev, weights_ref[...], 0.0), axis=0, keepdims=True)
    share = jnp.where(
        core == 0,
        jnp.concatenate([share[:, 0:128], share[:, 256:384]], axis=1),
        jnp.concatenate([share[:, 128:256], share[:, 384:512]], axis=1),
    )

    def down(p, by):
        first, rows, _ = PARTS[p]
        j = plane_of(p, by)
        weight = jnp.concatenate([weight_plane(downt.at[n], p, j) for n in range(2)], axis=1)
        product = jnp.dot(weight, act[...], preferred_element_type=F32)
        product = (product * share).astype(BF16)
        for h in range(2):
            lanes = product[:, h * LANES : (h + 1) * LANES]
            if p == 0:
                o0[2 * h : 2 * h + 2, :, j] = lanes.reshape(2, 4, rows, LANES)
            elif p == 1:
                o1[2 * h : 2 * h + 2, j] = lanes.reshape(2, 4, rows, LANES)
            else:
                o2[j + 2 * h] = lanes.reshape(4, 4, rows, LANES)

    def o_slab(p, by, m):
        a, b, c = axes[p]
        return at(outs[p], **{c: shift(c, by), b: shift(b, m)})

    for p in range(3):
        c = axes[p][2]
        down(p, 2 if p < 2 else 0)
        for m in (2, 0, 3, 1):
            by = 1 if m in (0, 1) else 3
            send(("s1", p, m), o_slab(p, 2, m), r1[p].at[m], neighbour(c, by))
    for p in range(3):
        c = axes[p][2]
        if p < 2:
            down(p, 1)
            down(p, 3)
        else:
            down(p, 1)
        for m in (2, 3):
            send(("s2", p, m), o_slab(p, 1, m), r2[p].at[m, 0], neighbour(c, 1))
        for m in (1, 0):
            send(("s2", p, m), o_slab(p, 3, m), r2[p].at[m, 1], neighbour(c, 3))
    for p in range(2):
        down(p, 0)

    def add_to(slab, other):
        slab[...] = (slab[...].astype(F32) + other[...].astype(F32)).astype(BF16)

    for m in (2, 1, 3, 0):
        for p in range(3):
            c = axes[p][2]
            recv(("s1", p, m), r1[p].at[m])
            by = 1 if m in (0, 1) else 3
            side = 0 if by == 1 else 1
            slab = o_slab(p, by, m)
            add_to(slab, r1[p].at[m])
            send(("s2", p, m), slab, r2[p].at[m, side], neighbour(c, by))

    for m in (2, 1, 3, 0):
        for p in range(3):
            a, b, c = axes[p]
            slab = o_slab(p, 0, m)
            recv(("s2", p, m), r2[p].at[m])
            slab[...] = (
                slab[...].astype(F32) + r2[p][m, 0].astype(F32) + r2[p][m, 1].astype(F32)
            ).astype(BF16)
            for k in (2, 1, 3, 0):
                if k or m:
                    send(("s5", p), slab.at[shift(a, k)], r5[p].at[4 * m + k - 1], away(**{a: k, b: m}))
    for p, (first, rows, _) in enumerate(PARTS):
        a = axes[p][0]
        total = kept[first : first + rows, :] + outs[p][me["x"], me["y"], me["z"]].astype(F32)
        recv(("s5", p), r5[p])
        for n in range(15):
            total = total + r5[p][n].astype(F32)
        out_ref[first : first + rows, :] = total.astype(BF16)
    drain()


def body(
    query_latent, query_rope, cache_latent, cache_rope, lengths, value_up, output_proj, hidden,
    norm_gain, route_ids, route_weights, gate_proj, up_proj, down_proj,
):
    def bf(*shape):
        return pltpu.VMEM(shape, BF16)

    def f32(*shape):
        return pltpu.VMEM(shape, F32)

    users, heads, latent = query_latent.shape
    history = cache_latent.shape[1]
    half = heads * LANES // 2
    rows = [r for _, r, _ in PARTS]
    hbm = pl.BlockSpec(memory_space=pl.ANY)
    vmem = pl.BlockSpec(memory_space=pltpu.VMEM)
    scratch = [
        bf(users, heads, latent), bf(users, heads * ROPE), bf(users, heads, ROPE),
        bf(2 * GROUP, history, latent), bf(2 * GROUP, ROPE, history), f32(latent // LANES, users * heads, LANES),
        bf(*value_up.shape),
        bf(2, 4, 4, 16, half), bf(2, 4, 4, 16, half), bf(FEATS, 2 * half), f32(2, 4, 4, 16, FEATS),
        f32(2, 2, 4, 16, FEATS), bf(2, 4, 16, FEATS), bf(2, 4, 16, FEATS), bf(FEATS, LANES),
        bf(2, 4, 4, FEATS, 256), bf(256, 32 * FEATS),
        f32(4, 1, 640), f32(4, 1, 640), f32(2, 1, 1024),
        bf(4, 2, 512, 640), bf(4, 2, 512, 640), bf(2, 2, 512, 1024), bf(2, 2, 4, 4, FEATS, 256),
        *[bf(4, 4, 4, r, LANES) for r in rows],
        f32(1024, 256), bf(512, 256),
        *[bf(4, 4, 4, r, LANES) for r in rows],
        *[bf(4, 4, r, LANES) for r in rows],
        *[bf(4, 2, 4, r, LANES) for r in rows],
        *[bf(15, r, LANES) for r in rows],
        f32(FEATS, LANES),
        pltpu.SemaphoreType.DMA((2, 2)),
        pltpu.SemaphoreType.DMA((9,)),
        pltpu.SemaphoreType.DMA((2, 6)),
        pltpu.SemaphoreType.DMA((36,)),
        pltpu.SemaphoreType.DMA((107,)),
    ]
    gate_proj = gate_proj.reshape(2, 4, 4, FEATS, 256)
    up_proj = up_proj.reshape(2, 4, 4, FEATS, 256)
    down_proj = down_proj[0]
    out, *_ = pl.pallas_call(
        layer_kernel,
        out_shape=(
            jax.ShapeDtypeStruct((FEATS, LANES), BF16),
            *[jax.ShapeDtypeStruct(a.shape, BF16) for a in (gate_proj, up_proj, down_proj)],
        ),
        in_specs=[
            hbm, hbm, hbm, hbm, pl.BlockSpec(memory_space=pltpu.SMEM), hbm,
            hbm, hbm, vmem, vmem, vmem, hbm, hbm, hbm,
        ],
        out_specs=(vmem, hbm, hbm, hbm),
        scratch_shapes=scratch,
        compiler_params=pltpu.CompilerParams(
            collective_id=0, has_side_effects=True, vmem_limit_bytes=63 * 1024 * 1024
        ),
        cost_estimate=pl.CostEstimate(flops=9 * 10**9, bytes_accessed=27 * 2**20, transcendentals=0),
    )(
        query_latent, query_rope, cache_latent, cache_rope, lengths, value_up,
        output_proj.T, hidden.T, norm_gain.reshape(56, LANES), route_ids.T, route_weights.T,
        gate_proj, up_proj, down_proj,
    )
    return out.T


def solution(mesh):
    return jax.shard_map(
        body,
        mesh=mesh,
        in_specs=(
            P("dev", "sec", None),
            P("dev", "sec"),
            P("dev", None, None),
            P("dev", None, None),
            P("dev"),
            P("sec", None, None),
            P("sec", "dev"),
            P(None, "dev"),
            P(),
            P(),
            P(),
            P("dev", None, "sec"),
            P("dev", None, "sec"),
            P("dev", "sec", None),
        ),
        out_specs=P("sec", "dev"),
        check_vma=False,
    )
```

```python
import functools

import jax
import jax.numpy as jnp
from jax import lax
from jax.experimental import pallas as pl
from jax.experimental.pallas import tpu as pltpu
from jax.sharding import PartitionSpec as P

ROPE = 64
NOPE = 128
norm_eps = 1e-06
MESH = pl.DeviceIdType.MESH
F32 = jnp.float32
BF16 = jnp.bfloat16

PARTS = ((0, 80, "xyz"), (80, 80, "zxy"), (160, 64, "yzx"))
FEATS = 224
LANES = 128
GROUP = 4


def weight_plane(ref, p, j):
    first, rows, _ = PARTS[p]
    if p == 0:
        block = ref[:, :, j, first : first + rows, :]
    elif p == 1:
        block = ref[:, j, :, first : first + rows, :]
    else:
        block = ref[j, :, :, first : first + rows, :]
    return block.reshape(-1, block.shape[-1])


def at(ref, **index):
    return ref.at[tuple(index.get(axis, slice(None)) for axis in "xyz")]


def get(ref, **index):
    return ref[tuple(index.get(axis, slice(None)) for axis in "xyz")]


def layer_kernel(
    query_hbm, rope_hbm, cache_hbm, keys_hbm, lengths_ref, value_up_hbm,
    out_proj_hbm, hidden_hbm, gain_ref, ids_ref, weights_ref, gate_hbm, up_hbm, down_hbm,
    out_ref, gate_far, up_far, down_far,
    query, rope, positional, cache, keys, context, value_up,
    heads0, heads1, out_proj, attn, pair_in, far_in, far_out, hidden,
    weight_in, down_in, gain0, gain1, gain2, wt0, wt1, wt2, downt,
    rt0, rt1, rt2, gate_up, act, o0, o1, o2,
    r1_0, r1_1, r1_2, r2_0, r2_1, r2_2, r5_0, r5_1, r5_2,
    kept, cache_sem, local_sem, stage_sem, send_sem, recv_sem,
):
    sec = lax.axis_index("sec")
    dev = lax.axis_index("dev")
    x_hi, core = lax.div(sec, 2), lax.rem(sec, 2)
    x_lo = lax.div(dev, 16)
    me = {
        "x": x_hi * 2 + x_lo,
        "y": lax.rem(lax.div(dev, 4), 4),
        "z": lax.rem(dev, 4),
    }

    def device(x, y, z, c):
        return (lax.div(x, 2) * 2 + c, lax.rem(x, 2) * 16 + y * 4 + z)

    shifted = {(axis, by): lax.rem(me[axis] + by, 4) for axis in "xyz" for by in (1, 2, 3)}

    def shift(axis, by):
        return me[axis] if by % 4 == 0 else shifted[axis, by % 4]

    ids = {}

    def away(**by):
        offset = tuple(by.get(axis, 0) for axis in "xyz")
        if offset not in ids:
            ids[offset] = device(*[shift(axis, n) for axis, n in zip("xyz", offset)], core)
        return ids[offset]

    def neighbour(axis, by):
        return away(**{axis: by})

    partner = device(me["x"], me["y"], me["z"], 1 - core)
    x_lo_partner = (sec, (1 - x_lo) * 16 + me["y"] * 4 + me["z"])

    tags = {}
    kinds = {}
    sent = []

    def number(tag):
        return tags.setdefault(tag, len(tags))

    def send(tag, src, dst, to):
        i = number(tag)
        kind = tag[:2]
        copy = pltpu.make_async_remote_copy(
            src_ref=src, dst_ref=dst, send_sem=send_sem.at[kinds.setdefault(kind, len(kinds))],
            recv_sem=recv_sem.at[i], device_id=to, device_id_type=MESH,
        )
        copy.start()
        sent.append((kind, copy))

    def drain():
        blocks = dict(hb=4, hf=2, hc=16, hd=8, ga=3, gb=12, gc=32, gd=16, s1=16, s2=32, s5=15)
        alone = {kind: copy for kind, copy in sent}
        for kind, i in kinds.items():
            if kind[0] not in blocks:
                alone[kind].wait_send()
                continue
            p = kind[1]
            held = heads[p] if kind[0][0] == "h" else rts[p]
            views = {
                2: lambda: held.at[:, 0, 0], 3: lambda: held.at[0, 0, 0:3], 4: lambda: held.at[0, 0],
                8: lambda: held.at[0, 0:2], 12: lambda: held.at[0, 0:3], 15: lambda: r5[p],
                16: lambda: held.at[0], 32: lambda: held.at[0:2],
            }
            view = views[blocks[kind[0]]]()
            pltpu.make_async_remote_copy(
                src_ref=view, dst_ref=view, send_sem=send_sem.at[i], recv_sem=recv_sem.at[0],
                device_id=partner, device_id_type=MESH,
            ).wait_send()

    def recv(tag, region):
        i = number(tag)
        pltpu.make_async_remote_copy(
            src_ref=region, dst_ref=region, send_sem=send_sem.at[0], recv_sem=recv_sem.at[i],
            device_id=partner, device_id_type=MESH,
        ).wait_recv()


    offsets = {}
    for first, second in ("xy", "zx", "yz"):
        for m in range(4):
            for k in range(4):
                offset = {"x": 0, "y": 0, "z": 0, first: k, second: m}
                if k or m:
                    offsets[tuple(offset.values())] = offset
    around = [away(**offset) for offset in offsets.values()] + [partner]
    barrier = pltpu.get_barrier_semaphore()
    for other in around:
        pl.semaphore_signal(barrier, inc=1, device_id=other, device_id_type=MESH)

    heads = (heads0, heads1)
    rts = (rt0, rt1, rt2)
    r1, r2, r5 = (r1_0, r1_1, r1_2), (r2_0, r2_1, r2_2), (r5_0, r5_1, r5_2)
    half = heads0.shape[-1]
    own_heads = [at(h, x=x_lo, y=me["y"], z=me["z"]) for h in heads]
    my_hidden = hidden_hbm.at[:, pl.ds(pl.multiple_of(sec * LANES, LANES), LANES)]

    def user_loads(step):
        slot = lax.rem(step, 2) if not isinstance(step, int) else step % 2
        users, place = pl.ds(step * GROUP, GROUP), pl.ds(slot * GROUP, GROUP)
        return (
            pltpu.make_async_copy(cache_hbm.at[users], cache.at[place], cache_sem.at[slot, 0]),
            pltpu.make_async_copy(keys_hbm.at[users], keys.at[place], cache_sem.at[slot, 1]),
        )

    def stage_up(source, n):
        copies = []
        for p, (first, rows, _) in enumerate(PARTS):
            for q in range(2):
                copies.append(
                    pltpu.make_async_copy(
                        source.at[:, :, :, pl.ds(first, rows), pl.ds(q * LANES, LANES)],
                        (o0, o1, o2)[p].at[pl.ds(2 * q, 2)],
                        stage_sem.at[n, 2 * p + q],
                    )
                )
        return copies

    loads = [
        pltpu.make_async_copy(rope_hbm, rope, local_sem.at[0]),
        pltpu.make_async_copy(query_hbm, query, local_sem.at[1]),
        pltpu.make_async_copy(value_up_hbm, value_up, local_sem.at[2]),
        pltpu.make_async_copy(gate_hbm, weight_in, local_sem.at[3]),
        pltpu.make_async_copy(out_proj_hbm, out_proj, local_sem.at[4]),
        pltpu.make_async_copy(down_hbm, down_in, local_sem.at[5]),
        pltpu.make_async_copy(my_hidden, hidden, local_sem.at[6]),
        pltpu.make_async_copy(gate_far, weight_in, local_sem.at[7]),
        pltpu.make_async_copy(down_far, down_in, local_sem.at[8]),
    ]
    up_loads = stage_up(up_hbm, 0), stage_up(up_far, 1)
    for copy in (loads[0], loads[1], *user_loads(0), *user_loads(1)):
        copy.start()
    loads[2].start()

    for p, gain in enumerate((gain0, gain1, gain2)):
        first, rows, _ = PARTS[p]
        width = gain.shape[-1]
        block = lax.broadcasted_iota(jnp.int32, (LANES, width), 1) // rows
        offset = lax.rem(lax.broadcasted_iota(jnp.int32, (LANES, width), 1), rows) + first
        lane = lax.broadcasted_iota(jnp.int32, (LANES, width), 0)
        for j in range(gain.shape[0]):
            if p == 0:
                owner = block * 4 + j
            elif p == 1:
                owner = (block // 4) * 16 + j * 4 + lax.rem(block, 4)
            else:
                owner = j * 16 + block
            place = owner * FEATS + offset
            spread = jnp.dot(
                gain_ref[...], (lax.rem(place, LANES) == lane).astype(F32),
                preferred_element_type=F32, precision=lax.Precision.HIGHEST,
            )
            held = (place // LANES)[:56] == lane[:56]
            gain[j] = jnp.sum(jnp.where(held, spread, 0.0), axis=0, keepdims=True)

    users_here, heads_here = query.shape[0], query.shape[1]
    loads[0].wait()
    wide = heads_here * ROPE
    owner = lax.broadcasted_iota(jnp.int32, (heads_here, wide), 1) // ROPE
    mask = owner == lax.broadcasted_iota(jnp.int32, (heads_here, wide), 0)
    fold = lax.rem(lax.broadcasted_iota(jnp.int32, (wide, ROPE), 0), ROPE)
    fold = (fold == lax.broadcasted_iota(jnp.int32, (wide, ROPE), 1)).astype(F32).astype(BF16)
    for r in range(users_here):
        row = jnp.broadcast_to(rope[r : r + 1, :].astype(F32), (heads_here, wide))
        row = jnp.where(mask, row, 0.0).astype(BF16)
        positional[r] = jnp.dot(row, fold, preferred_element_type=F32).astype(BF16)
    loads[1].wait()
    history = cache.shape[1]
    moment = lax.broadcasted_iota(jnp.int32, (heads_here, history), 1)

    def attend(step, carry):
        slot = lax.rem(step, 2)
        for copy in user_loads(step):
            copy.wait()
        weights = []
        for n in range(GROUP):
            r = step * GROUP + n
            place = slot * GROUP + n
            scores = lax.dot_general(
                query[r], cache[place], (((1,), (1,)), ((), ())), preferred_element_type=F32
            )
            scores += jnp.dot(positional[r], keys[place], preferred_element_type=F32)
            scores = scores * (NOPE + ROPE) ** (-0.5)
            scores = jnp.where(moment < lengths_ref[r], scores, -1e30)
            exponent = jnp.exp(scores - jnp.max(scores, axis=-1, keepdims=True))
            weights.append((exponent / jnp.sum(exponent, axis=-1, keepdims=True)).astype(BF16))
        for n in range(GROUP):
            r = step * GROUP + n
            value = jnp.dot(weights[n], cache[slot * GROUP + n], preferred_element_type=F32)
            value = value.astype(BF16).astype(F32)
            rows = pl.ds(pl.multiple_of(r * heads_here, heads_here), heads_here)
            for t in range(context.shape[0]):
                context[t, rows, :] = value[:, t * LANES : (t + 1) * LANES]

        @pl.when(step < users_here // GROUP - 2)
        def _():
            for copy in user_loads(step + 2):
                copy.start()

        return carry

    lax.fori_loop(0, 1, attend, 0)
    pl.semaphore_wait(barrier, len(around))
    send(("wg",), gate_hbm, gate_far, partner)
    send(("wu",), up_hbm, up_far, partner)
    send(("wd",), down_hbm, down_far, partner)
    lax.fori_loop(1, users_here // GROUP, attend, 0)
    for copy in (loads[3], *up_loads[0], *loads[4:7]):
        copy.start()
    loads[2].wait()

    def head_value(h):
        tiles = [context[t, pl.ds(h, users_here, stride=heads_here), :] for t in range(context.shape[0])]
        rows = jnp.concatenate(tiles, axis=1).astype(BF16)
        value = jnp.dot(rows, value_up[h], preferred_element_type=F32)
        return value.astype(BF16)

    order = (("y", "z"), ("z", "y"))

    def head_block(p, k, **index):
        place = {"x": lax.rem(x_lo + k, 2), "y": me["y"], "z": me["z"]}
        place.update(index)
        return at(heads[p], **place)

    def head_slab(p, **index):
        return at(heads[p], **index)

    for p in range(2):
        for h in range(heads_here // 2):
            heads[p][x_lo, me["y"], me["z"], :, h * 128 : h * 128 + 128] = head_value(p * (heads_here // 2) + h)
        send(("hx", p), own_heads[p], own_heads[p], x_lo_partner)
        b, c = order[p]
        for by in (1, 3):
            send(("hb", p, 0, by), own_heads[p], own_heads[p], neighbour(b, by))
        for by in (1, 3):
            send(("hc", p, 0, by), own_heads[p], own_heads[p], neighbour(c, by))

    wts = (wt0, wt1, wt2)
    gains = (gain0, gain1, gain2)

    def gate_task(slot, p):
        if p == 0:
            loads[7 if slot else 3].wait()

        def step(j, carry):
            block = weight_plane(weight_in, p, j).T.astype(F32) * gains[p][j]
            wts[p][j, slot, 0:256, :] = block.astype(BF16)
            return carry

        lax.fori_loop(0, wts[p].shape[0], step, 0)

    def up_task(slot, p):
        if p == 0:
            for copy in up_loads[slot]:
                copy.wait()

        def step(j, carry):
            for q in range(2):
                if p == 0:
                    block = o0[2 * q : 2 * q + 2, :, j]
                elif p == 1:
                    block = o1[2 * q : 2 * q + 2, j]
                else:
                    block = o2[2 * q + j]
                block = block.reshape(-1, LANES).T.astype(F32) * gains[p][j]
                wts[p][j, slot, 256 + q * LANES : 256 + (q + 1) * LANES, :] = block.astype(BF16)
            return carry

        lax.fori_loop(0, wts[p].shape[0], step, 0)

    def down_task(slot, half_of):
        if half_of == 0:
            loads[8 if slot else 5].wait()

        def step(j, carry):
            block = down_in[:, pl.ds(pl.multiple_of(j * 896, 896), 896)].T
            downt[slot, j // 4, lax.rem(j, 4)] = block.reshape(4, FEATS, 256)
            return carry

        lax.fori_loop(4 * half_of, 4 * half_of + 4, step, 0)

    tasks = []
    for slot in range(2):
        tasks += [functools.partial(gate_task, slot, p) for p in range(3)]
        tasks += [functools.partial(up_task, slot, p) for p in range(3)]
        tasks += [functools.partial(down_task, slot, n) for n in range(2)]

    def fetch_partner():
        recv(("wg",), gate_far)
        loads[7].start()
        recv(("wu",), up_far)
        for copy in up_loads[1]:
            copy.start()
        recv(("wd",), down_far)
        loads[8].start()

    def work(count=1):
        for task in tasks[:count]:
            task()
        del tasks[:count]

    work(4)

    def onward(p, m, k):
        b, c = order[p]
        block = head_block(p, k, **{b: shift(b, m)})
        for by in (1, 3):
            send(("hc", p, m, by), block, block, neighbour(c, by))

    def from_sides(k):
        for p in range(2):
            b, c = order[p]
            for m, by in ((3, 1), (1, 3)) if k == 0 else ((1, 3), (3, 1)):
                block = head_block(p, k, **{b: shift(b, m)})
                recv(("hb", p, k, by), block)
                if (by == 1) == (k == 0):
                    send(("hf", p, k), block, block, neighbour(b, by))
        for p in range(2):
            for m in (3, 1):
                onward(p, m, k)

    def from_opposite(k):
        for p in range(2):
            b, c = order[p]
            recv(("hf", p, k), head_block(p, k, **{b: shift(b, 2)}))
            onward(p, 2, k)

    from_sides(0)
    work(2)
    for p in range(2):
        b, c = order[p]
        other = head_block(p, 1)
        recv(("hx", p), other)
        for by in (1, 3):
            send(("hb", p, 1, by), other, other, neighbour(b, by))
    for p in range(2):
        onward(p, 0, 1)
    from_opposite(0)
    work(2)
    from_sides(1)
    from_opposite(1)
    fetch_partner()

    def project(p, by, first=False):
        c = order[p][1]
        j = shift(c, by)
        rows = get(heads[p], **{c: j}).reshape(-1, half)
        product = lax.dot_general(
            rows, out_proj[:, p * half : (p + 1) * half], (((1,), (1,)), ((), ())), preferred_element_type=F32
        )
        product = product.reshape(2, 4, 16, FEATS)
        if c == "z":
            attn[:, :, j] = product
        else:
            attn[:, j] += product

    loads[4].wait()
    project(0, 0)
    for m in (0, 1, 3, 2):
        for p in range(2):
            b, c = order[p]
            for by in (1, 3):
                region = head_slab(p, **{b: shift(b, m), c: shift(c, -by)})
                recv(("hc", p, m, by), region)
                passed = head_slab(p, **{"x": by // 2, b: shift(b, m), c: shift(c, -by)})
                send(("hd", p), passed, passed, neighbour(c, by))
        work(2)
    work(len(tasks))
    project(0, 1)
    project(0, 3)
    recv(("hd", 0), head_slab(0, **{order[0][1]: shift(order[0][1], 2)}))
    project(0, 2)
    for by in (0, 1, 3):
        project(1, by)
    recv(("hd", 1), head_slab(1, **{order[1][1]: shift(order[1][1], 2)}))
    project(1, 2)

    attn_mine = attn.at[:, pl.ds(core * 2, 2)]
    send(("pair",), attn.at[:, pl.ds((1 - core) * 2, 2)], pair_in, partner)
    recv(("pair",), pair_in)
    far_out[...] = (attn_mine[1 - x_hi] + pair_in[1 - x_hi]).astype(BF16)
    send(("far",), far_out, far_in, neighbour("x", 2))
    loads[6].wait()
    near = (attn_mine[x_hi] + pair_in[x_hi]).reshape(LANES, FEATS)
    recv(("far",), far_in)
    residual = near + far_in[...].reshape(LANES, FEATS).astype(F32)
    residual = jnp.concatenate([residual, jnp.zeros((LANES, 32), F32)], axis=1).T[:FEATS]
    residual = residual + hidden[...].astype(F32)
    kept[...] = residual
    routed = residual.astype(BF16)

    for p, (first, rows, _) in enumerate(PARTS):
        rts[p][me["x"], me["y"], me["z"]] = routed[first : first + rows]

    def spot(p, **index):
        place = dict(me)
        place.update(index)
        return at(rts[p], **place)

    axes = [tuple(o) for _, _, o in PARTS]
    for p in range(3):
        a, b, c = axes[p]
        for k in (1, 3, 2):
            send(("ga", p, k), spot(p), spot(p), away(**{a: k}))
        for by in (1, 3):
            send(("gc", p, 0, by), spot(p), spot(p), neighbour(c, by))
    for p in range(3):
        a, b, c = axes[p]
        for m in (2, 1, 3):
            send(("gb", p, m), spot(p), spot(p), away(**{b: m}))
    for k in (1, 3, 2):
        for p in range(3):
            a, b, c = axes[p]
            block = spot(p, **{a: shift(a, k)})
            recv(("ga", p, 4 - k), block)
            for m in (2, 1, 3):
                send(("gb", p, m), block, block, away(**{b: m}))
            for by in (1, 3):
                send(("gc", p, 0, by), block, block, neighbour(c, by))
    for m in (1, 3, 2):
        for p in range(3):
            a, b, c = axes[p]
            slab = at(rts[p], **{b: shift(b, m), c: me[c]})
            recv(("gb", p, 4 - m), slab)
            for by in (1, 3):
                send(("gc", p, m, by), slab, slab, neighbour(c, by))

    def pass_on(m):
        for p in range(3):
            a, b, c = axes[p]
            for by in (1, 3):
                region = at(rts[p], **{b: shift(b, m), c: shift(c, -by)})
                recv(("gc", p, m, by), region)
                half_of = pl.ds(0, 2) if by == 1 else pl.ds(2, 2)
                passed = at(rts[p], **{a: half_of, b: shift(b, m), c: shift(c, -by)})
                send(("gd", p), passed, passed, neighbour(c, by))

    pass_on(0)

    totals = {"square": jnp.zeros((1, 256), F32), "first": True}

    def users_of(p, by):
        if p == 0:
            block = rts[0][:, :, shift("z", by)]
            low, high = block[0:2], block[2:4]
        elif p == 1:
            block = rts[1][:, shift("y", by)]
            low, high = block[0:2], block[2:4]
        else:
            plane = lax.rem(x_lo + by, 2)
            low, high = rts[2][plane], rts[2][plane + 2]
        return jnp.concatenate([low.reshape(-1, LANES), high.reshape(-1, LANES)], axis=1)

    def plane_of(p, by):
        if p == 2:
            return lax.rem(x_lo + by, 2)
        return shift(axes[p][2], by)

    def multiply(*planes):
        weights, rows = [], []
        for p, by in planes:
            block = users_of(p, by)
            wide = block.astype(F32)
            totals["square"] = totals["square"] + jnp.sum(wide * wide, axis=0, keepdims=True)
            weight = wts[p][plane_of(p, by)]
            weights.append(weight.reshape(1024, weight.shape[-1]))
            rows.append(block)
        if len(planes) > 1:
            weights, rows = [jnp.concatenate(weights, axis=1)], [jnp.concatenate(rows, axis=0)]
        product = jnp.dot(weights[0], rows[0], preferred_element_type=F32)
        if totals["first"]:
            gate_up[...] = product
        else:
            gate_up[...] += product
        totals["first"] = False

    multiply((0, 0), (1, 0))
    for m in (1, 3, 2):
        pass_on(m)
    multiply((0, 1), (0, 3))
    multiply((1, 1), (1, 3))
    multiply((2, 1),)
    for p in range(2):
        c = axes[p][2]
        recv(("gd", p), at(rts[p], **{c: shift(c, 2)}))
    multiply((0, 2), (1, 2))
    recv(("gd", 2), at(rts[2], x=shift("x", 2)))
    multiply((2, 0),)

    scale = lax.rsqrt(totals["square"] * (1.0 / (32 * FEATS)) + norm_eps)
    for slot in range(2):
        gate = gate_up[slot * 512 : slot * 512 + 256] * scale
        upward = gate_up[slot * 512 + 256 : slot * 512 + 512] * scale
        act[slot * 256 : slot * 256 + 256] = (gate / (1.0 + jnp.exp(-gate)) * upward).astype(BF16)

    outs = (o0, o1, o2)
    share = jnp.sum(jnp.where(ids_ref[...] == dev, weights_ref[...], 0.0), axis=0, keepdims=True)
    share = jnp.where(
        core == 0,
        jnp.concatenate([share[:, 0:128], share[:, 256:384]], axis=1),
        jnp.concatenate([share[:, 128:256], share[:, 384:512]], axis=1),
    )

    def down(p, by):
        first, rows, _ = PARTS[p]
        j = plane_of(p, by)
        weight = jnp.concatenate([weight_plane(downt.at[n], p, j) for n in range(2)], axis=1)
        product = jnp.dot(weight, act[...], preferred_element_type=F32)
        product = (product * share).astype(BF16)
        for h in range(2):
            lanes = product[:, h * LANES : (h + 1) * LANES]
            if p == 0:
                o0[2 * h : 2 * h + 2, :, j] = lanes.reshape(2, 4, rows, LANES)
            elif p == 1:
                o1[2 * h : 2 * h + 2, j] = lanes.reshape(2, 4, rows, LANES)
            else:
                o2[j + 2 * h] = lanes.reshape(4, 4, rows, LANES)

    def o_slab(p, by, m):
        a, b, c = axes[p]
        return at(outs[p], **{c: shift(c, by), b: shift(b, m)})

    for p in range(3):
        c = axes[p][2]
        down(p, 2 if p < 2 else 0)
        for m in (2, 0, 3, 1):
            by = 1 if m in (0, 1) else 3
            send(("s1", p, m), o_slab(p, 2, m), r1[p].at[m], neighbour(c, by))
    for p in range(3):
        c = axes[p][2]
        if p < 2:
            down(p, 1)
            down(p, 3)
        else:
            down(p, 1)
        for m in (2, 3):
            send(("s2", p, m), o_slab(p, 1, m), r2[p].at[m, 0], neighbour(c, 1))
        for m in (1, 0):
            send(("s2", p, m), o_slab(p, 3, m), r2[p].at[m, 1], neighbour(c, 3))
    for p in range(2):
        down(p, 0)

    def add_to(slab, other):
        slab[...] = (slab[...].astype(F32) + other[...].astype(F32)).astype(BF16)

    for m in (2, 1, 3, 0):
        for p in range(3):
            c = axes[p][2]
            recv(("s1", p, m), r1[p].at[m])
            by = 1 if m in (0, 1) else 3
            side = 0 if by == 1 else 1
            slab = o_slab(p, by, m)
            add_to(slab, r1[p].at[m])
            send(("s2", p, m), slab, r2[p].at[m, side], neighbour(c, by))

    for m in (2, 1, 3, 0):
        for p in range(3):
            a, b, c = axes[p]
            slab = o_slab(p, 0, m)
            recv(("s2", p, m), r2[p].at[m])
            slab[...] = (
                slab[...].astype(F32) + r2[p][m, 0].astype(F32) + r2[p][m, 1].astype(F32)
            ).astype(BF16)
            for k in (2, 1, 3, 0):
                if k or m:
                    send(("s5", p), slab.at[shift(a, k)], r5[p].at[4 * m + k - 1], away(**{a: k, b: m}))
    for p, (first, rows, _) in enumerate(PARTS):
        a = axes[p][0]
        total = kept[first : first + rows, :] + outs[p][me["x"], me["y"], me["z"]].astype(F32)
        recv(("s5", p), r5[p])
        for n in range(15):
            total = total + r5[p][n].astype(F32)
        out_ref[first : first + rows, :] = total.astype(BF16)
    drain()


def body(
    query_latent, query_rope, cache_latent, cache_rope, lengths, value_up, output_proj, hidden,
    norm_gain, route_ids, route_weights, gate_proj, up_proj, down_proj,
):
    def bf(*shape):
        return pltpu.VMEM(shape, BF16)

    def f32(*shape):
        return pltpu.VMEM(shape, F32)

    users, heads, latent = query_latent.shape
    history = cache_latent.shape[1]
    half = heads * LANES // 2
    rows = [r for _, r, _ in PARTS]
    hbm = pl.BlockSpec(memory_space=pl.ANY)
    vmem = pl.BlockSpec(memory_space=pltpu.VMEM)
    scratch = [
        bf(users, heads, latent), bf(users, heads * ROPE), bf(users, heads, ROPE),
        bf(2 * GROUP, history, latent), bf(2 * GROUP, ROPE, history), f32(latent // LANES, users * heads, LANES),
        bf(*value_up.shape),
        bf(2, 4, 4, 16, half), bf(2, 4, 4, 16, half), bf(FEATS, 2 * half), f32(2, 4, 4, 16, FEATS),
        f32(2, 2, 4, 16, FEATS), bf(2, 4, 16, FEATS), bf(2, 4, 16, FEATS), bf(FEATS, LANES),
        bf(2, 4, 4, FEATS, 256), bf(256, 32 * FEATS),
        f32(4, 1, 640), f32(4, 1, 640), f32(2, 1, 1024),
        bf(4, 2, 512, 640), bf(4, 2, 512, 640), bf(2, 2, 512, 1024), bf(2, 2, 4, 4, FEATS, 256),
        *[bf(4, 4, 4, r, LANES) for r in rows],
        f32(1024, 256), bf(512, 256),
        *[bf(4, 4, 4, r, LANES) for r in rows],
        *[bf(4, 4, r, LANES) for r in rows],
        *[bf(4, 2, 4, r, LANES) for r in rows],
        *[bf(15, r, LANES) for r in rows],
        f32(FEATS, LANES),
        pltpu.SemaphoreType.DMA((2, 2)),
        pltpu.SemaphoreType.DMA((9,)),
        pltpu.SemaphoreType.DMA((2, 6)),
        pltpu.SemaphoreType.DMA((36,)),
        pltpu.SemaphoreType.DMA((109,)),
    ]
    gate_proj = gate_proj.reshape(2, 4, 4, FEATS, 256)
    up_proj = up_proj.reshape(2, 4, 4, FEATS, 256)
    down_proj = down_proj[0]
    out, *_ = pl.pallas_call(
        layer_kernel,
        out_shape=(
            jax.ShapeDtypeStruct((FEATS, LANES), BF16),
            *[jax.ShapeDtypeStruct(a.shape, BF16) for a in (gate_proj, up_proj, down_proj)],
        ),
        in_specs=[
            hbm, hbm, hbm, hbm, pl.BlockSpec(memory_space=pltpu.SMEM), hbm,
            hbm, hbm, vmem, vmem, vmem, hbm, hbm, hbm,
        ],
        out_specs=(vmem, hbm, hbm, hbm),
        scratch_shapes=scratch,
        compiler_params=pltpu.CompilerParams(
            collective_id=0, has_side_effects=True, vmem_limit_bytes=63 * 1024 * 1024
        ),
        cost_estimate=pl.CostEstimate(flops=9 * 10**9, bytes_accessed=27 * 2**20, transcendentals=0),
    )(
        query_latent, query_rope, cache_latent, cache_rope, lengths, value_up,
        output_proj.T, hidden.T, norm_gain.reshape(56, LANES), route_ids.T, route_weights.T,
        gate_proj, up_proj, down_proj,
    )
    return out.T


def solution(mesh):
    return jax.shard_map(
        body,
        mesh=mesh,
        in_specs=(
            P("dev", "sec", None),
            P("dev", "sec"),
            P("dev", None, None),
            P("dev", None, None),
            P("dev"),
            P("sec", None, None),
            P("sec", "dev"),
            P(None, "dev"),
            P(),
            P(),
            P(),
            P("dev", None, "sec"),
            P("dev", None, "sec"),
            P("dev", "sec", None),
        ),
        out_specs=P("sec", "dev"),
        check_vma=False,
    )
```

```python
import functools

import jax
import jax.numpy as jnp
from jax import lax
from jax.experimental import pallas as pl
from jax.experimental.pallas import tpu as pltpu
from jax.sharding import PartitionSpec as P

ROPE = 64
NOPE = 128
norm_eps = 1e-06
MESH = pl.DeviceIdType.MESH
F32 = jnp.float32
BF16 = jnp.bfloat16

PARTS = ((0, 80, "xyz"), (80, 80, "zxy"), (160, 64, "yzx"))
FEATS = 224
LANES = 128
LATE = 640
GROUP = 4


def weight_plane(ref, p, j):
    first, rows, _ = PARTS[p]
    if p == 0:
        block = ref[:, :, j, first : first + rows, :]
    elif p == 1:
        block = ref[:, j, :, first : first + rows, :]
    else:
        block = ref[j, :, :, first : first + rows, :]
    return block.reshape(-1, block.shape[-1])


def at(ref, **index):
    return ref.at[tuple(index.get(axis, slice(None)) for axis in "xyz")]


def get(ref, **index):
    return ref[tuple(index.get(axis, slice(None)) for axis in "xyz")]


def layer_kernel(
    query_hbm, rope_hbm, cache_hbm, keys_hbm, lengths_ref, value_up_hbm,
    out_proj_hbm, hidden_hbm, gain_ref, ids_ref, weights_ref, gate_hbm, up_hbm, down_hbm,
    out_ref, gate_far, up_far, down_far,
    query, rope, positional, cache, keys, context, value_up,
    heads0, heads1, out_proj, attn, pair_in, far_in, far_out, hidden,
    weight_in, down_in, gain0, gain1, gain2, wt0, wt1, wt2, downt,
    rt0, rt1, rt2, gate_up, act, o0, o1, o2,
    r1_0, r1_1, r1_2, r2_0, r2_1, r2_2, r5_0, r5_1, r5_2,
    kept, cache_sem, local_sem, stage_sem, send_sem, recv_sem,
):
    sec = lax.axis_index("sec")
    dev = lax.axis_index("dev")
    x_hi, core = lax.div(sec, 2), lax.rem(sec, 2)
    x_lo = lax.div(dev, 16)
    me = {
        "x": x_hi * 2 + x_lo,
        "y": lax.rem(lax.div(dev, 4), 4),
        "z": lax.rem(dev, 4),
    }

    def device(x, y, z, c):
        return (lax.div(x, 2) * 2 + c, lax.rem(x, 2) * 16 + y * 4 + z)

    shifted = {(axis, by): lax.rem(me[axis] + by, 4) for axis in "xyz" for by in (1, 2, 3)}

    def shift(axis, by):
        return me[axis] if by % 4 == 0 else shifted[axis, by % 4]

    ids = {}

    def away(**by):
        offset = tuple(by.get(axis, 0) for axis in "xyz")
        if offset not in ids:
            ids[offset] = device(*[shift(axis, n) for axis, n in zip("xyz", offset)], core)
        return ids[offset]

    def neighbour(axis, by):
        return away(**{axis: by})

    partner = device(me["x"], me["y"], me["z"], 1 - core)
    x_lo_partner = (sec, (1 - x_lo) * 16 + me["y"] * 4 + me["z"])

    tags = {}
    kinds = {}
    sent = []

    def number(tag):
        return tags.setdefault(tag, len(tags))

    def send(tag, src, dst, to):
        i = number(tag)
        kind = tag[: 3 if tag[0] in ("hb", "hf", "hc", "hd") else 2]
        copy = pltpu.make_async_remote_copy(
            src_ref=src, dst_ref=dst, send_sem=send_sem.at[kinds.setdefault(kind, len(kinds))],
            recv_sem=recv_sem.at[i], device_id=to, device_id_type=MESH,
        )
        copy.start()
        sent.append((kind, copy))

    def drain():
        blocks = dict(hb=2, hc=8, hd=4, hl=16, ga=3, gb=12, gc=32, gd=16, s1=16, s2=32, s5=15)
        alone = {kind: copy for kind, copy in sent}
        for kind, i in kinds.items():
            if kind[0] not in blocks:
                alone[kind].wait_send()
                continue
            p = kind[1]
            held = heads[p] if kind[0][0] == "h" else rts[p]
            views = {
                2: lambda: held.at[:, 0, 0], 3: lambda: held.at[0, 0, 0:3], 4: lambda: held.at[0, 0],
                8: lambda: held.at[0, 0:2], 12: lambda: held.at[0, 0:3], 15: lambda: r5[p],
                16: lambda: held.at[0], 32: lambda: held.at[0:2],
            }
            view = views[blocks[kind[0]]]()
            if kind[0] == "hl":
                view = late(view)
            elif kind[0][0] == "h" and kind[2] == 1:
                view = early(view)
            pltpu.make_async_remote_copy(
                src_ref=view, dst_ref=view, send_sem=send_sem.at[i], recv_sem=recv_sem.at[0],
                device_id=partner, device_id_type=MESH,
            ).wait_send()

    def recv(tag, region):
        i = number(tag)
        pltpu.make_async_remote_copy(
            src_ref=region, dst_ref=region, send_sem=send_sem.at[0], recv_sem=recv_sem.at[i],
            device_id=partner, device_id_type=MESH,
        ).wait_recv()


    offsets = {}
    for first, second in ("xy", "zx", "yz"):
        for m in range(4):
            for k in range(4):
                offset = {"x": 0, "y": 0, "z": 0, first: k, second: m}
                if k or m:
                    offsets[tuple(offset.values())] = offset
    around = [away(**offset) for offset in offsets.values()] + [partner]
    barrier = pltpu.get_barrier_semaphore()
    for other in around:
        pl.semaphore_signal(barrier, inc=1, device_id=other, device_id_type=MESH)

    heads = (heads0, heads1)
    rts = (rt0, rt1, rt2)
    r1, r2, r5 = (r1_0, r1_1, r1_2), (r2_0, r2_1, r2_2), (r5_0, r5_1, r5_2)
    half = heads0.shape[-1]
    own_heads = [at(h, x=x_lo, y=me["y"], z=me["z"]) for h in heads]
    my_hidden = hidden_hbm.at[:, pl.ds(pl.multiple_of(sec * LANES, LANES), LANES)]

    def user_loads(step):
        slot = lax.rem(step, 2) if not isinstance(step, int) else step % 2
        users, place = pl.ds(step * GROUP, GROUP), pl.ds(slot * GROUP, GROUP)
        return (
            pltpu.make_async_copy(cache_hbm.at[users], cache.at[place], cache_sem.at[slot, 0]),
            pltpu.make_async_copy(keys_hbm.at[users], keys.at[place], cache_sem.at[slot, 1]),
        )

    def stage_up(source, n):
        copies = []
        for p, (first, rows, _) in enumerate(PARTS):
            for q in range(2):
                copies.append(
                    pltpu.make_async_copy(
                        source.at[:, :, :, pl.ds(first, rows), pl.ds(q * LANES, LANES)],
                        (o0, o1, o2)[p].at[pl.ds(2 * q, 2)],
                        stage_sem.at[n, 2 * p + q],
                    )
                )
        return copies

    loads = [
        pltpu.make_async_copy(rope_hbm, rope, local_sem.at[0]),
        pltpu.make_async_copy(query_hbm, query, local_sem.at[1]),
        pltpu.make_async_copy(value_up_hbm, value_up, local_sem.at[2]),
        pltpu.make_async_copy(gate_hbm, weight_in, local_sem.at[3]),
        pltpu.make_async_copy(out_proj_hbm, out_proj, local_sem.at[4]),
        pltpu.make_async_copy(down_hbm, down_in, local_sem.at[5]),
        pltpu.make_async_copy(my_hidden, hidden, local_sem.at[6]),
        pltpu.make_async_copy(gate_far, weight_in, local_sem.at[7]),
        pltpu.make_async_copy(down_far, down_in, local_sem.at[8]),
    ]
    up_loads = stage_up(up_hbm, 0), stage_up(up_far, 1)
    for copy in (loads[0], loads[1], *user_loads(0), *user_loads(1)):
        copy.start()
    loads[2].start()

    for p, gain in enumerate((gain0, gain1, gain2)):
        first, rows, _ = PARTS[p]
        width = gain.shape[-1]
        block = lax.broadcasted_iota(jnp.int32, (LANES, width), 1) // rows
        offset = lax.rem(lax.broadcasted_iota(jnp.int32, (LANES, width), 1), rows) + first
        lane = lax.broadcasted_iota(jnp.int32, (LANES, width), 0)
        for j in range(gain.shape[0]):
            if p == 0:
                owner = block * 4 + j
            elif p == 1:
                owner = (block // 4) * 16 + j * 4 + lax.rem(block, 4)
            else:
                owner = j * 16 + block
            place = owner * FEATS + offset
            spread = jnp.dot(
                gain_ref[...], (lax.rem(place, LANES) == lane).astype(F32),
                preferred_element_type=F32, precision=lax.Precision.HIGHEST,
            )
            held = (place // LANES)[:56] == lane[:56]
            gain[j] = jnp.sum(jnp.where(held, spread, 0.0), axis=0, keepdims=True)

    users_here, heads_here = query.shape[0], query.shape[1]
    loads[0].wait()
    wide = heads_here * ROPE
    owner = lax.broadcasted_iota(jnp.int32, (heads_here, wide), 1) // ROPE
    mask = owner == lax.broadcasted_iota(jnp.int32, (heads_here, wide), 0)
    fold = lax.rem(lax.broadcasted_iota(jnp.int32, (wide, ROPE), 0), ROPE)
    fold = (fold == lax.broadcasted_iota(jnp.int32, (wide, ROPE), 1)).astype(F32).astype(BF16)
    for r in range(users_here):
        row = jnp.broadcast_to(rope[r : r + 1, :].astype(F32), (heads_here, wide))
        row = jnp.where(mask, row, 0.0).astype(BF16)
        positional[r] = jnp.dot(row, fold, preferred_element_type=F32).astype(BF16)
    loads[1].wait()
    history = cache.shape[1]
    moment = lax.broadcasted_iota(jnp.int32, (heads_here, history), 1)

    def attend(step, carry):
        slot = lax.rem(step, 2)
        for copy in user_loads(step):
            copy.wait()
        weights = []
        for n in range(GROUP):
            r = step * GROUP + n
            place = slot * GROUP + n
            scores = lax.dot_general(
                query[r], cache[place], (((1,), (1,)), ((), ())), preferred_element_type=F32
            )
            scores += jnp.dot(positional[r], keys[place], preferred_element_type=F32)
            scores = scores * (NOPE + ROPE) ** (-0.5)
            scores = jnp.where(moment < lengths_ref[r], scores, -1e30)
            exponent = jnp.exp(scores - jnp.max(scores, axis=-1, keepdims=True))
            weights.append((exponent / jnp.sum(exponent, axis=-1, keepdims=True)).astype(BF16))
        for n in range(GROUP):
            r = step * GROUP + n
            value = jnp.dot(weights[n], cache[slot * GROUP + n], preferred_element_type=F32)
            value = value.astype(BF16).astype(F32)
            rows = pl.ds(pl.multiple_of(r * heads_here, heads_here), heads_here)
            for t in range(context.shape[0]):
                context[t, rows, :] = value[:, t * LANES : (t + 1) * LANES]

        @pl.when(step < users_here // GROUP - 2)
        def _():
            for copy in user_loads(step + 2):
                copy.start()

        return carry

    lax.fori_loop(0, 1, attend, 0)
    pl.semaphore_wait(barrier, len(around))
    send(("wg",), gate_hbm, gate_far, partner)
    send(("wu",), up_hbm, up_far, partner)
    send(("wd",), down_hbm, down_far, partner)
    lax.fori_loop(1, users_here // GROUP, attend, 0)
    for copy in (loads[3], *up_loads[0], *loads[4:7]):
        copy.start()
    loads[2].wait()

    def head_value(h):
        tiles = [context[t, pl.ds(h, users_here, stride=heads_here), :] for t in range(context.shape[0])]
        rows = jnp.concatenate(tiles, axis=1).astype(BF16)
        value = jnp.dot(rows, value_up[h], preferred_element_type=F32)
        return value.astype(BF16)

    order = (("y", "z"), ("z", "y"))

    def early(ref):
        return ref.at[(slice(None),) * (len(ref.shape) - 1) + (pl.ds(0, half - LATE),)]

    def late(ref):
        return ref.at[(slice(None),) * (len(ref.shape) - 1) + (pl.ds(half - LATE, LATE),)]

    def head_block(p, k, **index):
        place = {"x": lax.rem(x_lo + k, 2), "y": me["y"], "z": me["z"]}
        place.update(index)
        return early(at(heads[p], **place)) if k else at(heads[p], **place)

    def head_slab(p, **index):
        return at(heads[p], **index)

    for p in range(2):
        for h in range(heads_here // 2):
            heads[p][x_lo, me["y"], me["z"], :, h * 128 : h * 128 + 128] = head_value(p * (heads_here // 2) + h)
        send(("hx", p), early(own_heads[p]), early(own_heads[p]), x_lo_partner)
        b, c = order[p]
        for by in (1, 3):
            send(("hb", p, 0, by), own_heads[p], own_heads[p], neighbour(b, by))
        for by in (1, 3):
            send(("hc", p, 0, 0, by), own_heads[p], own_heads[p], neighbour(c, by))

    wts = (wt0, wt1, wt2)
    gains = (gain0, gain1, gain2)

    def gate_task(slot, p):
        if p == 0:
            loads[7 if slot else 3].wait()

        def step(j, carry):
            block = weight_plane(weight_in, p, j).T.astype(F32) * gains[p][j]
            wts[p][j, slot, 0:256, :] = block.astype(BF16)
            return carry

        lax.fori_loop(0, wts[p].shape[0], step, 0)

    def up_task(slot, p):
        if p == 0:
            for copy in up_loads[slot]:
                copy.wait()

        def step(j, carry):
            for q in range(2):
                if p == 0:
                    block = o0[2 * q : 2 * q + 2, :, j]
                elif p == 1:
                    block = o1[2 * q : 2 * q + 2, j]
                else:
                    block = o2[2 * q + j]
                block = block.reshape(-1, LANES).T.astype(F32) * gains[p][j]
                wts[p][j, slot, 256 + q * LANES : 256 + (q + 1) * LANES, :] = block.astype(BF16)
            return carry

        lax.fori_loop(0, wts[p].shape[0], step, 0)

    def down_task(slot, half_of):
        if half_of == 0:
            loads[8 if slot else 5].wait()

        def step(j, carry):
            block = down_in[:, pl.ds(pl.multiple_of(j * 896, 896), 896)].T
            downt[slot, j // 4, lax.rem(j, 4)] = block.reshape(4, FEATS, 256)
            return carry

        lax.fori_loop(4 * half_of, 4 * half_of + 4, step, 0)

    tasks = []
    for slot in range(2):
        tasks += [functools.partial(gate_task, slot, p) for p in range(3)]
        tasks += [functools.partial(up_task, slot, p) for p in range(3)]
        tasks += [functools.partial(down_task, slot, n) for n in range(2)]

    def fetch_partner():
        recv(("wg",), gate_far)
        loads[7].start()
        recv(("wu",), up_far)
        for copy in up_loads[1]:
            copy.start()
        recv(("wd",), down_far)
        loads[8].start()

    def work(count=1):
        for task in tasks[:count]:
            task()
        del tasks[:count]

    work(4)

    def onward(p, m, k):
        b, c = order[p]
        block = head_block(p, k, **{b: shift(b, m)})
        for by in (1, 3):
            send(("hc", p, k, m, by), block, block, neighbour(c, by))

    def from_sides(k):
        for p in range(2):
            b, c = order[p]
            for m, by in ((3, 1), (1, 3)) if k == 0 else ((1, 3), (3, 1)):
                block = head_block(p, k, **{b: shift(b, m)})
                recv(("hb", p, k, by), block)
                if (by == 1) == (k == 0):
                    send(("hf", p, k), block, block, neighbour(b, by))
        for p in range(2):
            for m in (3, 1):
                onward(p, m, k)

    def from_opposite(k):
        for p in range(2):
            b, c = order[p]
            recv(("hf", p, k), head_block(p, k, **{b: shift(b, 2)}))
            onward(p, 2, k)

    from_sides(0)
    work(2)
    for p in range(2):
        b, c = order[p]
        other = head_block(p, 1)
        recv(("hx", p), other)
        for by in (1, 3):
            send(("hb", p, 1, by), other, other, neighbour(b, by))
    for p in range(2):
        onward(p, 0, 1)
    from_opposite(0)
    work(2)
    from_sides(1)
    from_opposite(1)
    fetch_partner()

    def project(p, by, first=False):
        c = order[p][1]
        j = shift(c, by)
        rows = get(heads[p], **{c: j}).reshape(-1, half)
        product = lax.dot_general(
            rows, out_proj[:, p * half : (p + 1) * half], (((1,), (1,)), ((), ())), preferred_element_type=F32
        )
        product = product.reshape(2, 4, 16, FEATS)
        if c == "z":
            attn[:, :, j] = product
        else:
            attn[:, j] += product

    def plane_late(p, by, k):
        c = order[p][1]
        return late(at(heads[p], **{"x": lax.rem(x_lo + k, 2), c: shift(c, by)}))

    def cross(*planes):
        for by in planes:
            for p in range(2):
                mine = plane_late(p, by, 0)
                send(("hl", p, by), mine, mine, x_lo_partner)

    def take(m, k):
        for p in range(2):
            b, c = order[p]
            for by in (1, 3):
                block = head_block(p, k, **{b: shift(b, m), c: shift(c, -by)})
                recv(("hc", p, k, m, by), block)
                if (by == 1) == (p == k):
                    send(("hd", p, k), block, block, neighbour(c, by))

    def opposite(p, k):
        c = order[p][1]
        block = at(heads[p], **{"x": lax.rem(x_lo + k, 2), c: shift(c, 2)})
        recv(("hd", p, k), early(block) if k else block)

    def finished(p, by):
        recv(("hl", p, by), plane_late(p, by, 1))
        project(p, by)

    cross(0)
    loads[4].wait()
    for m, k in ((0, 0), (3, 0), (1, 0), (0, 1)):
        take(m, k)
        work(1)
    take(2, 0)
    cross(1, 3)
    work(2)
    take(1, 1)
    take(3, 1)
    for p in range(2):
        opposite(p, 0)
    cross(2)
    take(2, 1)
    work(len(tasks))
    for by in (0, 1, 3):
        finished(0, by)
    opposite(0, 1)
    finished(0, 2)
    for by in (0, 1, 3):
        finished(1, by)
    opposite(1, 1)
    finished(1, 2)

    attn_mine = attn.at[:, pl.ds(core * 2, 2)]
    send(("pair",), attn.at[:, pl.ds((1 - core) * 2, 2)], pair_in, partner)
    recv(("pair",), pair_in)
    far_out[...] = (attn_mine[1 - x_hi] + pair_in[1 - x_hi]).astype(BF16)
    send(("far",), far_out, far_in, neighbour("x", 2))
    loads[6].wait()
    near = (attn_mine[x_hi] + pair_in[x_hi]).reshape(LANES, FEATS)
    recv(("far",), far_in)
    residual = near + far_in[...].reshape(LANES, FEATS).astype(F32)
    residual = jnp.concatenate([residual, jnp.zeros((LANES, 32), F32)], axis=1).T[:FEATS]
    residual = residual + hidden[...].astype(F32)
    kept[...] = residual
    routed = residual.astype(BF16)

    for p, (first, rows, _) in enumerate(PARTS):
        rts[p][me["x"], me["y"], me["z"]] = routed[first : first + rows]

    def spot(p, **index):
        place = dict(me)
        place.update(index)
        return at(rts[p], **place)

    axes = [tuple(o) for _, _, o in PARTS]
    for p in range(3):
        a, b, c = axes[p]
        for k in (1, 3, 2):
            send(("ga", p, k), spot(p), spot(p), away(**{a: k}))
        for by in (1, 3):
            send(("gc", p, 0, by), spot(p), spot(p), neighbour(c, by))
    for p in range(3):
        a, b, c = axes[p]
        for m in (2, 1, 3):
            send(("gb", p, m), spot(p), spot(p), away(**{b: m}))
    for k in (1, 3, 2):
        for p in range(3):
            a, b, c = axes[p]
            block = spot(p, **{a: shift(a, k)})
            recv(("ga", p, 4 - k), block)
            for m in (2, 1, 3):
                send(("gb", p, m), block, block, away(**{b: m}))
            for by in (1, 3):
                send(("gc", p, 0, by), block, block, neighbour(c, by))
    for m in (1, 3, 2):
        for p in range(3):
            a, b, c = axes[p]
            slab = at(rts[p], **{b: shift(b, m), c: me[c]})
            recv(("gb", p, 4 - m), slab)
            for by in (1, 3):
                send(("gc", p, m, by), slab, slab, neighbour(c, by))

    def pass_on(m):
        for p in range(3):
            a, b, c = axes[p]
            for by in (1, 3):
                region = at(rts[p], **{b: shift(b, m), c: shift(c, -by)})
                recv(("gc", p, m, by), region)
                half_of = pl.ds(0, 2) if by == 1 else pl.ds(2, 2)
                passed = at(rts[p], **{a: half_of, b: shift(b, m), c: shift(c, -by)})
                send(("gd", p), passed, passed, neighbour(c, by))

    pass_on(0)

    totals = {"square": jnp.zeros((1, 256), F32), "first": True}

    def users_of(p, by):
        if p == 0:
            block = rts[0][:, :, shift("z", by)]
            low, high = block[0:2], block[2:4]
        elif p == 1:
            block = rts[1][:, shift("y", by)]
            low, high = block[0:2], block[2:4]
        else:
            plane = lax.rem(x_lo + by, 2)
            low, high = rts[2][plane], rts[2][plane + 2]
        return jnp.concatenate([low.reshape(-1, LANES), high.reshape(-1, LANES)], axis=1)

    def plane_of(p, by):
        if p == 2:
            return lax.rem(x_lo + by, 2)
        return shift(axes[p][2], by)

    def multiply(*planes):
        weights, rows = [], []
        for p, by in planes:
            block = users_of(p, by)
            wide = block.astype(F32)
            totals["square"] = totals["square"] + jnp.sum(wide * wide, axis=0, keepdims=True)
            weight = wts[p][plane_of(p, by)]
            weights.append(weight.reshape(1024, weight.shape[-1]))
            rows.append(block)
        if len(planes) > 1:
            weights, rows = [jnp.concatenate(weights, axis=1)], [jnp.concatenate(rows, axis=0)]
        product = jnp.dot(weights[0], rows[0], preferred_element_type=F32)
        if totals["first"]:
            gate_up[...] = product
        else:
            gate_up[...] += product
        totals["first"] = False

    multiply((0, 0), (1, 0))
    for m in (1, 3, 2):
        pass_on(m)
    multiply((0, 1), (0, 3))
    multiply((1, 1), (1, 3))
    multiply((2, 1),)
    for p in range(2):
        c = axes[p][2]
        recv(("gd", p), at(rts[p], **{c: shift(c, 2)}))
    multiply((0, 2), (1, 2))
    recv(("gd", 2), at(rts[2], x=shift("x", 2)))
    multiply((2, 0),)

    scale = lax.rsqrt(totals["square"] * (1.0 / (32 * FEATS)) + norm_eps)
    for slot in range(2):
        gate = gate_up[slot * 512 : slot * 512 + 256] * scale
        upward = gate_up[slot * 512 + 256 : slot * 512 + 512] * scale
        act[slot * 256 : slot * 256 + 256] = (gate / (1.0 + jnp.exp(-gate)) * upward).astype(BF16)

    outs = (o0, o1, o2)
    share = jnp.sum(jnp.where(ids_ref[...] == dev, weights_ref[...], 0.0), axis=0, keepdims=True)
    share = jnp.where(
        core == 0,
        jnp.concatenate([share[:, 0:128], share[:, 256:384]], axis=1),
        jnp.concatenate([share[:, 128:256], share[:, 384:512]], axis=1),
    )

    def down(p, by):
        first, rows, _ = PARTS[p]
        j = plane_of(p, by)
        weight = jnp.concatenate([weight_plane(downt.at[n], p, j) for n in range(2)], axis=1)
        product = jnp.dot(weight, act[...], preferred_element_type=F32)
        product = (product * share).astype(BF16)
        for h in range(2):
            lanes = product[:, h * LANES : (h + 1) * LANES]
            if p == 0:
                o0[2 * h : 2 * h + 2, :, j] = lanes.reshape(2, 4, rows, LANES)
            elif p == 1:
                o1[2 * h : 2 * h + 2, j] = lanes.reshape(2, 4, rows, LANES)
            else:
                o2[j + 2 * h] = lanes.reshape(4, 4, rows, LANES)

    def o_slab(p, by, m):
        a, b, c = axes[p]
        return at(outs[p], **{c: shift(c, by), b: shift(b, m)})

    for p in range(3):
        c = axes[p][2]
        down(p, 2 if p < 2 else 0)
        for m in (2, 0, 3, 1):
            by = 1 if m in (0, 1) else 3
            send(("s1", p, m), o_slab(p, 2, m), r1[p].at[m], neighbour(c, by))
    for p in range(3):
        c = axes[p][2]
        if p < 2:
            down(p, 1)
            down(p, 3)
        else:
            down(p, 1)
        for m in (2, 3):
            send(("s2", p, m), o_slab(p, 1, m), r2[p].at[m, 0], neighbour(c, 1))
        for m in (1, 0):
            send(("s2", p, m), o_slab(p, 3, m), r2[p].at[m, 1], neighbour(c, 3))
    for p in range(2):
        down(p, 0)

    def add_to(slab, other):
        slab[...] = (slab[...].astype(F32) + other[...].astype(F32)).astype(BF16)

    for m in (2, 1, 3, 0):
        for p in range(3):
            c = axes[p][2]
            recv(("s1", p, m), r1[p].at[m])
            by = 1 if m in (0, 1) else 3
            side = 0 if by == 1 else 1
            slab = o_slab(p, by, m)
            add_to(slab, r1[p].at[m])
            send(("s2", p, m), slab, r2[p].at[m, side], neighbour(c, by))

    for m in (2, 1, 3, 0):
        for p in range(3):
            a, b, c = axes[p]
            slab = o_slab(p, 0, m)
            recv(("s2", p, m), r2[p].at[m])
            slab[...] = (
                slab[...].astype(F32) + r2[p][m, 0].astype(F32) + r2[p][m, 1].astype(F32)
            ).astype(BF16)
            for k in (2, 1, 3, 0):
                if k or m:
                    send(("s5", p), slab.at[shift(a, k)], r5[p].at[4 * m + k - 1], away(**{a: k, b: m}))
    for p, (first, rows, _) in enumerate(PARTS):
        a = axes[p][0]
        total = kept[first : first + rows, :] + outs[p][me["x"], me["y"], me["z"]].astype(F32)
        recv(("s5", p), r5[p])
        for n in range(15):
            total = total + r5[p][n].astype(F32)
        out_ref[first : first + rows, :] = total.astype(BF16)
    drain()


def body(
    query_latent, query_rope, cache_latent, cache_rope, lengths, value_up, output_proj, hidden,
    norm_gain, route_ids, route_weights, gate_proj, up_proj, down_proj,
):
    def bf(*shape):
        return pltpu.VMEM(shape, BF16)

    def f32(*shape):
        return pltpu.VMEM(shape, F32)

    users, heads, latent = query_latent.shape
    history = cache_latent.shape[1]
    half = heads * LANES // 2
    rows = [r for _, r, _ in PARTS]
    hbm = pl.BlockSpec(memory_space=pl.ANY)
    vmem = pl.BlockSpec(memory_space=pltpu.VMEM)
    scratch = [
        bf(users, heads, latent), bf(users, heads * ROPE), bf(users, heads, ROPE),
        bf(2 * GROUP, history, latent), bf(2 * GROUP, ROPE, history), f32(latent // LANES, users * heads, LANES),
        bf(*value_up.shape),
        bf(2, 4, 4, 16, half), bf(2, 4, 4, 16, half), bf(FEATS, 2 * half), f32(2, 4, 4, 16, FEATS),
        f32(2, 2, 4, 16, FEATS), bf(2, 4, 16, FEATS), bf(2, 4, 16, FEATS), bf(FEATS, LANES),
        bf(2, 4, 4, FEATS, 256), bf(256, 32 * FEATS),
        f32(4, 1, 640), f32(4, 1, 640), f32(2, 1, 1024),
        bf(4, 2, 512, 640), bf(4, 2, 512, 640), bf(2, 2, 512, 1024), bf(2, 2, 4, 4, FEATS, 256),
        *[bf(4, 4, 4, r, LANES) for r in rows],
        f32(1024, 256), bf(512, 256),
        *[bf(4, 4, 4, r, LANES) for r in rows],
        *[bf(4, 4, r, LANES) for r in rows],
        *[bf(4, 2, 4, r, LANES) for r in rows],
        *[bf(15, r, LANES) for r in rows],
        f32(FEATS, LANES),
        pltpu.SemaphoreType.DMA((2, 2)),
        pltpu.SemaphoreType.DMA((9,)),
        pltpu.SemaphoreType.DMA((2, 6)),
        pltpu.SemaphoreType.DMA((46,)),
        pltpu.SemaphoreType.DMA((135,)),
    ]
    gate_proj = gate_proj.reshape(2, 4, 4, FEATS, 256)
    up_proj = up_proj.reshape(2, 4, 4, FEATS, 256)
    down_proj = down_proj[0]
    out, *_ = pl.pallas_call(
        layer_kernel,
        out_shape=(
            jax.ShapeDtypeStruct((FEATS, LANES), BF16),
            *[jax.ShapeDtypeStruct(a.shape, BF16) for a in (gate_proj, up_proj, down_proj)],
        ),
        in_specs=[
            hbm, hbm, hbm, hbm, pl.BlockSpec(memory_space=pltpu.SMEM), hbm,
            hbm, hbm, vmem, vmem, vmem, hbm, hbm, hbm,
        ],
        out_specs=(vmem, hbm, hbm, hbm),
        scratch_shapes=scratch,
        compiler_params=pltpu.CompilerParams(
            collective_id=0, has_side_effects=True, vmem_limit_bytes=63 * 1024 * 1024
        ),
        cost_estimate=pl.CostEstimate(flops=9 * 10**9, bytes_accessed=27 * 2**20, transcendentals=0),
    )(
        query_latent, query_rope, cache_latent, cache_rope, lengths, value_up,
        output_proj.T, hidden.T, norm_gain.reshape(56, LANES), route_ids.T, route_weights.T,
        gate_proj, up_proj, down_proj,
    )
    return out.T


def solution(mesh):
    return jax.shard_map(
        body,
        mesh=mesh,
        in_specs=(
            P("dev", "sec", None),
            P("dev", "sec"),
            P("dev", None, None),
            P("dev", None, None),
            P("dev"),
            P("sec", None, None),
            P("sec", "dev"),
            P(None, "dev"),
            P(),
            P(),
            P(),
            P("dev", None, "sec"),
            P("dev", None, "sec"),
            P("dev", "sec", None),
        ),
        out_specs=P("sec", "dev"),
        check_vma=False,
    )
```

```python
import functools

import jax
import jax.numpy as jnp
from jax import lax
from jax.experimental import pallas as pl
from jax.experimental.pallas import tpu as pltpu
from jax.sharding import PartitionSpec as P

ROPE = 64
NOPE = 128
norm_eps = 1e-06
MESH = pl.DeviceIdType.MESH
F32 = jnp.float32
BF16 = jnp.bfloat16

PARTS = ((0, 80, "xyz"), (80, 80, "zxy"), (160, 64, "yzx"))
FEATS = 224
LANES = 128
GROUP = 4


def weight_plane(ref, p, j):
    first, rows, _ = PARTS[p]
    if p == 0:
        block = ref[:, :, j, first : first + rows, :]
    elif p == 1:
        block = ref[:, j, :, first : first + rows, :]
    else:
        block = ref[j, :, :, first : first + rows, :]
    return block.reshape(-1, block.shape[-1])


def at(ref, **index):
    return ref.at[tuple(index.get(axis, slice(None)) for axis in "xyz")]


def get(ref, **index):
    return ref[tuple(index.get(axis, slice(None)) for axis in "xyz")]


def layer_kernel(
    query_hbm, rope_hbm, cache_hbm, keys_hbm, lengths_ref, value_up_hbm,
    out_proj_hbm, hidden_hbm, gain_ref, ids_ref, weights_ref, gate_hbm, up_hbm, down_hbm,
    out_ref, gate_far, up_far, down_far,
    query, rope, positional, cache, keys, context, value_up,
    heads0, heads1, out_proj, attn, pair_in, far_in, far_out, hidden,
    weight_in, down_in, gain0, gain1, gain2, wt0, wt1, wt2, downt,
    rt0, rt1, rt2, gate_up, act, o0, o1, o2,
    r1_0, r1_1, r1_2, r2_0, r2_1, r2_2, r5_0, r5_1, r5_2,
    kept, cache_sem, local_sem, stage_sem, send_sem, recv_sem,
):
    sec = lax.axis_index("sec")
    dev = lax.axis_index("dev")
    x_hi, core = lax.div(sec, 2), lax.rem(sec, 2)
    x_lo = lax.div(dev, 16)
    me = {
        "x": x_hi * 2 + x_lo,
        "y": lax.rem(lax.div(dev, 4), 4),
        "z": lax.rem(dev, 4),
    }

    def device(x, y, z, c):
        return (lax.div(x, 2) * 2 + c, lax.rem(x, 2) * 16 + y * 4 + z)

    shifted = {(axis, by): lax.rem(me[axis] + by, 4) for axis in "xyz" for by in (1, 2, 3)}

    def shift(axis, by):
        return me[axis] if by % 4 == 0 else shifted[axis, by % 4]

    ids = {}

    def away(**by):
        offset = tuple(by.get(axis, 0) for axis in "xyz")
        if offset not in ids:
            ids[offset] = device(*[shift(axis, n) for axis, n in zip("xyz", offset)], core)
        return ids[offset]

    def neighbour(axis, by):
        return away(**{axis: by})

    partner = device(me["x"], me["y"], me["z"], 1 - core)
    x_lo_partner = (sec, (1 - x_lo) * 16 + me["y"] * 4 + me["z"])

    tags = {}
    kinds = {}
    sent = []

    def number(tag):
        return tags.setdefault(tag, len(tags))

    def send(tag, src, dst, to):
        i = number(tag)
        kind = tag[:2]
        copy = pltpu.make_async_remote_copy(
            src_ref=src, dst_ref=dst, send_sem=send_sem.at[kinds.setdefault(kind, len(kinds))],
            recv_sem=recv_sem.at[i], device_id=to, device_id_type=MESH,
        )
        copy.start()
        sent.append((kind, copy))

    def drain():
        blocks = dict(hb=4, hf=2, hc=16, hd=8, ga=3, gb=12, gc=32, gd=16, s1=16, s2=32, s5=15)
        alone = {kind: copy for kind, copy in sent}
        for kind, i in kinds.items():
            if kind[0] not in blocks:
                alone[kind].wait_send()
                continue
            p = kind[1]
            held = heads[p] if kind[0][0] == "h" else rts[p]
            views = {
                2: lambda: held.at[:, 0, 0], 3: lambda: held.at[0, 0, 0:3], 4: lambda: held.at[0, 0],
                8: lambda: held.at[0, 0:2], 12: lambda: held.at[0, 0:3], 15: lambda: r5[p],
                16: lambda: held.at[0], 32: lambda: held.at[0:2],
            }
            view = views[blocks[kind[0]]]()
            pltpu.make_async_remote_copy(
                src_ref=view, dst_ref=view, send_sem=send_sem.at[i], recv_sem=recv_sem.at[0],
                device_id=partner, device_id_type=MESH,
            ).wait_send()

    def recv(tag, region):
        i = number(tag)
        pltpu.make_async_remote_copy(
            src_ref=region, dst_ref=region, send_sem=send_sem.at[0], recv_sem=recv_sem.at[i],
            device_id=partner, device_id_type=MESH,
        ).wait_recv()


    offsets = {}
    for first, second in ("xy", "zx", "yz"):
        for m in range(4):
            for k in range(4):
                offset = {"x": 0, "y": 0, "z": 0, first: k, second: m}
                if k or m:
                    offsets[tuple(offset.values())] = offset
    around = [away(**offset) for offset in offsets.values()] + [partner]
    barrier = pltpu.get_barrier_semaphore()
    for other in around:
        pl.semaphore_signal(barrier, inc=1, device_id=other, device_id_type=MESH)

    heads = (heads0, heads1)
    rts = (rt0, rt1, rt2)
    r1, r2, r5 = (r1_0, r1_1, r1_2), (r2_0, r2_1, r2_2), (r5_0, r5_1, r5_2)
    half = heads0.shape[-1]
    own_heads = [at(h, x=x_lo, y=me["y"], z=me["z"]) for h in heads]
    my_hidden = hidden_hbm.at[:, pl.ds(pl.multiple_of(sec * LANES, LANES), LANES)]

    def user_loads(step):
        slot = lax.rem(step, 2) if not isinstance(step, int) else step % 2
        users, place = pl.ds(step * GROUP, GROUP), pl.ds(slot * GROUP, GROUP)
        return (
            pltpu.make_async_copy(cache_hbm.at[users], cache.at[place], cache_sem.at[slot, 0]),
            pltpu.make_async_copy(keys_hbm.at[users], keys.at[place], cache_sem.at[slot, 1]),
        )

    def stage_up(source, n):
        copies = []
        for p, (first, rows, _) in enumerate(PARTS):
            for q in range(2):
                copies.append(
                    pltpu.make_async_copy(
                        source.at[:, :, :, pl.ds(first, rows), pl.ds(q * LANES, LANES)],
                        (o0, o1, o2)[p].at[pl.ds(2 * q, 2)],
                        stage_sem.at[n, 2 * p + q],
                    )
                )
        return copies

    loads = [
        pltpu.make_async_copy(rope_hbm, rope, local_sem.at[0]),
        pltpu.make_async_copy(query_hbm, query, local_sem.at[1]),
        pltpu.make_async_copy(value_up_hbm, value_up, local_sem.at[2]),
        pltpu.make_async_copy(gate_hbm, weight_in, local_sem.at[3]),
        pltpu.make_async_copy(out_proj_hbm, out_proj, local_sem.at[4]),
        pltpu.make_async_copy(down_hbm, down_in, local_sem.at[5]),
        pltpu.make_async_copy(my_hidden, hidden, local_sem.at[6]),
        pltpu.make_async_copy(gate_far, weight_in, local_sem.at[7]),
        pltpu.make_async_copy(down_far, down_in, local_sem.at[8]),
    ]
    up_loads = stage_up(up_hbm, 0), stage_up(up_far, 1)
    for copy in (loads[0], loads[1], *user_loads(0), *user_loads(1)):
        copy.start()
    loads[2].start()

    for p, gain in enumerate((gain0, gain1, gain2)):
        first, rows, _ = PARTS[p]
        width = gain.shape[-1]
        block = lax.broadcasted_iota(jnp.int32, (LANES, width), 1) // rows
        offset = lax.rem(lax.broadcasted_iota(jnp.int32, (LANES, width), 1), rows) + first
        lane = lax.broadcasted_iota(jnp.int32, (LANES, width), 0)
        for j in range(gain.shape[0]):
            if p == 0:
                owner = block * 4 + j
            elif p == 1:
                owner = (block // 4) * 16 + j * 4 + lax.rem(block, 4)
            else:
                owner = j * 16 + block
            place = owner * FEATS + offset
            spread = jnp.dot(
                gain_ref[...], (lax.rem(place, LANES) == lane).astype(F32),
                preferred_element_type=F32, precision=lax.Precision.HIGHEST,
            )
            held = (place // LANES)[:56] == lane[:56]
            gain[j] = jnp.sum(jnp.where(held, spread, 0.0), axis=0, keepdims=True)

    users_here, heads_here = query.shape[0], query.shape[1]
    loads[0].wait()
    wide = heads_here * ROPE
    owner = lax.broadcasted_iota(jnp.int32, (heads_here, wide), 1) // ROPE
    mask = owner == lax.broadcasted_iota(jnp.int32, (heads_here, wide), 0)
    fold = lax.rem(lax.broadcasted_iota(jnp.int32, (wide, ROPE), 0), ROPE)
    fold = (fold == lax.broadcasted_iota(jnp.int32, (wide, ROPE), 1)).astype(F32).astype(BF16)
    for r in range(users_here):
        row = jnp.broadcast_to(rope[r : r + 1, :].astype(F32), (heads_here, wide))
        row = jnp.where(mask, row, 0.0).astype(BF16)
        positional[r] = jnp.dot(row, fold, preferred_element_type=F32).astype(BF16)
    loads[1].wait()
    history = cache.shape[1]
    moment = lax.broadcasted_iota(jnp.int32, (heads_here, history), 1)

    def attend(step, carry):
        slot = lax.rem(step, 2)
        for copy in user_loads(step):
            copy.wait()
        weights = []
        for n in range(GROUP):
            r = step * GROUP + n
            place = slot * GROUP + n
            scores = lax.dot_general(
                query[r], cache[place], (((1,), (1,)), ((), ())), preferred_element_type=F32
            )
            scores += jnp.dot(positional[r], keys[place], preferred_element_type=F32)
            scores = scores * (NOPE + ROPE) ** (-0.5)
            scores = jnp.where(moment < lengths_ref[r], scores, -1e30)
            exponent = jnp.exp(scores - jnp.max(scores, axis=-1, keepdims=True))
            weights.append((exponent / jnp.sum(exponent, axis=-1, keepdims=True)).astype(BF16))
        for n in range(GROUP):
            r = step * GROUP + n
            value = jnp.dot(weights[n], cache[slot * GROUP + n], preferred_element_type=F32)
            value = value.astype(BF16).astype(F32)
            rows = pl.ds(pl.multiple_of(r * heads_here, heads_here), heads_here)
            for t in range(context.shape[0]):
                context[t, rows, :] = value[:, t * LANES : (t + 1) * LANES]

        @pl.when(step < users_here // GROUP - 2)
        def _():
            for copy in user_loads(step + 2):
                copy.start()

        return carry

    lax.fori_loop(0, 1, attend, 0)
    pl.semaphore_wait(barrier, len(around))
    send(("wg",), gate_hbm, gate_far, partner)
    send(("wu",), up_hbm, up_far, partner)
    send(("wd",), down_hbm, down_far, partner)
    lax.fori_loop(1, users_here // GROUP, attend, 0)
    for copy in (loads[3], *up_loads[0], *loads[4:7]):
        copy.start()
    loads[2].wait()

    def head_value(h):
        tiles = [context[t, pl.ds(h, users_here, stride=heads_here), :] for t in range(context.shape[0])]
        rows = jnp.concatenate(tiles, axis=1).astype(BF16)
        value = jnp.dot(rows, value_up[h], preferred_element_type=F32)
        return value.astype(BF16)

    order = (("y", "z"), ("z", "y"))

    def head_block(p, k, **index):
        place = {"x": lax.rem(x_lo + k, 2), "y": me["y"], "z": me["z"]}
        place.update(index)
        return at(heads[p], **place)

    def head_slab(p, **index):
        return at(heads[p], **index)

    for p in range(2):
        for h in range(heads_here // 2):
            heads[p][x_lo, me["y"], me["z"], :, h * 128 : h * 128 + 128] = head_value(p * (heads_here // 2) + h)
        send(("hx", p), own_heads[p], own_heads[p], x_lo_partner)
        b, c = order[p]
        for by in (1, 3):
            send(("hb", p, 0, by), own_heads[p], own_heads[p], neighbour(b, by))
        for by in (1, 3):
            send(("hc", p, 0, by), own_heads[p], own_heads[p], neighbour(c, by))

    wts = (wt0, wt1, wt2)
    gains = (gain0, gain1, gain2)

    def gate_task(slot, p):
        if p == 0:
            loads[7 if slot else 3].wait()

        def step(j, carry):
            block = weight_plane(weight_in, p, j).T.astype(F32) * gains[p][j]
            wts[p][j, slot, 0:256, :] = block.astype(BF16)
            return carry

        lax.fori_loop(0, wts[p].shape[0], step, 0)

    def up_task(slot, p):
        if p == 0:
            for copy in up_loads[slot]:
                copy.wait()

        def step(j, carry):
            for q in range(2):
                if p == 0:
                    block = o0[2 * q : 2 * q + 2, :, j]
                elif p == 1:
                    block = o1[2 * q : 2 * q + 2, j]
                else:
                    block = o2[2 * q + j]
                block = block.reshape(-1, LANES).T.astype(F32) * gains[p][j]
                wts[p][j, slot, 256 + q * LANES : 256 + (q + 1) * LANES, :] = block.astype(BF16)
            return carry

        lax.fori_loop(0, wts[p].shape[0], step, 0)

    def down_task(slot, half_of):
        if half_of == 0:
            loads[8 if slot else 5].wait()

        def step(j, carry):
            block = down_in[:, pl.ds(pl.multiple_of(j * 896, 896), 896)].T
            downt[slot, j // 4, lax.rem(j, 4)] = block.reshape(4, FEATS, 256)
            return carry

        lax.fori_loop(4 * half_of, 4 * half_of + 4, step, 0)

    tasks = []
    for slot in range(2):
        tasks += [functools.partial(gate_task, slot, p) for p in range(3)]
        tasks += [functools.partial(up_task, slot, p) for p in range(3)]
        tasks += [functools.partial(down_task, slot, n) for n in range(2)]

    def fetch_partner():
        recv(("wg",), gate_far)
        loads[7].start()
        recv(("wu",), up_far)
        for copy in up_loads[1]:
            copy.start()
        recv(("wd",), down_far)
        loads[8].start()

    def work(count=1):
        for task in tasks[:count]:
            task()
        del tasks[:count]

    work(8)

    def slab_sends(p, m):
        b, c = order[p]
        slab = head_slab(p, **{b: shift(b, m), c: me[c]})
        for by in (1, 3):
            send(("hc", p, m, by), slab, slab, neighbour(c, by))

    for p in range(2):
        b, c = order[p]
        other = head_block(p, 1)
        recv(("hx", p), other)
        for by in (1, 3):
            send(("hb", p, 1, by), other, other, neighbour(b, by))
    for p in range(2):
        other = head_block(p, 1)
        for by in (1, 3):
            send(("hc", p, 0, by), other, other, neighbour(order[p][1], by))
    for p in range(2):
        b, c = order[p]
        block = head_block(p, 0, **{b: shift(b, 3)})
        recv(("hb", p, 0, 1), block)
        send(("hf", p), block, block, neighbour(b, 1))
        recv(("hb", p, 0, 3), head_block(p, 0, **{b: shift(b, 1)}))
    for p in range(2):
        b, c = order[p]
        block = head_block(p, 1, **{b: shift(b, 1)})
        recv(("hb", p, 1, 3), block)
        send(("hf", p), block, block, neighbour(b, 3))
        slab_sends(p, 1)
        recv(("hb", p, 1, 1), head_block(p, 1, **{b: shift(b, 3)}))
        slab_sends(p, 3)
    for p in range(2):
        b, c = order[p]
        recv(("hf", p), head_slab(p, **{b: shift(b, 2), c: me[c]}))
        slab_sends(p, 2)
    fetch_partner()

    def project(p, by, first=False):
        c = order[p][1]
        j = shift(c, by)
        rows = get(heads[p], **{c: j}).reshape(-1, half)
        product = lax.dot_general(
            rows, out_proj[:, p * half : (p + 1) * half], (((1,), (1,)), ((), ())), preferred_element_type=F32
        )
        product = product.reshape(2, 4, 16, FEATS)
        if c == "z":
            attn[:, :, j] = product
        else:
            attn[:, j] += product

    loads[4].wait()
    project(0, 0)
    for m in (0, 1, 3, 2):
        for p in range(2):
            b, c = order[p]
            for by in (1, 3):
                region = head_slab(p, **{b: shift(b, m), c: shift(c, -by)})
                recv(("hc", p, m, by), region)
                passed = head_slab(p, **{"x": by // 2, b: shift(b, m), c: shift(c, -by)})
                send(("hd", p), passed, passed, neighbour(c, by))
        work(2)
    work(len(tasks))
    project(0, 1)
    project(0, 3)
    recv(("hd", 0), head_slab(0, **{order[0][1]: shift(order[0][1], 2)}))
    project(0, 2)
    for by in (0, 1, 3):
        project(1, by)
    recv(("hd", 1), head_slab(1, **{order[1][1]: shift(order[1][1], 2)}))
    project(1, 2)

    attn_mine = attn.at[:, pl.ds(core * 2, 2)]
    send(("pair",), attn.at[:, pl.ds((1 - core) * 2, 2)], pair_in, partner)
    recv(("pair",), pair_in)
    far_out[...] = (attn_mine[1 - x_hi] + pair_in[1 - x_hi]).astype(BF16)
    send(("far",), far_out, far_in, neighbour("x", 2))
    loads[6].wait()
    near = (attn_mine[x_hi] + pair_in[x_hi]).reshape(LANES, FEATS)
    recv(("far",), far_in)
    residual = near + far_in[...].reshape(LANES, FEATS).astype(F32)
    residual = jnp.concatenate([residual, jnp.zeros((LANES, 32), F32)], axis=1).T[:FEATS]
    residual = residual + hidden[...].astype(F32)
    kept[...] = residual
    routed = residual.astype(BF16)

    for p, (first, rows, _) in enumerate(PARTS):
        rts[p][me["x"], me["y"], me["z"]] = routed[first : first + rows]

    def spot(p, **index):
        place = dict(me)
        place.update(index)
        return at(rts[p], **place)

    axes = [tuple(o) for _, _, o in PARTS]
    for p in range(3):
        a, b, c = axes[p]
        for k in (1, 3, 2):
            send(("ga", p, k), spot(p), spot(p), away(**{a: k}))
        for by in (1, 3):
            send(("gc", p, 0, by), spot(p), spot(p), neighbour(c, by))
    for p in range(3):
        a, b, c = axes[p]
        for m in (2, 1, 3):
            send(("gb", p, m), spot(p), spot(p), away(**{b: m}))
    for k in (1, 3, 2):
        for p in range(3):
            a, b, c = axes[p]
            block = spot(p, **{a: shift(a, k)})
            recv(("ga", p, 4 - k), block)
            for m in (2, 1, 3):
                send(("gb", p, m), block, block, away(**{b: m}))
            for by in (1, 3):
                send(("gc", p, 0, by), block, block, neighbour(c, by))
    for m in (1, 3, 2):
        for p in range(3):
            a, b, c = axes[p]
            slab = at(rts[p], **{b: shift(b, m), c: me[c]})
            recv(("gb", p, 4 - m), slab)
            for by in (1, 3):
                send(("gc", p, m, by), slab, slab, neighbour(c, by))

    def pass_on(m):
        for p in range(3):
            a, b, c = axes[p]
            for by in (1, 3):
                region = at(rts[p], **{b: shift(b, m), c: shift(c, -by)})
                recv(("gc", p, m, by), region)
                half_of = pl.ds(0, 2) if by == 1 else pl.ds(2, 2)
                passed = at(rts[p], **{a: half_of, b: shift(b, m), c: shift(c, -by)})
                send(("gd", p), passed, passed, neighbour(c, by))

    pass_on(0)

    totals = {"square": jnp.zeros((1, 256), F32), "first": True}

    def users_of(p, by):
        if p == 0:
            block = rts[0][:, :, shift("z", by)]
            low, high = block[0:2], block[2:4]
        elif p == 1:
            block = rts[1][:, shift("y", by)]
            low, high = block[0:2], block[2:4]
        else:
            plane = lax.rem(x_lo + by, 2)
            low, high = rts[2][plane], rts[2][plane + 2]
        return jnp.concatenate([low.reshape(-1, LANES), high.reshape(-1, LANES)], axis=1)

    def plane_of(p, by):
        if p == 2:
            return lax.rem(x_lo + by, 2)
        return shift(axes[p][2], by)

    def multiply(*planes):
        weights, rows = [], []
        for p, by in planes:
            block = users_of(p, by)
            wide = block.astype(F32)
            totals["square"] = totals["square"] + jnp.sum(wide * wide, axis=0, keepdims=True)
            weight = wts[p][plane_of(p, by)]
            weights.append(weight.reshape(1024, weight.shape[-1]))
            rows.append(block)
        if len(planes) > 1:
            weights, rows = [jnp.concatenate(weights, axis=1)], [jnp.concatenate(rows, axis=0)]
        product = jnp.dot(weights[0], rows[0], preferred_element_type=F32)
        if totals["first"]:
            gate_up[...] = product
        else:
            gate_up[...] += product
        totals["first"] = False

    multiply((0, 0), (1, 0))
    for m in (1, 3, 2):
        pass_on(m)
    multiply((0, 1), (0, 3))
    multiply((1, 1), (1, 3))
    multiply((2, 1),)
    for p in range(2):
        c = axes[p][2]
        recv(("gd", p), at(rts[p], **{c: shift(c, 2)}))
    multiply((0, 2), (1, 2))
    recv(("gd", 2), at(rts[2], x=shift("x", 2)))
    multiply((2, 0),)

    scale = lax.rsqrt(totals["square"] * (1.0 / (32 * FEATS)) + norm_eps)
    for slot in range(2):
        gate = gate_up[slot * 512 : slot * 512 + 256] * scale
        upward = gate_up[slot * 512 + 256 : slot * 512 + 512] * scale
        act[slot * 256 : slot * 256 + 256] = (gate / (1.0 + jnp.exp(-gate)) * upward).astype(BF16)

    outs = (o0, o1, o2)
    share = jnp.sum(jnp.where(ids_ref[...] == dev, weights_ref[...], 0.0), axis=0, keepdims=True)
    share = jnp.where(
        core == 0,
        jnp.concatenate([share[:, 0:128], share[:, 256:384]], axis=1),
        jnp.concatenate([share[:, 128:256], share[:, 384:512]], axis=1),
    )

    def down(p, by):
        first, rows, _ = PARTS[p]
        j = plane_of(p, by)
        weight = jnp.concatenate([weight_plane(downt.at[n], p, j) for n in range(2)], axis=1)
        product = jnp.dot(weight, act[...], preferred_element_type=F32)
        product = (product * share).astype(BF16)
        for h in range(2):
            lanes = product[:, h * LANES : (h + 1) * LANES]
            if p == 0:
                o0[2 * h : 2 * h + 2, :, j] = lanes.reshape(2, 4, rows, LANES)
            elif p == 1:
                o1[2 * h : 2 * h + 2, j] = lanes.reshape(2, 4, rows, LANES)
            else:
                o2[j + 2 * h] = lanes.reshape(4, 4, rows, LANES)

    def o_slab(p, by, m):
        a, b, c = axes[p]
        return at(outs[p], **{c: shift(c, by), b: shift(b, m)})

    for p in range(3):
        c = axes[p][2]
        down(p, 2 if p < 2 else 0)
        for m in (2, 1, 3, 0):
            by = 1 if m in (0, 1) else 3
            send(("s1", p, m), o_slab(p, 2, m), r1[p].at[m], neighbour(c, by))
    for p in range(3):
        c = axes[p][2]
        if p < 2:
            down(p, 1)
            down(p, 3)
        else:
            down(p, 1)
        for m in (2, 3):
            send(("s2", p, m), o_slab(p, 1, m), r2[p].at[m, 0], neighbour(c, 1))
        for m in (1, 0):
            send(("s2", p, m), o_slab(p, 3, m), r2[p].at[m, 1], neighbour(c, 3))
    for p in range(2):
        down(p, 0)

    def add_to(slab, other):
        slab[...] = (slab[...].astype(F32) + other[...].astype(F32)).astype(BF16)

    for m in (2, 1, 3, 0):
        for p in range(3):
            c = axes[p][2]
            recv(("s1", p, m), r1[p].at[m])
            by = 1 if m in (0, 1) else 3
            side = 0 if by == 1 else 1
            slab = o_slab(p, by, m)
            add_to(slab, r1[p].at[m])
            send(("s2", p, m), slab, r2[p].at[m, side], neighbour(c, by))

    for m in (2, 1, 3, 0):
        for p in range(3):
            a, b, c = axes[p]
            slab = o_slab(p, 0, m)
            recv(("s2", p, m), r2[p].at[m])
            slab[...] = (
                slab[...].astype(F32) + r2[p][m, 0].astype(F32) + r2[p][m, 1].astype(F32)
            ).astype(BF16)
            for k in (2, 1, 3, 0):
                if k or m:
                    send(("s5", p), slab.at[shift(a, k)], r5[p].at[4 * m + k - 1], away(**{a: k, b: m}))
    for p, (first, rows, _) in enumerate(PARTS):
        a = axes[p][0]
        total = kept[first : first + rows, :] + outs[p][me["x"], me["y"], me["z"]].astype(F32)
        recv(("s5", p), r5[p])
        for n in range(15):
            total = total + r5[p][n].astype(F32)
        out_ref[first : first + rows, :] = total.astype(BF16)
    drain()


def body(
    query_latent, query_rope, cache_latent, cache_rope, lengths, value_up, output_proj, hidden,
    norm_gain, route_ids, route_weights, gate_proj, up_proj, down_proj,
):
    def bf(*shape):
        return pltpu.VMEM(shape, BF16)

    def f32(*shape):
        return pltpu.VMEM(shape, F32)

    users, heads, latent = query_latent.shape
    history = cache_latent.shape[1]
    half = heads * LANES // 2
    rows = [r for _, r, _ in PARTS]
    hbm = pl.BlockSpec(memory_space=pl.ANY)
    vmem = pl.BlockSpec(memory_space=pltpu.VMEM)
    scratch = [
        bf(users, heads, latent), bf(users, heads * ROPE), bf(users, heads, ROPE),
        bf(2 * GROUP, history, latent), bf(2 * GROUP, ROPE, history), f32(latent // LANES, users * heads, LANES),
        bf(*value_up.shape),
        bf(2, 4, 4, 16, half), bf(2, 4, 4, 16, half), bf(FEATS, 2 * half), f32(2, 4, 4, 16, FEATS),
        f32(2, 2, 4, 16, FEATS), bf(2, 4, 16, FEATS), bf(2, 4, 16, FEATS), bf(FEATS, LANES),
        bf(2, 4, 4, FEATS, 256), bf(256, 32 * FEATS),
        f32(4, 1, 640), f32(4, 1, 640), f32(2, 1, 1024),
        bf(4, 2, 512, 640), bf(4, 2, 512, 640), bf(2, 2, 512, 1024), bf(2, 2, 4, 4, FEATS, 256),
        *[bf(4, 4, 4, r, LANES) for r in rows],
        f32(1024, 256), bf(512, 256),
        *[bf(4, 4, 4, r, LANES) for r in rows],
        *[bf(4, 4, r, LANES) for r in rows],
        *[bf(4, 2, 4, r, LANES) for r in rows],
        *[bf(15, r, LANES) for r in rows],
        f32(FEATS, LANES),
        pltpu.SemaphoreType.DMA((2, 2)),
        pltpu.SemaphoreType.DMA((9,)),
        pltpu.SemaphoreType.DMA((2, 6)),
        pltpu.SemaphoreType.DMA((36,)),
        pltpu.SemaphoreType.DMA((107,)),
    ]
    gate_proj = gate_proj.reshape(2, 4, 4, FEATS, 256)
    up_proj = up_proj.reshape(2, 4, 4, FEATS, 256)
    down_proj = down_proj[0]
    out, *_ = pl.pallas_call(
        layer_kernel,
        out_shape=(
            jax.ShapeDtypeStruct((FEATS, LANES), BF16),
            *[jax.ShapeDtypeStruct(a.shape, BF16) for a in (gate_proj, up_proj, down_proj)],
        ),
        in_specs=[
            hbm, hbm, hbm, hbm, pl.BlockSpec(memory_space=pltpu.SMEM), hbm,
            hbm, hbm, vmem, vmem, vmem, hbm, hbm, hbm,
        ],
        out_specs=(vmem, hbm, hbm, hbm),
        scratch_shapes=scratch,
        compiler_params=pltpu.CompilerParams(
            collective_id=0, has_side_effects=True, vmem_limit_bytes=63 * 1024 * 1024
        ),
        cost_estimate=pl.CostEstimate(flops=9 * 10**9, bytes_accessed=27 * 2**20, transcendentals=0),
    )(
        query_latent, query_rope, cache_latent, cache_rope, lengths, value_up,
        output_proj.T, hidden.T, norm_gain.reshape(56, LANES), route_ids.T, route_weights.T,
        gate_proj, up_proj, down_proj,
    )
    return out.T


def solution(mesh):
    return jax.shard_map(
        body,
        mesh=mesh,
        in_specs=(
            P("dev", "sec", None),
            P("dev", "sec"),
            P("dev", None, None),
            P("dev", None, None),
            P("dev"),
            P("sec", None, None),
            P("sec", "dev"),
            P(None, "dev"),
            P(),
            P(),
            P(),
            P("dev", None, "sec"),
            P("dev", None, "sec"),
            P("dev", "sec", None),
        ),
        out_specs=P("sec", "dev"),
        check_vma=False,
    )
```
